32 devices in a mesh: rep: 4 (over y, x), shard: 8 (over z, core).
Axes of the slice: x: 2, y: 2, z: 4, core: 2. Of those that a mesh axis runs over, the one named last changes fastest.
Arguments:
- tokens: bfloat16 [32768, 768], P(('rep', 'shard')), may hold values from -6 to 6
- cotangent: bfloat16 [32768, 768], P(('rep', 'shard')), may hold values from -6 to 6
- deletion: int32 [128, 256], P(('rep', 'shard')), may hold values 0 or 1
- lengths: int32 [128], P(('rep', 'shard')), may hold values from 64 to 256, as said below
- qkv_weight: float32 [768, 2304], P('shard'), may hold values from -0.21875 to 0.21875
- out_weight: float32 [768, 768], P('shard'), may hold values from -0.875 to 0.875
- up_weight: float32 [768, 3072], P('shard'), may hold values from -0.21875 to 0.21875
- down_weight: float32 [3072, 768], P('shard'), may hold values from -0.109375 to 0.109375
- vectors: float32 [12, 768], P(None, 'shard'), may hold values from -2 to 2
- qkv_first: float32 [768, 2304], P('shard'), may hold values from -192 to 192
- out_first: float32 [768, 768], P('shard'), may hold values from -192 to 192
- up_first: float32 [768, 3072], P('shard'), may hold values from -192 to 192
- down_first: float32 [3072, 768], P('shard'), may hold values from -192 to 192
- vector_first: float32 [12, 768], P(None, 'shard'), may hold values from -192 to 192
- qkv_second: float32 [768, 2304], P('shard'), may hold values from 10 to 100000
- out_second: float32 [768, 768], P('shard'), may hold values from 10 to 100000
- up_second: float32 [768, 3072], P('shard'), may hold values from 10 to 100000
- down_second: float32 [3072, 768], P('shard'), may hold values from 10 to 100000
- vector_second: float32 [12, 768], P(None, 'shard'), may hold values from 10 to 100000
Outputs:
- output: bfloat16 [32768, 768], P(('rep', 'shard'))
- token_grad: bfloat16 [32768, 768], P(('rep', 'shard'))
- qkv_grad: float32 [768, 2304], P('shard')
- out_grad: float32 [768, 768], P('shard')
- up_grad: float32 [768, 3072], P('shard')
- down_grad: float32 [3072, 768], P('shard')
- vector_grad: float32 [12, 768], P(None, 'shard')
- qkv_step: float32 [768, 2304], P('shard')
- out_step: float32 [768, 768], P('shard')
- up_step: float32 [768, 3072], P('shard')
- down_step: float32 [3072, 768], P('shard')
- vector_step: float32 [12, 768], P(None, 'shard')
- qkv_first_new: float32 [768, 2304], P('shard')
- out_first_new: float32 [768, 768], P('shard')
- up_first_new: float32 [768, 3072], P('shard')
- down_first_new: float32 [3072, 768], P('shard')
- vector_first_new: float32 [12, 768], P(None, 'shard')
The draws below stay inside these ranges and needn't reach their ends.
Inputs may be any that keep to these rules, and one draw needn't show every extreme that they name: `lengths`: in every draw some crop has all 256 positions in use and another only 64.
All inputs are finite; a program needn't handle non-finite values. No bound on the sum of `deletion` on one device may be relied on, other than what follows from the above.
Results may differ from the reference program's by a relative error of at most 0.015.
The reference program's roundings to bfloat16 on the way count: a program that leaves them out, or rounds other values in their place, can miss the bound.
Values may be sent and summed in bfloat16 or wider, within the bound.
A program may use at most 256 MiB of HBM per device.

```python
import math
import jax
import jax.numpy as jnp
from jax import lax

D = 768
H = 12
FF = 3072
HD = 64
CROP = 256
CROPS = 128
TOKENS = 32768


def draw_lengths(key, part):
    first_key, second_key, third_key = jax.random.split(key, 3)
    lowest = CROP // 4
    counts = jax.random.randint(first_key, (CROPS,), lowest, CROP + 1)
    full_at = jax.random.randint(second_key, (), 0, CROPS)
    short_at = (full_at + jax.random.randint(third_key, (), 1, CROPS)) % CROPS
    counts = counts.at[full_at].set(CROP)
    counts = counts.at[short_at].set(lowest)
    return counts.astype(jnp.int32)


def draw_vectors(key, part):
    normal_key, gain_key = jax.random.split(key)
    biases = 0.5 * jnp.clip(jax.random.normal(normal_key, (12, D), jnp.float32), -4.0, 4.0)
    gains = jnp.exp(jax.random.uniform(gain_key, (12, D), jnp.float32, -0.5, 0.5))
    row_index = lax.broadcasted_iota(jnp.int32, (12, D), 0)
    gain_rows = (row_index == 3) | (row_index == 10)
    return jnp.where(gain_rows, gains, biases).astype(jnp.float32)


def plant(entries, own_key, least, largest):
    extent = entries.shape
    place = [jax.random.randint(jax.random.fold_in(own_key, axis), (), 0, extent[axis]) for axis in range(len(extent))]
    entries = entries.at[tuple(place)].set(least)
    longest = extent.index(max(extent))
    place[longest] = (place[longest] + 1) % extent[longest]
    return entries.at[tuple(place)].set(largest)


def levels(stream_key, shape, cuts, smallest, top_value):
    def one(axis_at, shards_of):
        heights = jax.random.uniform(jax.random.fold_in(jax.random.fold_in(stream_key, 6), axis_at), (shards_of,), jnp.float32, smallest / len(cuts), top_value / len(cuts))
        return jnp.repeat(jnp.exp(heights), shape[axis_at] // shards_of).reshape((-1,) + (1,) * (len(shape) - axis_at - 1))

    factor_of = one(*cuts[0])
    for cut in cuts[1:]:
        factor_of = factor_of * one(*cut)
    return factor_of


def noise(stream_key, extent, scale, most, shards=(), kind=jnp.bfloat16):
    factor_of = levels(stream_key, extent, shards, -0.22, 0.18) if shards else 1.0
    array = jax.random.normal(stream_key, extent, jnp.float32) * scale * factor_of
    return jnp.minimum(jnp.maximum(array, -most), most).astype(kind)


def setup_inputs(seed: int = 0) -> dict:
    seeds = jax.random.split(jax.random.key(seed), 20)
    return {
        "tokens": noise(seeds[0], (TOKENS, D), 1.0, 6.0, ((0, 32),)),
        "cotangent": noise(seeds[1], (TOKENS, D), 1.0, 6.0, ((0, 32),)),
        "deletion": plant((jax.random.randint(seeds[2], (CROPS, CROP), 0, 10) < 9).astype(jnp.int32), jax.random.fold_in(seeds[2], 1), 0, 1),
        "lengths": draw_lengths(jax.random.fold_in(seeds[19], 71), 0),
        "qkv_weight": noise(seeds[4], (D, 3 * D), D ** -0.5, 0.21875, ((0, 8),), jnp.float32),
        "out_weight": noise(seeds[5], (D, D), (D // 16) ** -0.5, 0.875, ((0, 8),), jnp.float32),
        "up_weight": noise(seeds[6], (D, FF), D ** -0.5, 0.21875, ((0, 8),), jnp.float32),
        "down_weight": noise(seeds[7], (FF, D), FF ** -0.5, 0.109375, ((0, 8),), jnp.float32),
        "vectors": draw_vectors(jax.random.fold_in(seeds[19], 71), 0),
        "qkv_first": noise(seeds[9], (D, 3 * D), 30.0, 192.0, ((0, 8),), jnp.float32),
        "out_first": noise(seeds[10], (D, D), 30.0, 192.0, ((0, 8),), jnp.float32),
        "up_first": noise(seeds[11], (D, FF), 30.0, 192.0, ((0, 8),), jnp.float32),
        "down_first": noise(seeds[12], (FF, D), 30.0, 192.0, ((0, 8),), jnp.float32),
        "vector_first": noise(seeds[13], (12, D), 30.0, 192.0, ((1, 8),), jnp.float32),
        "qkv_second": jnp.clip(jnp.exp(math.log(100000.0) - 9.2103404 * jax.random.uniform(seeds[14], (D, 3 * D), jnp.float32) ** levels(seeds[14], (D, 3 * D), ((0, 8),), -0.2, 0.2)), 10.0, 100000.0),
        "out_second": jnp.clip(jnp.exp(math.log(100000.0) - 9.2103404 * jax.random.uniform(seeds[15], (D, D), jnp.float32) ** levels(seeds[15], (D, D), ((0, 8),), -0.2, 0.2)), 10.0, 100000.0),
        "up_second": jnp.clip(jnp.exp(math.log(100000.0) - 9.2103404 * jax.random.uniform(seeds[16], (D, FF), jnp.float32) ** levels(seeds[16], (D, FF), ((0, 8),), -0.2, 0.2)), 10.0, 100000.0),
        "down_second": jnp.clip(jnp.exp(math.log(100000.0) - 9.2103404 * jax.random.uniform(seeds[17], (FF, D), jnp.float32) ** levels(seeds[17], (FF, D), ((0, 8),), -0.2, 0.2)), 10.0, 100000.0),
        "vector_second": jnp.clip(jnp.exp(math.log(100000.0) - 9.2103404 * jax.random.uniform(seeds[18], (12, D), jnp.float32) ** levels(seeds[18], (12, D), ((1, 8),), -0.2, 0.2)), 10.0, 100000.0),
    }


norm_epsilon = 1e-06
decay_first = 0.9
decay_second = 0.999
correct_first = 1.0 - 2.6561398887587544e-05
correct_second = 0.0952078528862904
adam_epsilon = 1e-08
highest = lax.Precision.HIGHEST

@jax.custom_vjp
def low(v):
    return lax.optimization_barrier(v.astype(jnp.bfloat16)).astype(jnp.float32)

@jax.custom_vjp
def low_back(v):
    return v

def low_keep(v):
    return (low(v), None)

def low_pass(kept, grad):
    return (grad,)

def back_keep(v):
    return (v, None)

def back_low(kept, grad):
    return (low(grad),)
low.defvjp(low_keep, low_pass)
low_back.defvjp(back_keep, back_low)

def layer_norm(hidden, gain_row, shift_row):
    average = lax.optimization_barrier(jnp.mean(hidden, axis=-1, keepdims=True))
    centred = hidden - average
    variance = lax.optimization_barrier(jnp.mean(centred * centred, axis=-1, keepdims=True))
    return centred * lax.rsqrt(variance + norm_epsilon) * gain_row + shift_row

def block_forward(params, token_block, allow_block):
    qkv_weight, out_weight, up_weight, down_weight, vectors = params
    group_crops = allow_block.shape[0]
    qkv_bias = jnp.concatenate([vectors[0], jnp.zeros((D,), jnp.float32), vectors[1]])
    qkv_act = jnp.dot(token_block, qkv_weight, precision=highest) + qkv_bias
    qkv_act = low(low_back(qkv_act)).reshape(group_crops, CROP, 3, H, HD)
    queries = qkv_act[:, :, 0]
    keys_in = qkv_act[:, :, 1]
    values = qkv_act[:, :, 2]
    scores = jnp.einsum('clhd,cmhd->chlm', queries, keys_in, precision=highest) * (1.0 / math.sqrt(HD))
    scores = low_back(jnp.where(allow_block[:, None, None, :], scores, -1e+30))
    soft_probs = low(jax.nn.softmax(scores, axis=-1))
    mixed_rows = jnp.einsum('chlm,cmhd->clhd', soft_probs, values, precision=highest)
    mixed_rows = low(low_back(mixed_rows.reshape(group_crops * CROP, D)))
    branch = low_back(jnp.dot(mixed_rows, out_weight, precision=highest) + vectors[2])
    first_out = layer_norm(token_block + branch, vectors[3], vectors[4])
    inner_act = low_back(jnp.dot(low(first_out), up_weight, precision=highest) + vectors[5:9].reshape(FF))
    activated = low(jax.nn.gelu(inner_act, approximate=False))
    second = low_back(jnp.dot(activated, down_weight, precision=highest) + vectors[9])
    return layer_norm(first_out + second, vectors[10], vectors[11])

def adam_update(gradient, first_moment, second_moment):
    first_new = decay_first * first_moment + (1.0 - decay_first) * gradient
    second_new = decay_second * second_moment + (1.0 - decay_second) * gradient * gradient
    step_dir = first_new / correct_first / (jnp.sqrt(second_new / correct_second) + adam_epsilon)
    return (step_dir, first_new)

def reference(tokens, cotangent, deletion, lengths, qkv_weight, out_weight, up_weight, down_weight, vectors, qkv_first, out_first, up_first, down_first, vector_first, qkv_second, out_second, up_second, down_second, vector_second):
    places = jnp.arange(CROP, dtype=jnp.int32)[None, :]
    allowed = ((deletion == 1) | (places == 0)) & (places < lengths[:, None])
    group_crops = math.gcd(CROPS, 16)
    step_count = CROPS // group_crops
    token_groups = tokens.astype(jnp.float32).reshape(step_count, group_crops * CROP, D)
    allowed_groups = allowed.reshape(step_count, group_crops, CROP)
    masters = (qkv_weight, out_weight, up_weight, down_weight, vectors)
    checked = jax.checkpoint(block_forward)

    def forward(inputs, params):
        rounded = tuple((low(member) for member in params))

        def scan_step(carry, pieces):
            return (carry, checked(rounded, pieces[0], pieces[1]))
        _, outputs = lax.scan(scan_step, jnp.zeros((), jnp.float32), (inputs, allowed_groups))
        return outputs
    result, pullback = jax.vjp(forward, token_groups, masters)
    keep_rows = allowed_groups.reshape(step_count, group_crops * CROP).astype(jnp.float32)
    grad_result = cotangent.astype(jnp.float32).reshape(step_count, group_crops * CROP, D) * keep_rows[:, :, None]
    grad_tokens, gradients = pullback(grad_result)
    firsts = (qkv_first, out_first, up_first, down_first, vector_first)
    seconds = (qkv_second, out_second, up_second, down_second, vector_second)
    updated = [adam_update(gradient, first_moment, second_moment) for gradient, first_moment, second_moment in zip(gradients, firsts, seconds)]
    return (result.reshape(TOKENS, D).astype(jnp.bfloat16), grad_tokens.reshape(TOKENS, D).astype(jnp.bfloat16), gradients[0], gradients[1], gradients[2], gradients[3], gradients[4], updated[0][0], updated[1][0], updated[2][0], updated[3][0], updated[4][0], updated[0][1], updated[1][1], updated[2][1], updated[3][1], updated[4][1])
```

```python
import math
import jax, jax.numpy as jnp
from jax import lax
from jax.sharding import PartitionSpec as P
from jax.experimental import pallas as pl
from jax.experimental.pallas import tpu as pltpu
D=768; H=12; FF=3072; CROP=256; T=1024; NC=4
bf=jnp.bfloat16; f32=jnp.float32
EPS=1e-6
decay_first = 0.9
decay_second = 0.999
correct_first = 1.0 - 2.6561398887587544e-05
correct_second = 0.0952078528862904
adam_epsilon = 1e-08
def dg(a,b,ca,cb): return lax.dot_general(a,b,(((ca,),(cb,)),((),())),preferred_element_type=f32)
def rows_of(c): return pl.ds(pl.multiple_of(c*CROP,CROP),CROP)
def lanemean(v): return jnp.sum(v,axis=-1,keepdims=True)*(1.0/D)
def lanes(v,n): return jnp.concatenate([v]*n,axis=1)
OFF=dict(Q=0,K=768,V=1536,O=2304,U=3072,D=6144)

def gelu_parts(u):
    phi=jnp.exp(u*u*-0.5)*(1.0/math.sqrt(2*math.pi))
    cdf=0.5*(1.0+lax.erf(u*math.sqrt(0.5)))
    return u*cdf, cdf+u*phi

def kernel(tok_h,cot_h,allow_ref,vec_ref,w_h, out_h,tg_h,gw_h,vg_ref,
           W,x,qkv,pt,mixed,nrm1,root1,fl,act,gp,gs,gsec,cot,keep,sem):
    cps=[pltpu.make_async_copy(tok_h,x,sem.at[0]),pltpu.make_async_copy(cot_h,cot,sem.at[1]),pltpu.make_async_copy(w_h,W,sem.at[2])]
    for c in cps: c.start()
    mcol=allow_ref[...].T
    for c in range(NC):
        keep[c*CROP:(c+1)*CROP,:]=jnp.broadcast_to(mcol[:,c:c+1],(CROP,128))
    vg_ref[...]=jnp.zeros_like(vg_ref)
    for c in cps: c.wait()
    lane=lax.broadcasted_iota(jnp.int32,(CROP,128),1)
    low_half=lane<64
    def half(v,h): return jnp.where(low_half if h==0 else ~low_half, v, jnp.zeros_like(v))
    vrow=lambda r: vec_ref[r:r+1,:]
    @pl.loop(0,NC)
    def _(c):
      r=rows_of(c); xv=x[r,:]
      for b in range(3):
          y=dg(xv,W[b*D:(b+1)*D,:],1,0)
          if b==0: y=y+vrow(0)
          if b==2: y=y+vrow(1)
          qkv[r,b*D:(b+1)*D]=y.astype(bf)
    @pl.loop(0,NC)
    def _(c):
      r=rows_of(c)
      kp=lanes(keep[r,:],2)>0.5
      for p in range(6):
          q=qkv[r,p*128:(p+1)*128]*jnp.asarray(0.125,bf); k=qkv[r,D+p*128:D+(p+1)*128]; v=qkv[r,2*D+p*128:2*D+(p+1)*128]
          o=None
          for h in range(2):
              st=dg(k,half(q,h),1,1)
              st=jnp.where(kp,st,-1e30)
              e=jnp.exp(st-jnp.max(st,axis=0,keepdims=True))
              pr=(e*(1.0/jnp.sum(e,axis=0,keepdims=True))).astype(bf)
              pt[c,2*p+h]=pr
              t=dg(pr,half(v,h),0,0)
              o=t if o is None else o+t
          mixed[r,p*128:(p+1)*128]=o.astype(bf)
    @pl.loop(0,NC)
    def _(c):
      r=rows_of(c)
      h=x[r,:].astype(f32)+(dg(mixed[r,:],W[OFF['O']:OFF['O']+D,:],1,0)+vrow(2))
      h=h-lanemean(h)
      root=lax.rsqrt(lanemean(h*h)+EPS)
      n=h*root
      nrm1[r,:]=n
      root1[r,:]=jnp.broadcast_to(root,(CROP,128))
      fl[r,:]=(n*vrow(3)+vrow(4)).astype(bf)
    @pl.loop(0,NC)
    def _(c):
      r=rows_of(c); a=fl[r,:]
      for j in range(4):
          u=dg(a,W[OFF['U']+j*D:OFF['U']+(j+1)*D,:],1,0)+vrow(5+j)
          g,d=gelu_parts(u)
          act[r,j*D:(j+1)*D]=g.astype(bf)
          gp[r,j*D:(j+1)*D]=d.astype(bf)
    @pl.loop(0,NC)
    def _(c):
      r=rows_of(c)
      s=dg(act[r,:],W[OFF['D']:OFF['D']+FF,:],1,0)+vrow(9)
      h=nrm1[r,:]*vrow(3)+vrow(4)+s
      h=h-lanemean(h)
      root=lax.rsqrt(lanemean(h*h)+EPS)
      n=h*root
      G=cot[r,:].astype(f32)*lanes(keep[r,:],6)
      cot[r,:]=(n*vrow(10)+vrow(11)).astype(bf)
      vg_ref[10:11,:]+=jnp.sum(G*n,axis=0,keepdims=True)
      vg_ref[11:12,:]+=jnp.sum(G,axis=0,keepdims=True)
      dn=G*vrow(10)
      g2=root*(dn-lanemean(dn)-n*lanemean(dn*n))
      gs[r,:]=g2
      gb=g2.astype(bf)
      gsec[r,:]=gb
      vg_ref[9:10,:]+=jnp.sum(gb.astype(f32),axis=0,keepdims=True)
    oc=pltpu.make_async_copy(cot,out_h,sem.at[0]); oc.start()
    @pl.loop(0,NC)
    def _(c):
      r=rows_of(c); a=gsec[r,:]
      for j in range(4):
          ga=dg(a,W[OFF['D']+j*D:OFF['D']+(j+1)*D,:],1,1)
          gi=(ga*gp[r,j*D:(j+1)*D].astype(f32)).astype(bf)
          gp[r,j*D:(j+1)*D]=gi
          vg_ref[5+j:6+j,:]+=jnp.sum(gi.astype(f32),axis=0,keepdims=True)
    @pl.loop(0,6)
    def _(i):
      m=pl.ds(pl.multiple_of(i*512,512),512)
      W[pl.ds(pl.multiple_of(OFF['D']+i*512,512),512),:]=dg(act[:,m],gsec[...],0,0).astype(bf)
    @pl.loop(0,NC)
    def _(c):
      r=rows_of(c)
      G=gs[r,:]
      for j in range(4):
          G=G+dg(gp[r,j*D:(j+1)*D],W[OFF['U']+j*D:OFF['U']+(j+1)*D,:],1,1)
      n=nrm1[r,:]
      vg_ref[3:4,:]+=jnp.sum(G*n,axis=0,keepdims=True)
      vg_ref[4:5,:]+=jnp.sum(G,axis=0,keepdims=True)
      dn=G*vrow(3)
      g1=lanes(root1[r,:],6)*(dn-lanemean(dn)-n*lanemean(dn*n))
      gs[r,:]=g1
      gb=g1.astype(bf)
      gsec[r,:]=gb
      vg_ref[2:3,:]+=jnp.sum(gb.astype(f32),axis=0,keepdims=True)
    @pl.loop(0,4)
    def _(j):
      W[pl.ds(pl.multiple_of(OFF['U']+j*D,D),D),:]=dg(fl[...],gp[:,pl.ds(pl.multiple_of(j*D,D),D)],0,0).astype(bf)
    @pl.loop(0,NC)
    def _(c):
      r=rows_of(c)
      fl[r,:]=dg(gsec[r,:],W[OFF['O']:OFF['O']+D,:],1,1).astype(bf)
    @pl.loop(0,1)
    def _(i):
      W[OFF['O']:OFF['O']+D,:]=dg(mixed[...],gsec[...],0,0).astype(bf)
    @pl.loop(0,NC)
    def _(c):
      r=rows_of(c)
      for p in range(6):
          cq=slice(p*128,(p+1)*128); ck=slice(D+p*128,D+(p+1)*128); cv=slice(2*D+p*128,2*D+(p+1)*128)
          q=qkv[r,cq]*jnp.asarray(0.125,bf); k=qkv[r,ck]; v=qkv[r,cv]; do=fl[r,cq]
          dq=dk=dv=None
          for h in range(2):
              dom=half(do,h)
              dp=dg(v,dom,1,1)
              prb=pt[c,2*p+h]
              pr=prb.astype(f32)
              delta=jnp.sum(pr*dp,axis=0,keepdims=True)
              ds=(pr*(dp-delta)).astype(bf)
              tv=dg(prb,dom,1,0); tk=dg(ds,half(q,h),1,0); tq=dg(ds,half(k,h),0,0)
              dq,dk,dv=(tq,tk,tv) if dq is None else (dq+tq,dk+tk,dv+tv)
          act[r,cq]=(dq*0.125).astype(bf); act[r,ck]=dk.astype(bf); act[r,cv]=dv.astype(bf)
    @pl.loop(0,NC)
    def _(c):
      r=rows_of(c)
      G=gs[r,:]
      for b in range(3):
          g=act[r,b*D:(b+1)*D]
          G=G+dg(g,W[b*D:(b+1)*D,:],1,1)
          if b!=1:
              vg_ref[b//2:b//2+1,:]+=jnp.sum(g.astype(f32),axis=0,keepdims=True)
      gsec[r,:]=G.astype(bf)
    tc=pltpu.make_async_copy(gsec,tg_h,sem.at[1]); tc.start()
    @pl.loop(0,3)
    def _(j):
      W[pl.ds(pl.multiple_of(j*D,D),D),:]=dg(x[...],act[:,pl.ds(pl.multiple_of(j*D,D),D)],0,0).astype(bf)
    gc=pltpu.make_async_copy(W,gw_h,sem.at[2]); gc.start()
    for c in (oc,tc,gc): c.wait()

def layer(tok,cot,allow,vec,w):
    A=pl.BlockSpec(memory_space=pl.ANY); V=pl.BlockSpec(memory_space=pltpu.VMEM)
    VM=pltpu.VMEM
    return pl.pallas_call(kernel,
        out_shape=[jax.ShapeDtypeStruct((T,D),bf),jax.ShapeDtypeStruct((T,D),bf),jax.ShapeDtypeStruct((12*D,D),bf),jax.ShapeDtypeStruct((16,D),f32)],
        in_specs=[A,A,V,V,A],out_specs=[A,A,A,V],
        scratch_shapes=[VM((12*D,D),bf),VM((T,D),bf),VM((T,3*D),bf),VM((NC,H,CROP,CROP),bf),VM((T,D),bf),VM((T,D),f32),VM((T,128),f32),VM((T,D),bf),
            VM((T,FF),bf),VM((T,FF),bf),VM((T,D),f32),VM((T,D),bf),VM((T,D),bf),VM((T,128),f32),pltpu.SemaphoreType.DMA((3,))],
        compiler_params=pltpu.CompilerParams(vmem_limit_bytes=63*2**20))(tok,cot,allow,vec,w)


def adam_update(gradient, first_moment, second_moment):
    first_new = decay_first * first_moment + (1.0 - decay_first) * gradient
    second_new = decay_second * second_moment + (1.0 - decay_second) * gradient * gradient
    step_dir = first_new / correct_first / (jnp.sqrt(second_new / correct_second) + adam_epsilon)
    return (step_dir, first_new)


def allowed_rows(deletion, lengths):
    places = jnp.arange(CROP, dtype=jnp.int32)[None, :]
    allowed = ((deletion == 1) | (places == 0)) & (places < lengths[:, None])
    return jnp.pad(allowed.astype(f32), ((0, 8 - NC), (0, 0)))


def finish(output, token_grad, gradients, firsts, seconds):
    updated = [adam_update(g, m, s) for g, m, s in zip(gradients, firsts, seconds)]
    return (
        (output, token_grad)
        + tuple(gradients)
        + tuple(u[0] for u in updated)
        + tuple(u[1] for u in updated)
    )


def per_device_plain(tokens, cotangent, deletion, lengths, qkv, out, up, down, vectors, *moments):
    firsts, seconds = moments[:5], moments[5:]
    blocks = [qkv[:, b * D : (b + 1) * D] for b in range(3)] + [out]
    blocks += [up[:, b * D : (b + 1) * D] for b in range(4)]
    square = lax.all_gather(jnp.stack(blocks).astype(bf), "shard", axis=1, tiled=True)
    tall = lax.all_gather(down.astype(bf), "shard", axis=0, tiled=True)
    vec = lax.all_gather(vectors.astype(bf), "shard", axis=1, tiled=True).astype(f32)
    weights = jnp.concatenate([square.reshape(8 * D, D), tall], axis=0)
    output, token_grad, grads, vector_grads = layer(
        tokens, cotangent, allowed_rows(deletion, lengths), jnp.pad(vec, ((0, 4), (0, 0))), weights
    )
    grads = grads.astype(f32)
    square = lax.psum_scatter(
        grads[: 8 * D].reshape(8, D, D), "shard", scatter_dimension=1, tiled=True
    )
    tall = lax.psum_scatter(grads[8 * D :], "shard", scatter_dimension=0, tiled=True)
    vec = lax.psum_scatter(vector_grads[:12], "shard", scatter_dimension=1, tiled=True)
    square, tall, vec = (
        lax.psum(g.astype(bf), "rep").astype(f32) for g in (square, tall, vec)
    )
    gradients = (
        jnp.concatenate([square[0], square[1], square[2]], axis=1),
        square[3],
        jnp.concatenate([square[4], square[5], square[6], square[7]], axis=1),
        tall,
        vec,
    )
    return finish(output, token_grad, gradients, firsts, seconds)


def solution(mesh):
    rows = P(("rep", "shard"), None)
    weights = (P("shard", None),) * 4 + (P(None, "shard"),)
    return jax.shard_map(
        per_device_plain,
        mesh=mesh,
        in_specs=(rows, rows, rows, P(("rep", "shard"))) + weights * 3,
        out_specs=(rows, rows) + weights * 3,
        check_vma=False,
    )
```

```python
import functools
import math

import jax
import jax.numpy as jnp
from jax import lax
from jax.experimental import pallas as pl
from jax.experimental.pallas import tpu as pltpu
from jax.sharding import PartitionSpec as P

D = 768
H = 12
FF = 3072
CROP = 256
T = 1024
NC = 4
SUB = 96
bf = jnp.bfloat16
f32 = jnp.float32
MESH = pl.DeviceIdType.MESH

norm_epsilon = 1e-06
decay_first = 0.9
decay_second = 0.999
correct_first = 1.0 - 2.6561398887587544e-05
correct_second = 0.0952078528862904
adam_epsilon = 1e-08


def dg(a, b, ca, cb):
    return lax.dot_general(a, b, (((ca,), (cb,)), ((), ())), preferred_element_type=f32)


def rows_of(c):
    return pl.ds(pl.multiple_of(c * CROP, CROP), CROP)


def lane_mean(v):
    return jnp.sum(v, axis=-1, keepdims=True) * (1.0 / D)


def lanes(v, n):
    return jnp.concatenate([v] * n, axis=1)


def gelu_parts(u):
    density = jnp.exp(u * u * -0.5) * (1.0 / math.sqrt(2.0 * math.pi))
    cdf = 0.5 * (1.0 + lax.erf(u * math.sqrt(0.5)))
    return u * cdf, cdf + u * density


def crop_loop(body, after=None):
    @pl.loop(0, NC)
    def _(c):
        body(c)
        for k, steps in (after or {}).items():

            @pl.when(c == k)
            def _():
                for step in steps:
                    step()


class Links:
    def __init__(self, refs):
        self.__dict__.update(refs)
        r = lax.axis_index("rep")
        s = lax.axis_index("shard")
        self.y, self.x = r // 2, r % 2
        self.z, self.c = s // 2, s % 2
        self.r, self.s = r, s
        self.rx = self.y * 2 + 1 - self.x
        self.ry = (1 - self.y) * 2 + self.x
        self.rd = 3 - r
        self.others = [(self.z + d) % 4 for d in (1, 2, 3)]
        self.dev_core = (r, self.z * 2 + 1 - self.c)
        self.dev_x = (self.rx, s)
        self.dev_y = (self.ry, s)
        self.dev_d = (self.rd, s)
        self.dev_z = [(r, z * 2 + self.c) for z in self.others]
        self.x1, self.y1, self.c1 = 1 - self.x, 1 - self.y, 1 - self.c
        self.s1 = self.z * 2 + self.c1
        self.s_others = [z * 2 + self.c for z in self.others]
        self.s1_others = [z * 2 + self.c1 for z in self.others]
        self.count = 0
        self.sent = []

    def greet(self):
        barrier = pltpu.get_barrier_semaphore()
        partners = [self.dev_core, self.dev_x, self.dev_y, self.dev_d] + self.dev_z
        for device in partners:
            pl.semaphore_signal(barrier, inc=1, device_id=device, device_id_type=MESH)
        pl.semaphore_wait(barrier, len(partners))

    def slot(self):
        self.count += 1
        return self.count - 1

    def copy(self, src, dst, k, device):
        return pltpu.make_async_remote_copy(
            src_ref=src,
            dst_ref=dst,
            send_sem=self.send_sem.at[k],
            recv_sem=self.recv_sem.at[k],
            device_id=device,
            device_id_type=MESH,
        )

    def part(self, g, jy, jx, z, c):
        if g == 2:
            return self.wd.at[z, c, jy, jx]
        return self.ws.at[g, jy, jx, z, c]

    def plan_gather(self):
        self.ag = [
            dict(
                core=[self.slot() for _ in range(4)],
                zed=[self.slot() for _ in range(3)],
                px=[self.slot() for _ in range(3)],
                py=[self.slot() for _ in range(3)],
                relay=[self.slot() for _ in range(3)],
                sib=[[self.slot() for _ in range(3)] for _ in range(4)],
            )
            for _ in range(3)
        ]
        self.ag_vec = dict(
            core=self.slot(), zed=[self.slot() for _ in range(3)], sib=[self.slot() for _ in range(3)]
        )

    def send(self, src, dst, k, device, keep):
        def describe():
            return self.copy(src[0](*src[1:]), dst[0](*dst[1:]), k, device)

        describe().start()
        keep.append(describe)

    def at(self, name, *index):
        return getattr(self, name).at[index if len(index) > 1 else index[0]]

    def same(self, ref, k, device, keep):
        self.send(ref, ref, k, device, keep)

    def arrive(self, ref, k, device):
        self.copy(ref[0](*ref[1:]), ref[0](*ref[1:]), k, device).wait_recv()

    def gather_start(self, g):
        for j in range(4):
            self.same(
                (self.part, g, j // 2, j % 2, self.z, self.c), self.ag[g]["core"][j], self.dev_core, self.sent
            )
        own = (self.part, g, self.y, self.x, self.z, self.c)
        for d in range(3):
            self.same(own, self.ag[g]["zed"][d], self.dev_z[d], self.sent)
        if g == 0:
            block = (self.at, "vb", self.s)
            self.same(block, self.ag_vec["core"], self.dev_core, self.sent)
            for d in range(3):
                self.same(block, self.ag_vec["zed"][d], self.dev_z[d], self.sent)

    def x_first(self, g, d):
        return (d != 1) == (g != 1)

    def gather_plane(self, g):
        for d in range(3):
            z, k = self.others[d], 2 - d
            ref = (self.part, g, self.y, self.x, z, self.c)
            self.arrive(ref, self.ag[g]["zed"][k], self.dev_z[d])
            self.same(ref, self.ag[g]["px"][d], self.dev_x, self.sent)
            self.same(ref, self.ag[g]["py"][d], self.dev_y, self.sent)
            self.same(ref, self.ag[g]["sib"][0][d], self.dev_core, self.sent)
            if g == 0:
                block = (self.at, "vb", self.s_others[d])
                self.arrive(block, self.ag_vec["zed"][k], self.dev_z[d])
                self.same(block, self.ag_vec["sib"][d], self.dev_core, self.sent)

    def gather_relay(self, g):
        for d in range(3):
            z = self.others[d]
            ref_x = (self.part, g, self.y, self.x1, z, self.c)
            self.arrive(ref_x, self.ag[g]["px"][d], self.dev_x)
            if self.x_first(g, d):
                self.same(ref_x, self.ag[g]["relay"][d], self.dev_y, self.sent)
            self.same(ref_x, self.ag[g]["sib"][1][d], self.dev_core, self.sent)
            ref_y = (self.part, g, self.y1, self.x, z, self.c)
            self.arrive(ref_y, self.ag[g]["py"][d], self.dev_y)
            if not self.x_first(g, d):
                self.same(ref_y, self.ag[g]["relay"][d], self.dev_x, self.sent)
            self.same(ref_y, self.ag[g]["sib"][2][d], self.dev_core, self.sent)

    def gather_last(self, g):
        for d in range(3):
            ref = (self.part, g, self.y1, self.x1, self.others[d], self.c)
            self.arrive(ref, self.ag[g]["relay"][d], self.dev_y if self.x_first(g, d) else self.dev_x)
            self.same(ref, self.ag[g]["sib"][3][d], self.dev_core, self.sent)

    def gather_wait(self, g):
        c = self.c1
        for j in range(4):
            self.arrive((self.part, g, j // 2, j % 2, self.z, c), self.ag[g]["core"][j], self.dev_core)
        spots = [
            (self.y, self.x),
            (self.y, self.x1),
            (self.y1, self.x),
            (self.y1, self.x1),
        ]
        for j, (jy, jx) in enumerate(spots):
            for d in range(3):
                self.arrive((self.part, g, jy, jx, self.others[d], c), self.ag[g]["sib"][j][d], self.dev_core)
        if g == 0:
            self.arrive((self.at, "vb", self.s1), self.ag_vec["core"], self.dev_core)
            for d in range(3):
                self.arrive((self.at, "vb", self.s1_others[d]), self.ag_vec["sib"][d], self.dev_core)

    def gather_drain(self):
        for copy in self.sent:
            copy().wait_send()
        self.sent = []

    def plan_sum(self):
        self.rs = [
            dict(
                core=[self.slot() for _ in range(4)],
                one=[self.slot() for _ in range(4)],
                two=[self.slot() for _ in range(4)],
                zed=[self.slot() for _ in range(3)],
                plane=[self.slot() for _ in range(3)],
            )
            for _ in range(3)
        ]
        self.rs_vec = dict(
            core=self.slot(), one=self.slot(), two=self.slot(), zed=[self.slot() for _ in range(3)]
        )
        self.out = [[], [], []]

    def grads(self, g, z, c, jy=slice(None), jx=slice(None)):
        if g == 1:
            return self.ws.at[1, jy, jx, z, c]
        return self.wd.at[z, c, jy, jx]

    def credit(self, i, device):
        pl.semaphore_signal(self.credit_sem.at[i], inc=1, device_id=device, device_id_type=MESH)

    def spend(self, g, i):
        if g != 2:
            pl.semaphore_wait(self.credit_sem.at[i], 1)

    def add(self, ref, other):
        ref, other = ref[0](*ref[1:]), other[0](*other[1:])
        ref[...] = (ref[...].astype(f32) + other[...].astype(f32)).astype(bf)

    def sum_start(self, g):
        self.spend(g, 0)
        for z in range(4):
            self.send(
                (self.grads, g, z, self.c1), (self.at, "rc", z), self.rs[g]["core"][z], self.dev_core, self.out[g]
            )
        if g == 0:
            self.send((self.at, "vs", 0), (self.at, "vr", 0), self.rs_vec["core"], self.dev_core, self.out[g])

    def sum_one(self, g):
        y, x, c = self.y, self.x, self.c
        for z in range(4):
            mine, came = (self.grads, g, z, c), (self.at, "rc", z)
            self.arrive(came, self.rs[g]["core"][z], self.dev_core)
            self.add(mine, came)
            if z == 0:
                self.spend(g, 1)
                self.spend(g, 2)
            if z < 2:
                self.send((self.grads, g, z, c, slice(None), self.x1), (self.at, "r1", z), self.rs[g]["one"][z], self.dev_x, self.out[g])
            else:
                self.send((self.grads, g, z, c, self.y1), (self.at, "r1", z), self.rs[g]["one"][z], self.dev_y, self.out[g])
        if g != 0:
            self.credit(0, self.dev_core)
        else:
            self.arrive((self.at, "vr", 0), self.rs_vec["core"], self.dev_core)
            self.vs[1] = self.vs[0] + self.vr[0]
            self.send((self.at, "vs", 1), (self.at, "vr", 1), self.rs_vec["one"], self.dev_x, self.out[g])

    def sum_two(self, g):
        y, x, c = self.y, self.x, self.c
        for z in range(4):
            came = (self.at, "r1", z)
            self.arrive(came, self.rs[g]["one"][z], self.dev_x if z < 2 else self.dev_y)
            self.add((self.grads, g, z, c, slice(None), x) if z < 2 else (self.grads, g, z, c, y), came)
            if z == 0:
                self.spend(g, 3)
                self.spend(g, 4)
            if z < 2:
                self.send((self.grads, g, z, c, self.y1, x), (self.at, "r2", z), self.rs[g]["two"][z], self.dev_y, self.out[g])
            else:
                self.send((self.grads, g, z, c, y, self.x1), (self.at, "r2", z), self.rs[g]["two"][z], self.dev_x, self.out[g])
        if g != 0:
            self.credit(1, self.dev_x)
            self.credit(2, self.dev_y)
        else:
            self.arrive((self.at, "vr", 1), self.rs_vec["one"], self.dev_x)
            self.vs[2] = self.vs[1] + self.vr[1]
            self.send((self.at, "vs", 2), (self.at, "vr", 2), self.rs_vec["two"], self.dev_y, self.out[g])

    def sum_zed(self, g):
        y, x, c = self.y, self.x, self.c
        for z in range(4):
            came = (self.at, "r2", z)
            self.arrive(came, self.rs[g]["two"][z], self.dev_y if z < 2 else self.dev_x)
            self.add((self.grads, g, z, c, y, x), came)
        for d in range(3):
            self.spend(g, 5 + d)
            self.send(
                (self.grads, g, self.others[d], c, y, x),
                (self.at, "rz", 2 - d),
                self.rs[g]["zed"][d],
                self.dev_z[d],
                self.out[g],
            )
        if g != 0:
            self.credit(3, self.dev_y)
            self.credit(4, self.dev_x)
        else:
            self.arrive((self.at, "vr", 2), self.rs_vec["two"], self.dev_y)
            self.vs[3] = self.vs[2] + self.vr[2]
            for d in range(3):
                self.send((self.at, "vs", 3), (self.at, "vr", 3 + 2 - d), self.rs_vec["zed"][d], self.dev_z[d], self.out[g])

    def sum_plane(self, g):
        total = self.grads(g, self.z, self.c, self.y, self.x)[...].astype(f32)
        for d in range(3):
            self.arrive((self.at, "rz", d), self.rs[g]["zed"][2 - d], self.dev_z[d])
            total = total + self.rz[d].astype(f32)
        own = (self.at, "gt", g, self.r)
        self.gt[g, self.r] = total.astype(bf)
        for k, device in enumerate((self.dev_x, self.dev_y, self.dev_d)):
            self.send(own, own, self.rs[g]["plane"][k], device, self.out[g])
        if g != 0:
            for d in range(3):
                self.credit(5 + 2 - d, self.dev_z[d])
        else:
            vec = self.vs[3]
            for d in range(3):
                self.arrive((self.at, "vr", 3 + d), self.rs_vec["zed"][2 - d], self.dev_z[d])
                vec = vec + self.vr[3 + d]
            self.vec_total[...] = vec

    def sum_wait(self, g):
        for k, (r, device) in enumerate(((self.rx, self.dev_x), (self.ry, self.dev_y), (self.rd, self.dev_d))):
            self.arrive((self.at, "gt", g, r), self.rs[g]["plane"][k], device)

    def sum_drain(self, g):
        for copy in self.out[g]:
            copy().wait_send()
        self.out[g] = []


def layer_kernel(linked, *refs):
    if linked:
        (tok_h, cot_h, allow_ref, vec_in, qkv_h, out_h, up_h, down_h) = refs[:8]
        (y_h, tg_h, gt_h, vg_out) = refs[8:12]
        rest = refs[12:]
    else:
        (tok_h, cot_h, allow_ref, vec_in, ws_h, wd_h) = refs[:6]
        (y_h, tg_h, g0_h, g1_h, g2_h, vg_out) = refs[6:12]
        rest = refs[12:]
    (ws, wd, x, qkv, pt, mixed, nrm1, root1, fl, act, gp, gs, gsec, cot, keep, vec_ref, vg_ref, sem) = rest[:18]
    if linked:
        names = ("vb", "rc", "r1", "r2", "rz", "gt", "vs", "vr", "send_sem", "recv_sem", "credit_sem")
        net = Links(dict(zip(names, rest[18:]), ws=ws, wd=wd, vec_total=vg_out))
        net.plan_gather()
        net.plan_sum()

    cp_x = pltpu.make_async_copy(tok_h, x, sem.at[0])
    cp_cot = pltpu.make_async_copy(cot_h, cot, sem.at[1])
    lane = lax.broadcasted_iota(jnp.int32, (CROP, 128), 1)
    low_half = lane < 64

    def half(v, h):
        return jnp.where(low_half if h == 0 else ~low_half, v, jnp.zeros_like(v))

    def vrow(r):
        return vec_ref[r : r + 1, :]

    def mat(g, j):
        if g == 2:
            return wd[j].reshape(D, D)
        return ws[g, j // 2, j % 2].reshape(D, D)

    def step(name, *a):
        return functools.partial(getattr(net, name), *a) if linked else (lambda: None)

    if linked:
        loads = []
        for j in range(4):
            src = qkv_h.at[:, j * D : (j + 1) * D] if j < 3 else out_h
            loads.append(pltpu.make_async_copy(src, gs.at[j * SUB : (j + 1) * SUB], sem.at[2 + j]))
        for j in range(4):
            loads.append(
                pltpu.make_async_copy(
                    up_h.at[:, j * D : (j + 1) * D], nrm1.at[j * SUB : (j + 1) * SUB], sem.at[6 + j]
                )
            )
        loads.append(pltpu.make_async_copy(down_h, gs.at[4 * SUB : 8 * SUB], sem.at[10]))
        for load in loads:
            load.start()
        cp_x.start()
        cp_cot.start()
        net.vb[net.s] = vec_in[...]
        for j in range(4):
            loads[j].wait()
            ws[0, j // 2, j % 2, net.z, net.c] = gs[j * SUB : (j + 1) * SUB].astype(bf)
        net.greet()
        net.gather_start(0)
        for j in range(4):
            loads[4 + j].wait()
            ws[1, j // 2, j % 2, net.z, net.c] = nrm1[j * SUB : (j + 1) * SUB].astype(bf)
        loads[8].wait()
        for j in range(4):
            wd[net.z, net.c, j // 2, j % 2] = gs[(4 + j) * SUB : (5 + j) * SUB].astype(bf)
    else:
        vec_ref[...] = vec_in[...]
        cp_ws = pltpu.make_async_copy(ws_h, ws, sem.at[2])
        cp_wd = pltpu.make_async_copy(wd_h, wd, sem.at[3])
        for copy in (cp_ws, cp_wd, cp_x, cp_cot):
            copy.start()
        cp_ws.wait()
        cp_wd.wait()
    mcol = allow_ref[...].T
    for c in range(NC):
        keep[c * CROP : (c + 1) * CROP, :] = jnp.broadcast_to(mcol[:, c : c + 1], (CROP, 128))
    vg_ref[...] = jnp.zeros_like(vg_ref)
    cp_x.wait()
    cp_cot.wait()
    if linked:
        net.gather_plane(0)
        net.gather_start(1)
        net.gather_relay(0)
        net.gather_last(0)
        net.gather_wait(0)
        row = lax.broadcasted_iota(jnp.int32, (128, D), 0)
        col = lax.broadcasted_iota(jnp.int32, (128, D), 1)
        vec = jnp.zeros((16, D), f32)
        for s in range(8):
            pick = ((col == row + s * SUB) & (row < SUB)).astype(f32).astype(bf)
            vec = vec + dg(net.vb[s], pick, 1, 0)
        vec_ref[...] = vec

    def body(c):
        r = rows_of(c)
        xv = x[r, :]
        for b in range(3):
            y = dg(xv, mat(0, b), 1, 0)
            if b == 0:
                y = y + vrow(0)
            if b == 2:
                y = y + vrow(1)
            qkv[r, b * D : (b + 1) * D] = y.astype(bf)

    crop_loop(body, {0: [step("gather_plane", 1)], 3: [step("gather_start", 2)]})

    def body(c):
        r = rows_of(c)
        kp = lanes(keep[r, :], 2) > 0.5
        for p in range(6):
            q = qkv[r, p * 128 : (p + 1) * 128] * jnp.asarray(0.125, bf)
            k = qkv[r, D + p * 128 : D + (p + 1) * 128]
            v = qkv[r, 2 * D + p * 128 : 2 * D + (p + 1) * 128]
            o = None
            for h in range(2):
                st = dg(k, half(q, h), 1, 1)
                st = jnp.where(kp, st, -1e30)
                e = jnp.exp(st - jnp.max(st, axis=0, keepdims=True))
                pr = (e * (1.0 / jnp.sum(e, axis=0, keepdims=True))).astype(bf)
                pt[c, 2 * p + h] = pr
                t = dg(pr, half(v, h), 0, 0)
                o = t if o is None else o + t
            mixed[r, p * 128 : (p + 1) * 128] = o.astype(bf)

    crop_loop(
        body,
        {
            0: [step("gather_relay", 1)],
            1: [step("gather_last", 1), step("gather_plane", 2)],
            3: [step("gather_relay", 2)],
        },
    )

    def body(c):
        r = rows_of(c)
        h = x[r, :].astype(f32) + (dg(mixed[r, :], mat(0, 3), 1, 0) + vrow(2))
        h = h - lane_mean(h)
        root = lax.rsqrt(lane_mean(h * h) + norm_epsilon)
        n = h * root
        nrm1[r, :] = n
        root1[r, :] = jnp.broadcast_to(root, (CROP, 128))
        fl[r, :] = (n * vrow(3) + vrow(4)).astype(bf)

    crop_loop(body)
    step("gather_last", 2)()
    step("gather_wait", 1)()

    def body(c):
        r = rows_of(c)
        a = fl[r, :]
        for j in range(4):
            u = dg(a, mat(1, j), 1, 0) + vrow(5 + j)
            g, d = gelu_parts(u)
            act[r, j * D : (j + 1) * D] = g.astype(bf)
            gp[r, j * D : (j + 1) * D] = d.astype(bf)

    crop_loop(body)
    step("gather_wait", 2)()

    def body(c):
        r = rows_of(c)
        s = dg(act[r, :], wd[...].reshape(FF, D), 1, 0) + vrow(9)
        h = nrm1[r, :] * vrow(3) + vrow(4) + s
        h = h - lane_mean(h)
        root = lax.rsqrt(lane_mean(h * h) + norm_epsilon)
        n = h * root
        G = cot[r, :].astype(f32) * lanes(keep[r, :], 6)
        cot[r, :] = (n * vrow(10) + vrow(11)).astype(bf)
        vg_ref[10:11, :] += jnp.sum(G * n, axis=0, keepdims=True)
        vg_ref[11:12, :] += jnp.sum(G, axis=0, keepdims=True)
        dn = G * vrow(10)
        g2 = root * (dn - lane_mean(dn) - n * lane_mean(dn * n))
        gs[r, :] = g2
        gb = g2.astype(bf)
        gsec[r, :] = gb
        vg_ref[9:10, :] += jnp.sum(gb.astype(f32), axis=0, keepdims=True)

    crop_loop(body)
    cp_y = pltpu.make_async_copy(cot, y_h, sem.at[0])
    cp_y.start()

    def body(c):
        r = rows_of(c)
        a = gsec[r, :]
        for j in range(4):
            ga = dg(a, mat(2, j), 1, 1)
            gi = (ga * gp[r, j * D : (j + 1) * D].astype(f32)).astype(bf)
            gp[r, j * D : (j + 1) * D] = gi
            vg_ref[5 + j : 6 + j, :] += jnp.sum(gi.astype(f32), axis=0, keepdims=True)

    crop_loop(body)
    step("gather_drain")()

    @pl.loop(0, 4)
    def _(i):
        m = pl.ds(pl.multiple_of(i * D, D), D)
        wd[i] = dg(act[:, m], gsec[...], 0, 0).astype(bf).reshape(2, 2, 2, SUB, D)

    step("sum_start", 2)()

    def body(c):
        r = rows_of(c)
        G = gs[r, :]
        for j in range(4):
            G = G + dg(gp[r, j * D : (j + 1) * D], mat(1, j), 1, 1)
        n = nrm1[r, :]
        vg_ref[3:4, :] += jnp.sum(G * n, axis=0, keepdims=True)
        vg_ref[4:5, :] += jnp.sum(G, axis=0, keepdims=True)
        dn = G * vrow(3)
        g1 = lanes(root1[r, :], 6) * (dn - lane_mean(dn) - n * lane_mean(dn * n))
        gs[r, :] = g1
        gb = g1.astype(bf)
        gsec[r, :] = gb
        vg_ref[2:3, :] += jnp.sum(gb.astype(f32), axis=0, keepdims=True)

    crop_loop(body, {2: [step("sum_one", 2)]})

    @pl.loop(0, 4)
    def _(j):
        g = gp[:, pl.ds(pl.multiple_of(j * D, D), D)]
        ws[1, j // 2, j % 2] = dg(fl[...], g, 0, 0).astype(bf).reshape(4, 2, SUB, D)

    step("sum_start", 1)()

    def body(c):
        r = rows_of(c)
        fl[r, :] = dg(gsec[r, :], mat(0, 3), 1, 1).astype(bf)

    crop_loop(body)
    step("sum_two", 2)()
    step("sum_one", 1)()

    def body(c):
        r = rows_of(c)
        for p in range(6):
            cq = slice(p * 128, (p + 1) * 128)
            ck = slice(D + p * 128, D + (p + 1) * 128)
            cv = slice(2 * D + p * 128, 2 * D + (p + 1) * 128)
            q = qkv[r, cq] * jnp.asarray(0.125, bf)
            k = qkv[r, ck]
            v = qkv[r, cv]
            do = fl[r, cq]
            dq = dk = dv = None
            for h in range(2):
                dom = half(do, h)
                dp = dg(v, dom, 1, 1)
                prb = pt[c, 2 * p + h]
                pr = prb.astype(f32)
                delta = jnp.sum(pr * dp, axis=0, keepdims=True)
                ds = (pr * (dp - delta)).astype(bf)
                tv = dg(prb, dom, 1, 0)
                tk = dg(ds, half(q, h), 1, 0)
                tq = dg(ds, half(k, h), 0, 0)
                dq, dk, dv = (tq, tk, tv) if dq is None else (dq + tq, dk + tk, dv + tv)
            dq = (dq * 0.125).astype(bf)
            dv = dv.astype(bf)
            act[r, cq] = dq
            act[r, ck] = dk.astype(bf)
            act[r, cv] = dv
            vg_ref[0:1, cq] += jnp.sum(dq.astype(f32), axis=0, keepdims=True)
            vg_ref[1:2, cq] += jnp.sum(dv.astype(f32), axis=0, keepdims=True)

    crop_loop(
        body,
        {
            0: [step("sum_zed", 2)],
            1: [step("sum_two", 1)],
            2: [step("sum_plane", 2)],
            3: [step("sum_zed", 1)],
        },
    )
    if linked:
        net.sum_drain(2)
        net.vs[0] = vg_ref[...]
    else:
        vg_out[...] = vg_ref[...]
        cp_g1 = pltpu.make_async_copy(ws.at[1], g1_h, sem.at[3])
        cp_g2 = pltpu.make_async_copy(wd, g2_h, sem.at[2])
        cp_g1.start()
        cp_g2.start()
        cp_g2.wait()

    for j in range(4):
        if j == 3:
            g = dg(mixed[...], gsec[...], 0, 0)
        else:
            g = dg(x[...], act[:, j * D : (j + 1) * D], 0, 0)
        wd[:, :, j // 2, j % 2] = g.astype(bf).reshape(4, 2, SUB, D)

    step("sum_start", 0)()

    def body(c):
        r = rows_of(c)
        G = gs[r, :]
        for b in range(3):
            G = G + dg(act[r, b * D : (b + 1) * D], mat(0, b), 1, 1)
        gsec[r, :] = G.astype(bf)

    crop_loop(body, {1: [step("sum_one", 0), step("sum_plane", 1)]})
    cp_tg = pltpu.make_async_copy(gsec, tg_h, sem.at[1])
    cp_tg.start()
    if linked:
        net.sum_two(0)
        net.sum_zed(0)
        net.sum_wait(2)
        net.sum_wait(1)
        net.sum_plane(0)
        net.sum_wait(0)
        cp_gt = pltpu.make_async_copy(net.gt, gt_h, sem.at[2])
        cp_gt.start()
        net.sum_drain(1)
        net.sum_drain(0)
        cp_gt.wait()
    else:
        cp_g0 = pltpu.make_async_copy(wd, g0_h, sem.at[2])
        cp_g0.start()
        cp_g0.wait()
        cp_g1.wait()
    cp_y.wait()
    cp_tg.wait()


WS = (2, 2, 2, 4, 2, SUB, D)
WD = (4, 2, 2, 2, SUB, D)


def layer(linked, *arrays):
    hbm = pl.BlockSpec(memory_space=pl.ANY)
    near = pl.BlockSpec(memory_space=pltpu.VMEM)
    VM = pltpu.VMEM
    shape = jax.ShapeDtypeStruct
    outs = [(shape((T, D), bf), hbm), (shape((T, D), bf), hbm)]
    if linked:
        outs += [(shape((3, 4, SUB, D), bf), hbm)]
    else:
        outs += [(shape(WD, bf), hbm), (shape(WS[1:], bf), hbm), (shape(WD, bf), hbm)]
    outs += [(shape((16, D), f32), near)]
    scratch = [
        VM(WS, bf),
        VM(WD, bf),
        VM((T, D), bf),
        VM((T, 3 * D), bf),
        VM((NC, H, CROP, CROP), bf),
        VM((T, D), bf),
        VM((T, D), f32),
        VM((T, 128), f32),
        VM((T, D), bf),
        VM((T, FF), bf),
        VM((T, FF), bf),
        VM((T, D), f32),
        VM((T, D), bf),
        VM((T, D), bf),
        VM((T, 128), f32),
        VM((16, D), f32),
        VM((16, D), f32),
        pltpu.SemaphoreType.DMA((11,)),
    ]
    params = dict(vmem_limit_bytes=63 * 2**20)
    if linked:
        transfers = 3 * (4 + 3 + 3 + 3 + 3 + 12) + 7 + 3 * (4 + 4 + 4 + 3 + 3) + 6
        scratch += [
            VM((8, 16, 128), bf),
            VM((4, 2, 2, SUB, D), bf),
            VM((4, 2, SUB, D), bf),
            VM((4, SUB, D), bf),
            VM((3, SUB, D), bf),
            VM((3, 4, SUB, D), bf),
            VM((4, 16, D), f32),
            VM((6, 16, D), f32),
            pltpu.SemaphoreType.DMA((transfers,)),
            pltpu.SemaphoreType.DMA((transfers,)),
            pltpu.SemaphoreType.REGULAR((8,)),
        ]
        params.update(collective_id=0, has_side_effects=True)
    return pl.pallas_call(
        functools.partial(layer_kernel, linked),
        out_shape=[o[0] for o in outs],
        in_specs=[hbm, hbm, near, near] + [hbm] * (len(arrays) - 4),
        out_specs=[o[1] for o in outs],
        scratch_shapes=scratch,
        compiler_params=pltpu.CompilerParams(**params),
    )(*arrays)


def adam_update(gradient, first_moment, second_moment):
    first_new = decay_first * first_moment + (1.0 - decay_first) * gradient
    second_new = decay_second * second_moment + (1.0 - decay_second) * gradient * gradient
    step_dir = first_new / correct_first / (jnp.sqrt(second_new / correct_second) + adam_epsilon)
    return (step_dir, first_new)


def allowed_rows(deletion, lengths):
    places = jnp.arange(CROP, dtype=jnp.int32)[None, :]
    allowed = ((deletion == 1) | (places == 0)) & (places < lengths[:, None])
    return jnp.pad(allowed.astype(f32), ((0, 8 - NC), (0, 0)))


def finish(output, token_grad, gradients, moments):
    updated = [adam_update(g, m, s) for g, m, s in zip(gradients, moments[:5], moments[5:])]
    return (
        (output, token_grad)
        + tuple(gradients)
        + tuple(u[0] for u in updated)
        + tuple(u[1] for u in updated)
    )


def side_by_side(blocks):
    return jnp.concatenate([blocks[j] for j in range(blocks.shape[0])], axis=1)


def per_device_linked(tokens, cotangent, deletion, lengths, qkv, out, up, down, vectors, *moments):
    vec = jnp.pad(vectors.astype(bf), ((0, 4), (0, 128 - vectors.shape[1])))
    output, token_grad, sums, vector_sums = layer(
        True, tokens, cotangent, allowed_rows(deletion, lengths), vec, qkv, out, up, down
    )
    sums = sums.astype(f32)
    width = vectors.shape[1]
    vec = lax.dynamic_slice(vector_sums, (0, lax.axis_index("shard") * width), (12, width))
    gradients = (
        side_by_side(sums[0, :3]),
        sums[0, 3],
        side_by_side(sums[1]),
        sums[2].reshape(4 * SUB, D),
        vec,
    )
    return finish(output, token_grad, gradients, moments)


def per_device_plain(tokens, cotangent, deletion, lengths, qkv, out, up, down, vectors, *moments):
    blocks = [qkv[:, b * D : (b + 1) * D] for b in range(3)] + [out]
    blocks += [up[:, b * D : (b + 1) * D] for b in range(4)]
    square = lax.all_gather(jnp.stack(blocks).astype(bf), "shard", axis=1, tiled=True)
    tall = lax.all_gather(down.astype(bf), "shard", axis=0, tiled=True)
    vec = lax.all_gather(vectors.astype(bf), "shard", axis=1, tiled=True).astype(f32)
    output, token_grad, g0, g1, g2, vec = layer(
        False,
        tokens,
        cotangent,
        allowed_rows(deletion, lengths),
        jnp.pad(vec, ((0, 4), (0, 0))),
        square.reshape(WS),
        tall.reshape(WD),
    )
    g0 = g0.transpose(2, 3, 0, 1, 4, 5).reshape(4, D, D)
    square = lax.psum_scatter(
        jnp.concatenate([g0, g1.reshape(4, D, D)]).astype(f32), "shard", scatter_dimension=1, tiled=True
    )
    tall = lax.psum_scatter(g2.reshape(FF, D).astype(f32), "shard", scatter_dimension=0, tiled=True)
    vec = lax.psum_scatter(vec[:12], "shard", scatter_dimension=1, tiled=True)
    square, tall, vec = (lax.psum(g.astype(bf), "rep").astype(f32) for g in (square, tall, vec))
    gradients = (side_by_side(square[:3]), square[3], side_by_side(square[4:]), tall, vec)
    return finish(output, token_grad, gradients, moments)


def solution(mesh):
    rows = P(("rep", "shard"), None)
    weights = (P("shard", None),) * 4 + (P(None, "shard"),)
    linked = mesh.shape["rep"] == 4 and mesh.shape["shard"] == 8
    return jax.shard_map(
        per_device_linked if linked else per_device_plain,
        mesh=mesh,
        in_specs=(rows, rows, rows, P(("rep", "shard"))) + weights * 3,
        out_specs=(rows, rows) + weights * 3,
        check_vma=False,
    )
```

```python
import functools
import math

import jax
import jax.numpy as jnp
from jax import lax
from jax.experimental import pallas as pl
from jax.experimental.pallas import tpu as pltpu
from jax.sharding import PartitionSpec as P

D = 768
H = 12
FF = 3072
CROP = 256
T = 1024
NC = 4
SUB = 96
bf = jnp.bfloat16
f32 = jnp.float32
MESH = pl.DeviceIdType.MESH

norm_epsilon = 1e-06
decay_first = 0.9
decay_second = 0.999
correct_first = 1.0 - 2.6561398887587544e-05
correct_second = 0.0952078528862904
adam_epsilon = 1e-08


def dg(a, b, ca, cb):
    return lax.dot_general(a, b, (((ca,), (cb,)), ((), ())), preferred_element_type=f32)


def rows_of(c):
    return pl.ds(pl.multiple_of(c * CROP, CROP), CROP)


def third(t):
    return slice(t * 256, (t + 1) * 256)


def columns(g):
    return third(g) if g < 3 else slice((g + 1) % 2 * 384, (g + 1) % 2 * 384 + 384)


def lane_mean(v):
    return jnp.sum(v, axis=-1, keepdims=True) * (1.0 / D)


def lanes(v, n):
    return jnp.concatenate([v] * n, axis=1)


def gelu_parts(u):
    density = jnp.exp(u * u * -0.5) * (1.0 / math.sqrt(2.0 * math.pi))
    cdf = 0.5 * (1.0 + lax.erf(u * math.sqrt(0.5)))
    return u * cdf, cdf + u * density


def crop_loop(body, after=None):
    @pl.loop(0, NC)
    def _(c):
        body(c)
        for k, steps in (after or {}).items():

            @pl.when(c == k)
            def _():
                for step in steps:
                    step()


class Links:
    def __init__(self, refs):
        self.__dict__.update(refs)
        r = lax.axis_index("rep")
        s = lax.axis_index("shard")
        self.y, self.x = r // 2, r % 2
        self.z, self.c = s // 2, s % 2
        self.r, self.s = r, s
        self.rx = self.y * 2 + 1 - self.x
        self.ry = (1 - self.y) * 2 + self.x
        self.rd = 3 - r
        self.others = [(self.z + d) % 4 for d in (1, 2, 3)]
        self.dev_core = (r, self.z * 2 + 1 - self.c)
        self.dev_x = (self.rx, s)
        self.dev_y = (self.ry, s)
        self.dev_d = (self.rd, s)
        self.dev_z = [(r, z * 2 + self.c) for z in self.others]
        self.x1, self.y1, self.c1 = 1 - self.x, 1 - self.y, 1 - self.c
        self.s1 = self.z * 2 + self.c1
        self.s_others = [z * 2 + self.c for z in self.others]
        self.s1_others = [z * 2 + self.c1 for z in self.others]
        self.count = 0
        self.sent = []

    def greet(self):
        barrier = pltpu.get_barrier_semaphore()
        partners = [self.dev_core, self.dev_x, self.dev_y, self.dev_d] + self.dev_z
        for device in partners:
            pl.semaphore_signal(barrier, inc=1, device_id=device, device_id_type=MESH)

    def greeted(self):
        pl.semaphore_wait(pltpu.get_barrier_semaphore(), 7)

    def slot(self):
        self.count += 1
        return self.count - 1

    def copy(self, src, dst, k, device):
        return pltpu.make_async_remote_copy(
            src_ref=src,
            dst_ref=dst,
            send_sem=self.send_sem.at[k],
            recv_sem=self.recv_sem.at[k],
            device_id=device,
            device_id_type=MESH,
        )

    def part(self, g, jy, jx, z, c):
        if g > 4:
            return self.wd.at[z, c, jy, jx, :, columns(g)]
        return self.ws.at[g // 3, jy, jx, z, c, :, columns(g)]

    def plan_gather(self):
        self.ag = [
            dict(
                core=[self.slot() for _ in range(4)],
                zed=[self.slot() for _ in range(3)],
                px=[self.slot() for _ in range(3)],
                py=[self.slot() for _ in range(3)],
                relay=[self.slot() for _ in range(3)],
                sib=[[self.slot() for _ in range(3)] for _ in range(4)],
            )
            for _ in range(7)
        ]
        self.ag_vec = dict(
            core=self.slot(), zed=[self.slot() for _ in range(3)], sib=[self.slot() for _ in range(3)]
        )

    def send(self, src, dst, k, device, keep):
        def describe():
            return self.copy(src[0](*src[1:]), dst[0](*dst[1:]), k, device)

        describe().start()
        keep.append(describe)

    def at(self, name, *index):
        return getattr(self, name).at[index if len(index) > 1 else index[0]]

    def same(self, ref, k, device, keep):
        self.send(ref, ref, k, device, keep)

    def arrive(self, ref, k, device):
        self.copy(ref[0](*ref[1:]), ref[0](*ref[1:]), k, device).wait_recv()

    def gather_start(self, g):
        for j in range(4):
            self.same(
                (self.part, g, j // 2, j % 2, self.z, self.c), self.ag[g]["core"][j], self.dev_core, self.sent
            )
        own = (self.part, g, self.y, self.x, self.z, self.c)
        for d in range(3):
            self.same(own, self.ag[g]["zed"][d], self.dev_z[d], self.sent)
        if g == 0:
            block = (self.at, "vb", self.s)
            self.same(block, self.ag_vec["core"], self.dev_core, self.sent)
            for d in range(3):
                self.same(block, self.ag_vec["zed"][d], self.dev_z[d], self.sent)

    def x_first(self, g, d):
        return (d != 1) == (g % 2 == 0)

    def gather_plane(self, g):
        for d in range(3):
            z, k = self.others[d], 2 - d
            ref = (self.part, g, self.y, self.x, z, self.c)
            self.arrive(ref, self.ag[g]["zed"][k], self.dev_z[d])
            self.same(ref, self.ag[g]["px"][d], self.dev_x, self.sent)
            self.same(ref, self.ag[g]["py"][d], self.dev_y, self.sent)
            self.same(ref, self.ag[g]["sib"][0][d], self.dev_core, self.sent)
            if g == 0:
                block = (self.at, "vb", self.s_others[d])
                self.arrive(block, self.ag_vec["zed"][k], self.dev_z[d])
                self.same(block, self.ag_vec["sib"][d], self.dev_core, self.sent)

    def gather_relay(self, g):
        for d in range(3):
            z = self.others[d]
            ref_x = (self.part, g, self.y, self.x1, z, self.c)
            self.arrive(ref_x, self.ag[g]["px"][d], self.dev_x)
            if self.x_first(g, d):
                self.same(ref_x, self.ag[g]["relay"][d], self.dev_y, self.sent)
            self.same(ref_x, self.ag[g]["sib"][1][d], self.dev_core, self.sent)
            ref_y = (self.part, g, self.y1, self.x, z, self.c)
            self.arrive(ref_y, self.ag[g]["py"][d], self.dev_y)
            if not self.x_first(g, d):
                self.same(ref_y, self.ag[g]["relay"][d], self.dev_x, self.sent)
            self.same(ref_y, self.ag[g]["sib"][2][d], self.dev_core, self.sent)

    def gather_last(self, g):
        for d in range(3):
            ref = (self.part, g, self.y1, self.x1, self.others[d], self.c)
            self.arrive(ref, self.ag[g]["relay"][d], self.dev_y if self.x_first(g, d) else self.dev_x)
            self.same(ref, self.ag[g]["sib"][3][d], self.dev_core, self.sent)

    def gather_wait(self, g):
        c = self.c1
        for j in range(4):
            self.arrive((self.part, g, j // 2, j % 2, self.z, c), self.ag[g]["core"][j], self.dev_core)
        spots = [
            (self.y, self.x),
            (self.y, self.x1),
            (self.y1, self.x),
            (self.y1, self.x1),
        ]
        for j, (jy, jx) in enumerate(spots):
            for d in range(3):
                self.arrive((self.part, g, jy, jx, self.others[d], c), self.ag[g]["sib"][j][d], self.dev_core)
        if g == 0:
            self.arrive((self.at, "vb", self.s1), self.ag_vec["core"], self.dev_core)
            for d in range(3):
                self.arrive((self.at, "vb", self.s1_others[d]), self.ag_vec["sib"][d], self.dev_core)

    def gather_drain(self):
        for copy in self.sent:
            copy().wait_send()
        self.sent = []

    def plan_sum(self):
        self.rs = [
            dict(
                core=[self.slot() for _ in range(4)],
                one=[self.slot() for _ in range(4)],
                two=[self.slot() for _ in range(4)],
                zed=[self.slot() for _ in range(3)],
                plane=[self.slot() for _ in range(3)],
            )
            for _ in range(7)
        ]
        self.rs_vec = dict(
            core=self.slot(), one=self.slot(), two=self.slot(), zed=[self.slot() for _ in range(3)]
        )
        self.out = [[] for _ in range(7)]

    def grads(self, g, z, c, jy=slice(None), jx=slice(None)):
        if g > 2:
            return self.part(g, jy, jx, z, c)
        return self.gp.at[jy, jx, pl.ds(pl.multiple_of((z * 2 + c) * SUB, SUB), SUB), third(g)]

    def land(self, name, g, *index):
        ref = getattr(self, name if name == "rc" or g > 2 else name + "t")
        return ref.at[index + (slice(None),) * (len(ref.shape) - len(index) - 1) + (columns(g),)]

    def total(self, g, r):
        return self.gt.at[0 if g < 3 else (g - 1) // 2, r, :, columns(g)]

    def credit(self, g, i, device):
        if g > 4 or (g > 2 and i == 0):
            pl.semaphore_signal(self.credit_sem.at[(g + 1) % 2 * 8 + i], inc=1, device_id=device, device_id_type=MESH)

    def spend(self, g, i):
        for h in range(2):
            if g == 3 + h or (g == 0 and i == 0):
                pl.semaphore_wait(self.credit_sem.at[h * 8 + i], 1)

    def add(self, ref, other):
        ref, other = ref[0](*ref[1:]), other[0](*other[1:])
        ref[...] = (ref[...].astype(f32) + other[...].astype(f32)).astype(bf)

    def sum_start(self, g):
        self.spend(g, 0)
        for z in range(4):
            self.send(
                (self.grads, g, z, self.c1), (self.land, "rc", g, z), self.rs[g]["core"][z], self.dev_core, self.out[g]
            )
        if g == 2:
            self.send((self.at, "vs", 0), (self.at, "vr", 0), self.rs_vec["core"], self.dev_core, self.out[g])

    def sum_one(self, g):
        y, x, c = self.y, self.x, self.c
        for z in range(4):
            mine, came = (self.grads, g, z, c), (self.land, "rc", g, z)
            self.arrive(came, self.rs[g]["core"][z], self.dev_core)
            self.add(mine, came)
            if z == 0:
                self.spend(g, 1)
                self.spend(g, 2)
            if z < 2:
                self.send((self.grads, g, z, c, slice(None), self.x1), (self.land, "r1", g, z), self.rs[g]["one"][z], self.dev_x, self.out[g])
            else:
                self.send((self.grads, g, z, c, self.y1), (self.land, "r1", g, z), self.rs[g]["one"][z], self.dev_y, self.out[g])
        self.credit(g, 0, self.dev_core)
        if g == 2:
            self.arrive((self.at, "vr", 0), self.rs_vec["core"], self.dev_core)
            self.vs[1] = self.vs[0] + self.vr[0]
            self.send((self.at, "vs", 1), (self.at, "vr", 1), self.rs_vec["one"], self.dev_x, self.out[g])

    def sum_two(self, g):
        y, x, c = self.y, self.x, self.c
        for z in range(4):
            came = (self.land, "r1", g, z)
            self.arrive(came, self.rs[g]["one"][z], self.dev_x if z < 2 else self.dev_y)
            self.add((self.grads, g, z, c, slice(None), x) if z < 2 else (self.grads, g, z, c, y), came)
            if z == 0:
                self.spend(g, 3)
                self.spend(g, 4)
            if z < 2:
                self.send((self.grads, g, z, c, self.y1, x), (self.land, "r2", g, z), self.rs[g]["two"][z], self.dev_y, self.out[g])
            else:
                self.send((self.grads, g, z, c, y, self.x1), (self.land, "r2", g, z), self.rs[g]["two"][z], self.dev_x, self.out[g])
        self.credit(g, 1, self.dev_x)
        self.credit(g, 2, self.dev_y)
        if g == 2:
            self.arrive((self.at, "vr", 1), self.rs_vec["one"], self.dev_x)
            self.vs[2] = self.vs[1] + self.vr[1]
            self.send((self.at, "vs", 2), (self.at, "vr", 2), self.rs_vec["two"], self.dev_y, self.out[g])

    def sum_zed(self, g):
        y, x, c = self.y, self.x, self.c
        for z in range(4):
            came = (self.land, "r2", g, z)
            self.arrive(came, self.rs[g]["two"][z], self.dev_y if z < 2 else self.dev_x)
            self.add((self.grads, g, z, c, y, x), came)
        for d in range(3):
            self.spend(g, 5 + d)
            self.send(
                (self.grads, g, self.others[d], c, y, x),
                (self.land, "rz", g, 2 - d),
                self.rs[g]["zed"][d],
                self.dev_z[d],
                self.out[g],
            )
        self.credit(g, 3, self.dev_y)
        self.credit(g, 4, self.dev_x)
        if g == 2:
            self.arrive((self.at, "vr", 2), self.rs_vec["two"], self.dev_y)
            self.vs[3] = self.vs[2] + self.vr[2]
            for d in range(3):
                self.send((self.at, "vs", 3), (self.at, "vr", 3 + 2 - d), self.rs_vec["zed"][d], self.dev_z[d], self.out[g])

    def sum_plane(self, g):
        total = self.grads(g, self.z, self.c, self.y, self.x)[...].astype(f32)
        for d in range(3):
            self.arrive((self.land, "rz", g, d), self.rs[g]["zed"][2 - d], self.dev_z[d])
            total = total + self.land("rz", g, d)[...].astype(f32)
        own = (self.total, g, self.r)
        self.total(g, self.r)[...] = total.astype(bf)
        for k, device in enumerate((self.dev_x, self.dev_y, self.dev_d)):
            self.send(own, own, self.rs[g]["plane"][k], device, self.out[g])
        for d in range(3):
            self.credit(g, 5 + 2 - d, self.dev_z[d])
        if g == 2:
            vec = self.vs[3]
            for d in range(3):
                self.arrive((self.at, "vr", 3 + d), self.rs_vec["zed"][2 - d], self.dev_z[d])
                vec = vec + self.vr[3 + d]
            self.vec_total[...] = pltpu.roll(vec, lax.rem(D - self.s * SUB, D), 1)[:, 0:128]

    def sum_wait(self, g):
        for k, (r, device) in enumerate(((self.rx, self.dev_x), (self.ry, self.dev_y), (self.rd, self.dev_d))):
            self.arrive((self.total, g, r), self.rs[g]["plane"][k], device)

    def sum_drain(self, g):
        for copy in self.out[g]:
            copy().wait_send()
        self.out[g] = []


def layer_kernel(linked, *refs):
    if linked:
        (tok_h, cot_h, del_ref, len_ref, vec_in, qkv_h, out_h, up_h, down_h) = refs[:9]
        (y_h, tg_h, t0_h, t1_h, t2_h, vg_out) = refs[9:15]
        rest = refs[15:]
    else:
        (tok_h, cot_h, del_ref, len_ref, vec_in, ws_h, wd_h) = refs[:7]
        (y_h, tg_h, g0_h, g1_h, g2_h, vg_out) = refs[7:13]
        rest = refs[13:]
    (ws, wd, x, qkv, pt, mixed, nrm1, root1, fl, act, gp, gs, gsec, cot, keep, vec_ref, vg_ref, sem) = rest[:18]
    if linked:
        names = ("vb", "rc", "r1", "r2", "rz", "r1t", "r2t", "rzt", "gt", "vs", "vr", "send_sem", "recv_sem", "credit_sem")
        net = Links(dict(zip(names, rest[18:]), ws=ws, wd=wd, gp=gp, vec_total=vg_out))
        net.plan_gather()
        net.plan_sum()

    cp_x = pltpu.make_async_copy(tok_h, x, sem.at[0])
    cp_cot = pltpu.make_async_copy(cot_h, cot, sem.at[1])
    lane = lax.broadcasted_iota(jnp.int32, (CROP, 128), 1)
    low_half = lane < 64

    def half(v, h):
        return jnp.where(low_half if h == 0 else ~low_half, v, jnp.zeros_like(v))

    def vrow(r):
        return vec_ref[r : r + 1, :]

    def mat(g, j):
        if g == 2:
            return wd[j].reshape(D, D)
        return ws[g, j // 2, j % 2].reshape(D, D)

    def mat_third(j, t):
        return ws[0, j // 2, j % 2, :, :, :, third(t)].reshape(D, 256)

    def step(name, *a):
        return functools.partial(getattr(net, name), *a) if linked else (lambda: None)

    if linked:
        net.greet()
        loads = []
        for j in range(4):
            src = qkv_h.at[:, j * D : (j + 1) * D] if j < 3 else out_h
            loads.append(pltpu.make_async_copy(src, gs.at[j * SUB : (j + 1) * SUB], sem.at[2 + j]))
        for j in range(4):
            loads.append(
                pltpu.make_async_copy(
                    up_h.at[:, j * D : (j + 1) * D], nrm1.at[j * SUB : (j + 1) * SUB], sem.at[6 + j]
                )
            )
        loads.append(pltpu.make_async_copy(down_h, gs.at[4 * SUB : 8 * SUB], sem.at[10]))
        for load in loads:
            load.start()
        cp_x.start()
        cp_cot.start()
        net.vs[0, :, 0:128] = jnp.zeros((16, 128), f32)
        net.vs[0, 0 : vec_in.shape[0], 0 : vec_in.shape[1]] = vec_in[...]
        net.vb[net.s] = net.vs[0, :, 0:128].astype(bf)
        for j in range(4):
            loads[j].wait()
            ws[0, j // 2, j % 2, net.z, net.c] = gs[j * SUB : (j + 1) * SUB].astype(bf)
        net.greeted()
        net.gather_start(0)
        for j in range(4):
            loads[4 + j].wait()
            ws[1, j // 2, j % 2, net.z, net.c] = nrm1[j * SUB : (j + 1) * SUB].astype(bf)
        loads[8].wait()
        for j in range(4):
            wd[net.z, net.c, j // 2, j % 2] = gs[(4 + j) * SUB : (5 + j) * SUB].astype(bf)
    else:
        vec_ref[...] = vec_in[...]
        cp_ws = pltpu.make_async_copy(ws_h, ws, sem.at[2])
        cp_wd = pltpu.make_async_copy(wd_h, wd, sem.at[3])
        for copy in (cp_ws, cp_wd, cp_x, cp_cot):
            copy.start()
        cp_ws.wait()
        cp_wd.wait()
    place = lax.broadcasted_iota(jnp.int32, (1, CROP), 1)
    allowed = [
        jnp.where(((del_ref[c : c + 1, :] == 1) | (place == 0)) & (place < len_ref[c]), 1.0, 0.0) for c in range(NC)
    ]
    mcol = jnp.concatenate(allowed * (8 // NC), axis=0).T
    for c in range(NC):
        keep[c * CROP : (c + 1) * CROP, :] = jnp.broadcast_to(mcol[:, c : c + 1], (CROP, 128)).astype(bf)
    vg_ref[...] = jnp.zeros_like(vg_ref)
    cp_x.wait()
    cp_cot.wait()
    if linked:
        net.gather_plane(0)
        net.gather_start(1)
        net.gather_relay(0)
        net.gather_plane(1)
        net.gather_start(2)
        net.gather_last(0)
        net.gather_wait(0)
        row = lax.broadcasted_iota(jnp.int32, (128, D), 0)
        col = lax.broadcasted_iota(jnp.int32, (128, D), 1)
        vec = jnp.zeros((16, D), f32)
        for s in range(8):
            pick = ((col == row + s * SUB) & (row < SUB)).astype(f32).astype(bf)
            vec = vec + dg(net.vb[s], pick, 1, 0)
        vec_ref[...] = vec

    def project(t, c):
        r = rows_of(c)
        xv = x[r, :]
        for b in range(3):
            y = dg(xv, mat_third(b, t), 1, 0)
            if b == 0:
                y = y + vec_ref[0:1, third(t)]
            if b == 2:
                y = y + vec_ref[1:2, third(t)]
            qkv[r, t * D + b * 256 : t * D + (b + 1) * 256] = y.astype(bf)

    def attend(t, c):
        r = rows_of(c)
        kp = lanes(keep[r, :].astype(f32), 2) > 0.5
        for p in range(2):
            q, k, v = (qkv[r, t * D + b * 256 + p * 128 : t * D + b * 256 + (p + 1) * 128] for b in range(3))
            q = q * jnp.asarray(0.125, bf)
            o = None
            for h in range(2):
                st = dg(k, half(q, h), 1, 1)
                st = jnp.where(kp, st, -1e30)
                e = jnp.exp(st - jnp.max(st, axis=0, keepdims=True))
                pr = (e * (1.0 / jnp.sum(e, axis=0, keepdims=True))).astype(bf)
                pt[c, 4 * t + 2 * p + h] = pr
                w = dg(pr, half(v, h), 0, 0)
                o = w if o is None else o + w
            mixed[r, t * 256 + p * 128 : t * 256 + (p + 1) * 128] = o.astype(bf)

    crop_loop(functools.partial(project, 0), {0: [step("gather_relay", 1), step("gather_plane", 2), step("gather_start", 3)]})
    crop_loop(
        functools.partial(attend, 0),
        {
            1: [step("gather_last", 1), step("gather_relay", 2)],
            3: [step("gather_wait", 1), step("gather_plane", 3), step("gather_start", 4), step("gather_last", 2)],
        },
    )
    crop_loop(functools.partial(project, 1))
    crop_loop(
        functools.partial(attend, 1),
        {
            1: [step("gather_wait", 2), step("gather_relay", 3)],
            3: [step("gather_plane", 4), step("gather_start", 5), step("gather_last", 3)],
        },
    )
    crop_loop(functools.partial(project, 2))
    crop_loop(
        functools.partial(attend, 2),
        {1: [step("gather_relay", 4)], 3: [step("gather_plane", 5), step("gather_start", 6), step("gather_last", 4)]},
    )

    def body(c):
        r = rows_of(c)
        h = x[r, :].astype(f32) + (dg(mixed[r, :], mat(0, 3), 1, 0) + vrow(2))
        h = h - lane_mean(h)
        root = lax.rsqrt(lane_mean(h * h) + norm_epsilon)
        n = h * root
        nrm1[r, :] = n
        root1[r, :] = jnp.broadcast_to(root, (CROP, 128))
        fl[r, :] = (n * vrow(3) + vrow(4)).astype(bf)

    crop_loop(
        body, {1: [step("gather_wait", 3)], 3: [step("gather_wait", 4), step("gather_relay", 5)]}
    )

    def body(c):
        r = rows_of(c)
        a = fl[r, :]
        for j in range(4):
            u = dg(a, mat(1, j), 1, 0) + vrow(5 + j)
            g, d = gelu_parts(u)
            act[r, j * D : (j + 1) * D] = g.astype(bf)
            gp[j // 2, j % 2, r, :] = d.astype(bf)

    crop_loop(
        body,
        {
            0: [step("gather_last", 5)],
            1: [step("gather_plane", 6)],
            3: [step("gather_wait", 5), step("gather_relay", 6), step("gather_last", 6), step("gather_wait", 6)],
        },
    )

    def body(c):
        r = rows_of(c)
        s = dg(act[r, :], wd[...].reshape(FF, D), 1, 0) + vrow(9)
        h = nrm1[r, :] * vrow(3) + vrow(4) + s
        h = h - lane_mean(h)
        root = lax.rsqrt(lane_mean(h * h) + norm_epsilon)
        n = h * root
        G = cot[r, :].astype(f32) * lanes(keep[r, :].astype(f32), 6)
        cot[r, :] = (n * vrow(10) + vrow(11)).astype(bf)
        vg_ref[10:11, :] += jnp.sum(G * n, axis=0, keepdims=True)
        vg_ref[11:12, :] += jnp.sum(G, axis=0, keepdims=True)
        dn = G * vrow(10)
        g2 = root * (dn - lane_mean(dn) - n * lane_mean(dn * n))
        gs[r, :] = g2
        gb = g2.astype(bf)
        gsec[r, :] = gb
        vg_ref[9:10, :] += jnp.sum(gb.astype(f32), axis=0, keepdims=True)

    crop_loop(body)
    cp_y = pltpu.make_async_copy(cot, y_h, sem.at[0])
    cp_y.start()

    def body(c):
        r = rows_of(c)
        a = gsec[r, :]
        for j in range(4):
            ga = dg(a, mat(2, j), 1, 1)
            gi = (ga * gp[j // 2, j % 2, r, :].astype(f32)).astype(bf)
            gp[j // 2, j % 2, r, :] = gi
            vg_ref[5 + j : 6 + j, :] += jnp.sum(gi.astype(f32), axis=0, keepdims=True)

    crop_loop(body)
    step("gather_drain")()

    @pl.loop(0, 4)
    def _(i):
        m = pl.ds(pl.multiple_of(i * D, D), D)
        wd[i] = dg(act[:, m], gsec[...], 0, 0).astype(bf).reshape(2, 2, 2, SUB, D)

    step("sum_start", 5)()
    step("sum_start", 6)()

    def body(c):
        r = rows_of(c)
        G = gs[r, :]
        for j in range(4):
            G = G + dg(gp[j // 2, j % 2, r, :], mat(1, j), 1, 1)
        n = nrm1[r, :]
        vg_ref[3:4, :] += jnp.sum(G * n, axis=0, keepdims=True)
        vg_ref[4:5, :] += jnp.sum(G, axis=0, keepdims=True)
        dn = G * vrow(3)
        g1 = lanes(root1[r, :], 6) * (dn - lane_mean(dn) - n * lane_mean(dn * n))
        gs[r, :] = g1
        gb = g1.astype(bf)
        gsec[r, :] = gb
        vg_ref[2:3, :] += jnp.sum(gb.astype(f32), axis=0, keepdims=True)

    crop_loop(body, {1: [step("sum_one", 5), step("sum_one", 6)]})

    @pl.loop(0, 4)
    def _(j):
        g = gp[j // 2, j % 2]
        ws[1, j // 2, j % 2] = dg(fl[...], g, 0, 0).astype(bf).reshape(4, 2, SUB, D)

        @pl.when(j == 1)
        def _():
            step("sum_two", 5)()

    step("sum_start", 3)()
    step("sum_start", 4)()

    def body(c):
        r = rows_of(c)
        fl[r, :] = dg(gsec[r, :], mat(0, 3), 1, 1).astype(bf)

    crop_loop(body, {3: [step("sum_two", 6)]})

    def attend_back(t, c):
        r = rows_of(c)
        for p in range(2):
            at = [slice(t * D + b * 256 + p * 128, t * D + b * 256 + (p + 1) * 128) for b in range(3)]
            cols = slice(t * 256 + p * 128, t * 256 + (p + 1) * 128)
            q, k, v = (qkv[r, cut] for cut in at)
            q = q * jnp.asarray(0.125, bf)
            do = fl[r, cols]
            dq = dk = dv = None
            for h in range(2):
                dom = half(do, h)
                dp = dg(v, dom, 1, 1)
                prb = pt[c, 4 * t + 2 * p + h]
                pr = prb.astype(f32)
                delta = jnp.sum(pr * dp, axis=0, keepdims=True)
                ds = (pr * (dp - delta)).astype(bf)
                tv = dg(prb, dom, 1, 0)
                tk = dg(ds, half(q, h), 1, 0)
                tq = dg(ds, half(k, h), 0, 0)
                dq, dk, dv = (tq, tk, tv) if dq is None else (dq + tq, dk + tk, dv + tv)
            dq = (dq * 0.125).astype(bf)
            dv = dv.astype(bf)
            act[r, at[0]] = dq
            act[r, at[1]] = dk.astype(bf)
            act[r, at[2]] = dv
            vg_ref[0:1, cols] += jnp.sum(dq.astype(f32), axis=0, keepdims=True)
            vg_ref[1:2, cols] += jnp.sum(dv.astype(f32), axis=0, keepdims=True)

    def third_grads(t):
        g = dg(x[...], act[:, t * D : (t + 1) * D], 0, 0).astype(bf)
        for j in range(3):
            gp[j // 2, j % 2, 0:D, third(t)] = g[:, third(j)]
        gp[1, 1, 0:D, third(t)] = dg(mixed[...], gsec[:, third(t)], 0, 0).astype(bf)

    crop_loop(
        functools.partial(attend_back, 0),
        {1: [step("sum_one", 3), step("sum_one", 4)], 3: [step("sum_zed", 5), step("sum_zed", 6)]},
    )
    third_grads(0)
    step("sum_start", 0)()
    crop_loop(
        functools.partial(attend_back, 1),
        {1: [step("sum_two", 3), step("sum_one", 0)], 3: [step("sum_plane", 5), step("sum_two", 4)]},
    )
    third_grads(1)
    step("sum_start", 1)()
    crop_loop(
        functools.partial(attend_back, 2),
        {
            1: [step("sum_two", 0), step("sum_one", 1), step("sum_plane", 6)],
            3: [step("sum_zed", 3)],
        },
    )
    if linked:
        net.vs[0] = vg_ref[...]
    third_grads(2)
    step("sum_start", 2)()

    def body(c):
        r = rows_of(c)
        G = gs[r, :]
        for b in range(3):
            for t in range(3):
                G = G + dg(act[r, t * D + b * 256 : t * D + (b + 1) * 256], mat_third(b, t), 1, 1)
        gsec[r, :] = G.astype(bf)

    crop_loop(
        body,
        {
            0: [step("sum_zed", 4)],
            1: [step("sum_one", 2), step("sum_two", 1), step("sum_zed", 0)],
            2: [step("sum_plane", 3)],
            3: [step("sum_two", 2), step("sum_zed", 1)],
        },
    )
    cp_tg = pltpu.make_async_copy(gsec, tg_h, sem.at[1])
    cp_tg.start()
    if linked:
        net.sum_plane(4)
        net.sum_plane(0)
        net.sum_zed(2)
        net.sum_plane(1)
        for g in (5, 6, 3, 4, 0, 1):
            net.sum_wait(g)
        net.sum_plane(2)
        net.sum_wait(2)
        shares = [pltpu.make_async_copy(net.gt.at[i], t_h, sem.at[2 + i]) for i, t_h in enumerate((t0_h, t1_h, t2_h))]
        for copy in shares:
            copy.start()
        for g in range(7):
            net.sum_drain(g)
        for copy in shares:
            copy.wait()
    else:
        vg_out[...] = vg_ref[...]
        copies = [
            pltpu.make_async_copy(gp.at[:, :, 0:D], g0_h, sem.at[2]),
            pltpu.make_async_copy(ws.at[1], g1_h, sem.at[3]),
            pltpu.make_async_copy(wd, g2_h, sem.at[4]),
        ]
        for copy in copies:
            copy.start()
        for copy in copies:
            copy.wait()
    cp_y.wait()
    cp_tg.wait()


WS = (2, 2, 2, 4, 2, SUB, D)
WD = (4, 2, 2, 2, SUB, D)


def layer(linked, *arrays):
    hbm = pl.BlockSpec(memory_space=pl.ANY)
    near = pl.BlockSpec(memory_space=pltpu.VMEM)
    VM = pltpu.VMEM
    shape = jax.ShapeDtypeStruct
    outs = [(shape((T, D), bf), hbm), (shape((T, D), bf), hbm)]
    if linked:
        outs += [(shape((4, SUB, D), bf), hbm)] * 3
    else:
        outs += [(shape((2, 2, D, D), bf), hbm), (shape(WS[1:], bf), hbm), (shape(WD, bf), hbm)]
    outs += [(shape((16, 128 if linked else D), f32), near)]
    scratch = [
        VM(WS, bf),
        VM(WD, bf),
        VM((T, D), bf),
        VM((T, 3 * D), bf),
        VM((NC, H, CROP, CROP), bf),
        VM((T, D), bf),
        VM((T, D), f32),
        VM((T, 128), f32),
        VM((T, D), bf),
        VM((T, FF), bf),
        VM((2, 2, T, D), bf),
        VM((T, D), f32),
        VM((T, D), bf),
        VM((T, D), bf),
        VM((T, 128), bf),
        VM((16, D), f32),
        VM((16, D), f32),
        pltpu.SemaphoreType.DMA((11,)),
    ]
    params = dict(vmem_limit_bytes=63 * 2**20)
    if linked:
        transfers = 7 * (4 + 3 + 3 + 3 + 3 + 12) + 7 + 7 * (4 + 4 + 4 + 3 + 3) + 6
        scratch += [
            VM((8, 16, 128), bf),
            VM((4, 2, 2, SUB, D), bf),
            VM((4, 2, SUB, D), bf),
            VM((4, SUB, D), bf),
            VM((3, SUB, D), bf),
            VM((4, 2, SUB, D), bf),
            VM((4, SUB, D), bf),
            VM((3, SUB, D), bf),
            VM((3, 4, SUB, D), bf),
            VM((4, 16, D), f32),
            VM((6, 16, D), f32),
            pltpu.SemaphoreType.DMA((transfers,)),
            pltpu.SemaphoreType.DMA((transfers,)),
            pltpu.SemaphoreType.REGULAR((16,)),
        ]
        params.update(collective_id=0, has_side_effects=True)
    return pl.pallas_call(
        functools.partial(layer_kernel, linked),
        out_shape=[o[0] for o in outs],
        in_specs=[hbm, hbm, near, pl.BlockSpec(memory_space=pltpu.SMEM), near] + [hbm] * (len(arrays) - 5),
        out_specs=[o[1] for o in outs],
        scratch_shapes=scratch,
        compiler_params=pltpu.CompilerParams(**params),
    )(*arrays)


def adam_update(gradient, first_moment, second_moment):
    first_new = decay_first * first_moment + (1.0 - decay_first) * gradient
    second_new = decay_second * second_moment + (1.0 - decay_second) * gradient * gradient
    step_dir = first_new / correct_first / (jnp.sqrt(second_new / correct_second) + adam_epsilon)
    return (step_dir, first_new)


def finish(output, token_grad, gradients, moments):
    updated = [adam_update(g, m, s) for g, m, s in zip(gradients, moments[:5], moments[5:])]
    return (
        (output, token_grad)
        + tuple(gradients)
        + tuple(u[0] for u in updated)
        + tuple(u[1] for u in updated)
    )


def side_by_side(blocks):
    return jnp.concatenate([blocks[j] for j in range(blocks.shape[0])], axis=1)


def adam_kernel(*refs):
    sums, moments, passed, outs, placed = refs[:4], refs[4:14], refs[14:16], refs[16:31], refs[31:33]
    hold, sem = refs[33:]
    fetch = [pltpu.make_async_copy(a, hold.at[i], sem.at[i]) for i, a in enumerate(passed)]
    store = [pltpu.make_async_copy(hold.at[i], a, sem.at[2 + i]) for i, a in enumerate(placed)]

    @pl.when(pl.program_id(0) == 0)
    def _():
        for copy in fetch:
            copy.start()

    @pl.when(pl.program_id(0) == 1)
    def _():
        for i in range(2):
            fetch[i].wait()
            store[i].start()

    square, up, down, vec = (ref[...] for ref in sums)

    def update(k, cut, g):
        at = Ellipsis if cut is None else (slice(None), cut)
        g = g.astype(f32)
        step, first = adam_update(g, moments[k][at], moments[5 + k][at])
        outs[k][at] = g
        outs[5 + k][at] = step
        outs[10 + k][at] = first

    for j in range(4):
        cut = slice(j * D, (j + 1) * D)
        update(*((0, cut) if j < 3 else (1, None)), square[j])
        update(2, cut, up[j])
    update(3, None, down)

    @pl.when(pl.program_id(0) == 0)
    def _():
        rows, width = outs[4].shape
        update(4, None, vec[0:rows, 0:width])

    @pl.when(pl.program_id(0) == pl.num_programs(0) - 1)
    def _():
        for copy in store:
            copy.wait()


def adam(sums, moments, passed, steps=3):
    def rows(shape):
        return pl.BlockSpec((shape[0] // steps, shape[1]), lambda i: (i, 0))

    def whole(shape):
        return pl.BlockSpec(shape, lambda i: (0, 0))

    hbm = pl.BlockSpec(memory_space=pl.ANY)
    parts = pl.BlockSpec((4, SUB // steps, D), lambda i: (0, i, 0))
    specs = [whole(m.shape) if k == 4 else rows(m.shape) for k, m in enumerate(moments[:5])]
    return pl.pallas_call(
        adam_kernel,
        grid=(steps,),
        out_shape=[jax.ShapeDtypeStruct(m.shape, f32) for m in moments[:5]] * 3
        + [jax.ShapeDtypeStruct(a.shape, a.dtype) for a in passed],
        in_specs=[parts, parts, rows((4 * SUB, D)), whole((16, 128))] + specs * 2 + [hbm] * 2,
        out_specs=specs * 3 + [hbm] * 2,
        scratch_shapes=[pltpu.VMEM((2, *passed[0].shape), bf), pltpu.SemaphoreType.DMA((4,))],
        compiler_params=pltpu.CompilerParams(vmem_limit_bytes=63 * 2**20),
    )(*sums, *moments, *passed)


def per_device_linked(tokens, cotangent, deletion, lengths, qkv, out, up, down, vectors, *moments):
    output, token_grad, square, tall, wide, vec = layer(
        True, tokens, cotangent, deletion, lengths, vectors, qkv, out, up, down
    )
    *updated, output, token_grad = adam((square, tall, wide.reshape(4 * SUB, D), vec), moments, (output, token_grad))
    return (output, token_grad) + tuple(updated)


def per_device_plain(tokens, cotangent, deletion, lengths, qkv, out, up, down, vectors, *moments):
    blocks = [qkv[:, b * D : (b + 1) * D] for b in range(3)] + [out]
    blocks += [up[:, b * D : (b + 1) * D] for b in range(4)]
    square = lax.all_gather(jnp.stack(blocks).astype(bf), "shard", axis=1, tiled=True)
    tall = lax.all_gather(down.astype(bf), "shard", axis=0, tiled=True)
    vec = lax.all_gather(vectors.astype(bf), "shard", axis=1, tiled=True).astype(f32)
    output, token_grad, g0, g1, g2, vec = layer(
        False,
        tokens,
        cotangent,
        deletion,
        lengths,
        jnp.pad(vec, ((0, 4), (0, 0))),
        square.reshape(WS),
        tall.reshape(WD),
    )
    g0 = g0.reshape(4, D, D)
    square = lax.psum_scatter(
        jnp.concatenate([g0, g1.reshape(4, D, D)]).astype(f32), "shard", scatter_dimension=1, tiled=True
    )
    tall = lax.psum_scatter(g2.reshape(FF, D).astype(f32), "shard", scatter_dimension=0, tiled=True)
    vec = lax.psum_scatter(vec[:12], "shard", scatter_dimension=1, tiled=True)
    square, tall, vec = (lax.psum(g.astype(bf), "rep").astype(f32) for g in (square, tall, vec))
    gradients = (side_by_side(square[:3]), square[3], side_by_side(square[4:]), tall, vec)
    return finish(output, token_grad, gradients, moments)


def solution(mesh):
    rows = P(("rep", "shard"), None)
    weights = (P("shard", None),) * 4 + (P(None, "shard"),)
    linked = mesh.shape["rep"] == 4 and mesh.shape["shard"] == 8
    return jax.shard_map(
        per_device_linked if linked else per_device_plain,
        mesh=mesh,
        in_specs=(rows, rows, rows, P(("rep", "shard"))) + weights * 3,
        out_specs=(rows, rows) + weights * 3,
        check_vma=False,
    )
```

```python
import functools
import math

import jax
import jax.numpy as jnp
from jax import lax
from jax.experimental import pallas as pl
from jax.experimental.pallas import tpu as pltpu
from jax.sharding import PartitionSpec as P

D = 768
H = 12
FF = 3072
CROP = 256
T = 1024
NC = 4
SUB = 96
bf = jnp.bfloat16
f32 = jnp.float32
MESH = pl.DeviceIdType.MESH
Z_FIRST = (4, 6, 2)
GATHER_PLAN = {
    "start": {
        0: [("start", 1), ("plane", 0), ("start", 2), ("plane", 1), ("relay", 0), ("start", 3), ("plane", 2), ("relay", 1), ("last", 0), ("wait", 0)],
    },
    "project0": {
        1: [("start", 4), ("relay", 2)],
        2: [("plane", 3), ("last", 1)],
    },
    "attend0": {
        0: [("wait", 1), ("last", 2)],
        2: [("wait", 2), ("start", 5)],
        3: [("plane", 4), ("relay", 3)],
    },
    "attend1": {
        2: [("start", 6)],
        3: [("relay", 4), ("plane", 5)],
    },
    "project2": {
        1: [("last", 3)],
    },
    "attend2": {
        0: [("wait", 3), ("last", 4)],
        2: [("wait", 4), ("plane", 6)],
        3: [("relay", 5)],
    },
    "up": {
        0: [("relay", 6)],
        1: [("last", 5)],
        2: [("last", 6), ("wait", 5)],
        3: [("wait", 6)],
    },
}
SUM_PLAN = {
    "down_grad": {
        0: [("start", 5), ("start", 6)],
    },
    "first_back": {
        1: [("one", 5)],
        2: [("half", 6)],
    },
    "up_grad": {
        2: [("two", 5)],
        3: [("start", 3), ("start", 4)],
    },
    "attend_back0": {
        0: [("zed", 5), ("one", 3)],
        1: [("one", 6), ("half", 4)],
    },
    "grads0": {
        0: [("start", 0), ("plane", 5)],
    },
    "attend_back1": {
        0: [("two", 3)],
        1: [("one", 0), ("two", 6)],
    },
    "grads1": {
        0: [("wait", 5), ("start", 1)],
    },
    "attend_back2": {
        0: [("zed", 3)],
        1: [("one", 4), ("one", 1)],
        2: [("two", 0)],
        3: [("zed", 6)],
    },
    "grads2": {
        0: [("plane", 3), ("start", 2), ("two", 4)],
    },
    "token": {
        1: [("plane", 6), ("half", 2), ("two", 1)],
    },
    "end": {
        0: [("zed", 0), ("wait", 3), ("zed", 4), ("one", 2), ("wait", 6), ("zed", 1), ("plane", 0), ("two", 2), ("plane", 4), ("wait", 0), ("zed", 2), ("plane", 1), ("wait", 4), ("plane", 2), ("wait", 1), ("wait", 2)],
    },
}

norm_epsilon = 1e-06
decay_first = 0.9
decay_second = 0.999
correct_first = 1.0 - 2.6561398887587544e-05
correct_second = 0.0952078528862904
adam_epsilon = 1e-08


def dg(a, b, ca, cb):
    return lax.dot_general(a, b, (((ca,), (cb,)), ((), ())), preferred_element_type=f32)


def rows_of(c):
    return pl.ds(pl.multiple_of(c * CROP, CROP), CROP)


def third(t):
    return slice(t * 256, (t + 1) * 256)


def columns(g):
    return third(g) if g < 3 else slice((g + 1) % 2 * 384, (g + 1) % 2 * 384 + 384)


def lane_mean(v):
    return jnp.sum(v, axis=-1, keepdims=True) * (1.0 / D)


def lanes(v, n):
    return jnp.concatenate([v] * n, axis=1)


def gelu_parts(u):
    density = jnp.exp(u * u * -0.5) * (1.0 / math.sqrt(2.0 * math.pi))
    cdf = 0.5 * (1.0 + lax.erf(u * math.sqrt(0.5)))
    return u * cdf, cdf + u * density


def crop_loop(body, after):
    @pl.loop(0, NC)
    def _(c):
        body(c)
        for k, steps in after.items():

            @pl.when(c == k)
            def _():
                for step in steps:
                    step()


class Links:
    def __init__(self, refs):
        self.__dict__.update(refs)
        r = lax.axis_index("rep")
        s = lax.axis_index("shard")
        self.y, self.x = r // 2, r % 2
        self.z, self.c = s // 2, s % 2
        self.r, self.s = r, s
        self.rx = self.y * 2 + 1 - self.x
        self.ry = (1 - self.y) * 2 + self.x
        self.rd = 3 - r
        self.others = [(self.z + d) % 4 for d in (1, 2, 3)]
        self.dev_core = (r, self.z * 2 + 1 - self.c)
        self.dev_x = (self.rx, s)
        self.dev_y = (self.ry, s)
        self.dev_d = (self.rd, s)
        self.dev_z = [(r, z * 2 + self.c) for z in self.others]
        self.x1, self.y1, self.c1 = 1 - self.x, 1 - self.y, 1 - self.c
        self.s1 = self.z * 2 + self.c1
        self.s_others = [z * 2 + self.c for z in self.others]
        self.s1_others = [z * 2 + self.c1 for z in self.others]
        z1 = self.z // 2 * 2 + 1 - self.z % 2
        self.dev_z1 = (r, z1 * 2 + self.c)
        self.z_give = [1 - self.z % 2, 3 - self.z % 2]
        self.z_keep = [self.z % 2, 2 + self.z % 2]
        self.count = 0
        self.sent = []

    def greet(self):
        barrier = pltpu.get_barrier_semaphore()
        partners = [self.dev_core, self.dev_x, self.dev_y, self.dev_d] + self.dev_z
        for device in partners:
            pl.semaphore_signal(barrier, inc=1, device_id=device, device_id_type=MESH)

    def greeted(self):
        pl.semaphore_wait(pltpu.get_barrier_semaphore(), 7)

    def slot(self):
        self.count += 1
        return self.count - 1

    def copy(self, src, dst, k, device):
        return pltpu.make_async_remote_copy(
            src_ref=src,
            dst_ref=dst,
            send_sem=self.send_sem.at[k],
            recv_sem=self.recv_sem.at[k],
            device_id=device,
            device_id_type=MESH,
        )

    def part(self, g, jy, jx, z, c):
        if g > 4:
            return self.wd.at[z, c, jy, jx, :, columns(g)]
        return self.ws.at[g // 3, jy, jx, z, c, :, columns(g)]

    def column(self, g, jy, jx, c):
        return self.part(g, jy, jx, slice(None), c)

    def plan_gather(self):
        self.ag = [
            dict(
                zed=[self.slot() for _ in range(3)],
                px=[self.slot() for _ in range(3)],
                py=[self.slot() for _ in range(3)],
                relay=[self.slot() for _ in range(3)],
                sib=[self.slot() for _ in range(4)],
            )
            for _ in range(7)
        ]
        self.ag_vec = dict(
            core=self.slot(), zed=[self.slot() for _ in range(3)], sib=[self.slot() for _ in range(3)]
        )

    def send(self, src, dst, k, device, keep):
        def describe():
            return self.copy(src[0](*src[1:]), dst[0](*dst[1:]), k, device)

        describe().start()
        keep.append(describe)

    def at(self, name, *index):
        return getattr(self, name).at[index if len(index) > 1 else index[0]]

    def same(self, ref, k, device, keep):
        self.send(ref, ref, k, device, keep)

    def arrive(self, ref, k, device):
        self.copy(ref[0](*ref[1:]), ref[0](*ref[1:]), k, device).wait_recv()

    def gather_start(self, g):
        own = (self.part, g, self.y, self.x, self.z, self.c)
        for d in range(3):
            self.same(own, self.ag[g]["zed"][d], self.dev_z[d], self.sent)
        if g == 0:
            block = (self.at, "vb", self.s)
            self.same(block, self.ag_vec["core"], self.dev_core, self.sent)
            for d in range(3):
                self.same(block, self.ag_vec["zed"][d], self.dev_z[d], self.sent)

    def x_first(self, g, d):
        return (d != 1) == (g % 2 == 0)

    def gather_plane(self, g):
        for d in range(3):
            z, k = self.others[d], 2 - d
            ref = (self.part, g, self.y, self.x, z, self.c)
            self.arrive(ref, self.ag[g]["zed"][k], self.dev_z[d])
            self.same(ref, self.ag[g]["px"][d], self.dev_x, self.sent)
            self.same(ref, self.ag[g]["py"][d], self.dev_y, self.sent)
            if g == 0:
                block = (self.at, "vb", self.s_others[d])
                self.arrive(block, self.ag_vec["zed"][k], self.dev_z[d])
                self.same(block, self.ag_vec["sib"][d], self.dev_core, self.sent)

        self.same((self.column, g, self.y, self.x, self.c), self.ag[g]["sib"][0], self.dev_core, self.sent)

    def gather_relay(self, g):
        for d in range(3):
            z = self.others[d]
            ref_x = (self.part, g, self.y, self.x1, z, self.c)
            self.arrive(ref_x, self.ag[g]["px"][d], self.dev_x)
            if self.x_first(g, d):
                self.same(ref_x, self.ag[g]["relay"][d], self.dev_y, self.sent)
            ref_y = (self.part, g, self.y1, self.x, z, self.c)
            self.arrive(ref_y, self.ag[g]["py"][d], self.dev_y)
            if not self.x_first(g, d):
                self.same(ref_y, self.ag[g]["relay"][d], self.dev_x, self.sent)

        self.same((self.column, g, self.y, self.x1, self.c), self.ag[g]["sib"][1], self.dev_core, self.sent)
        self.same((self.column, g, self.y1, self.x, self.c), self.ag[g]["sib"][2], self.dev_core, self.sent)

    def gather_last(self, g):
        for d in range(3):
            ref = (self.part, g, self.y1, self.x1, self.others[d], self.c)
            self.arrive(ref, self.ag[g]["relay"][d], self.dev_y if self.x_first(g, d) else self.dev_x)

        self.same((self.column, g, self.y1, self.x1, self.c), self.ag[g]["sib"][3], self.dev_core, self.sent)

    def gather_wait(self, g):
        c = self.c1
        spots = [
            (self.y, self.x),
            (self.y, self.x1),
            (self.y1, self.x),
            (self.y1, self.x1),
        ]
        for j, (jy, jx) in enumerate(spots):
            self.arrive((self.column, g, jy, jx, c), self.ag[g]["sib"][j], self.dev_core)
        if g == 0:
            self.arrive((self.at, "vb", self.s1), self.ag_vec["core"], self.dev_core)
            for d in range(3):
                self.arrive((self.at, "vb", self.s1_others[d]), self.ag_vec["sib"][d], self.dev_core)

    def gather_drain(self):
        for copy in self.sent:
            copy().wait_send()
        self.sent = []

    def plan_sum(self):
        self.rs = [
            dict(
                core=[self.slot() for _ in range(4)],
                one=[self.slot() for _ in range(4)],
                two=[self.slot() for _ in range(4)],
                half=[self.slot() for _ in range(2)],
                zed=[self.slot() for _ in range(3)],
                plane=[self.slot() for _ in range(3)],
            )
            for _ in range(7)
        ]
        self.rs_vec = dict(
            core=self.slot(), one=self.slot(), two=self.slot(), zed=[self.slot() for _ in range(3)]
        )
        self.out = [[] for _ in range(7)]

    def grads(self, g, z, c, jy=slice(None), jx=slice(None)):
        if g > 2:
            return self.part(g, jy, jx, z, c)
        return self.gp.at[jy, jx, pl.ds(pl.multiple_of((z * 2 + c) * SUB, SUB), SUB), third(g)]

    def land(self, name, g, *index):
        ref = getattr(self, name if name == "rc" or g > 2 else name + "t")
        return ref.at[index + (slice(None),) * (len(ref.shape) - len(index) - 1) + (columns(g),)]

    def halved(self, g, k):
        cols = slice(0, 384) if g == 4 else slice(384, 768 if g > 2 else 640)
        return self.act3.at[k, :, :, 0:SUB, cols]

    def total(self, g, r):
        return self.gt.at[0 if g < 3 else (g - 1) // 2, r, :, columns(g)]

    def credit(self, g, i, device):
        if g > 4 or (g > 2 and i == 0):
            pl.semaphore_signal(self.credit_sem.at[(g + 1) % 2 * 8 + i], inc=1, device_id=device, device_id_type=MESH)

    def spend(self, g, i):
        for h in range(2):
            if g == 3 + h or (g == h and i == 0):
                pl.semaphore_wait(self.credit_sem.at[h * 8 + i], 1)

    def add(self, ref, other):
        ref, other = ref[0](*ref[1:]), other[0](*other[1:])
        ref[...] = ref[...] + other[...]

    def sum_start(self, g):
        self.spend(g, 0)
        for z in range(4):
            self.send(
                (self.grads, g, z, self.c1), (self.land, "rc", g, z), self.rs[g]["core"][z], self.dev_core, self.out[g]
            )
        if g == 2:
            self.send((self.at, "vs", 0), (self.at, "vr", 0), self.rs_vec["core"], self.dev_core, self.out[g])

    def items(self, g):
        if g in Z_FIRST:
            return [(0, self.z_keep[0]), (2, self.z_keep[1])]
        return [(z, z) for z in range(4)]

    def sum_half(self, g):
        c = self.c
        for z in range(4):
            self.arrive((self.land, "rc", g, z), self.rs[g]["core"][z], self.dev_core)
            self.add((self.grads, g, z, c), (self.land, "rc", g, z))
        self.credit(g, 0, self.dev_core)
        pl.semaphore_signal(self.half_sem.at[g], inc=1, device_id=self.dev_z1, device_id_type=MESH)
        pl.semaphore_wait(self.half_sem.at[g], 1)
        for k in range(2):
            self.send(
                (self.grads, g, self.z_give[k], c), (self.halved, g, k), self.rs[g]["half"][k], self.dev_z1, self.out[g]
            )

    def sum_one(self, g):
        y, x, c = self.y, self.x, self.c
        for i, (slot, z) in enumerate(self.items(g)):
            mine, came = (self.grads, g, z, c), (self.land, "rc", g, i)
            if g in Z_FIRST:
                came = (self.halved, g, i)
                self.arrive(came, self.rs[g]["half"][i], self.dev_z1)
            else:
                self.arrive(came, self.rs[g]["core"][i], self.dev_core)
            self.add(mine, came)
            if i == 0:
                self.spend(g, 1)
                self.spend(g, 2)
            land = (self.land, "r1", g, slot)
            if slot < 2:
                self.send((self.grads, g, z, c, slice(None), self.x1), land, self.rs[g]["one"][i], self.dev_x, self.out[g])
            else:
                self.send((self.grads, g, z, c, self.y1), land, self.rs[g]["one"][i], self.dev_y, self.out[g])
        if g not in Z_FIRST:
            self.credit(g, 0, self.dev_core)
        if g == 2:
            self.arrive((self.at, "vr", 0), self.rs_vec["core"], self.dev_core)
            self.vs[1] = self.vs[0] + self.vr[0]
            self.send((self.at, "vs", 1), (self.at, "vr", 1), self.rs_vec["one"], self.dev_x, self.out[g])

    def sum_two(self, g):
        y, x, c = self.y, self.x, self.c
        for i, (slot, z) in enumerate(self.items(g)):
            came = (self.land, "r1", g, slot)
            self.arrive(came, self.rs[g]["one"][i], self.dev_x if slot < 2 else self.dev_y)
            self.add((self.grads, g, z, c, slice(None), x) if slot < 2 else (self.grads, g, z, c, y), came)
            if i == 0:
                self.spend(g, 3)
                self.spend(g, 4)
            land = (self.land, "r2", g, slot)
            if slot < 2:
                self.send((self.grads, g, z, c, self.y1, x), land, self.rs[g]["two"][i], self.dev_y, self.out[g])
            else:
                self.send((self.grads, g, z, c, y, self.x1), land, self.rs[g]["two"][i], self.dev_x, self.out[g])
        self.credit(g, 1, self.dev_x)
        self.credit(g, 2, self.dev_y)
        if g == 2:
            self.arrive((self.at, "vr", 1), self.rs_vec["one"], self.dev_x)
            self.vs[2] = self.vs[1] + self.vr[1]
            self.send((self.at, "vs", 2), (self.at, "vr", 2), self.rs_vec["two"], self.dev_y, self.out[g])

    def sum_zed(self, g):
        y, x, c = self.y, self.x, self.c
        for i, (slot, z) in enumerate(self.items(g)):
            came = (self.land, "r2", g, slot)
            self.arrive(came, self.rs[g]["two"][i], self.dev_y if slot < 2 else self.dev_x)
            self.add((self.grads, g, z, c, y, x), came)
        for d in range(3):
            self.spend(g, 5 + d)
        if g in Z_FIRST:
            self.send(
                (self.grads, g, self.others[1], c, y, x),
                (self.land, "rz", g, 1),
                self.rs[g]["zed"][1],
                self.dev_z[1],
                self.out[g],
            )
        else:
            for d in range(3):
                self.send(
                    (self.grads, g, self.others[d], c, y, x),
                    (self.land, "rz", g, 2 - d),
                    self.rs[g]["zed"][d],
                    self.dev_z[d],
                    self.out[g],
                )
        self.credit(g, 3, self.dev_y)
        self.credit(g, 4, self.dev_x)
        if g == 2:
            self.arrive((self.at, "vr", 2), self.rs_vec["two"], self.dev_y)
            self.vs[3] = self.vs[2] + self.vr[2]
            for d in range(3):
                self.send((self.at, "vs", 3), (self.at, "vr", 3 + 2 - d), self.rs_vec["zed"][d], self.dev_z[d], self.out[g])

    def sum_plane(self, g):
        total = self.grads(g, self.z, self.c, self.y, self.x)[...].astype(f32)
        for d in (1,) if g in Z_FIRST else range(3):
            self.arrive((self.land, "rz", g, d), self.rs[g]["zed"][2 - d], self.dev_z[d])
            total = total + self.land("rz", g, d)[...].astype(f32)
        own = (self.total, g, self.r)
        self.total(g, self.r)[...] = total.astype(bf)
        for k, device in enumerate((self.dev_x, self.dev_y, self.dev_d)):
            self.send(own, own, self.rs[g]["plane"][k], device, self.out[g])
        for d in range(3):
            self.credit(g, 5 + 2 - d, self.dev_z[d])
        if g == 2:
            vec = self.vs[3]
            for d in range(3):
                self.arrive((self.at, "vr", 3 + d), self.rs_vec["zed"][2 - d], self.dev_z[d])
                vec = vec + self.vr[3 + d]
            self.vec_total[...] = pltpu.roll(vec, lax.rem(D - self.s * SUB, D), 1)[:, 0:128]

    def sum_wait(self, g):
        for k, (r, device) in enumerate(((self.rx, self.dev_x), (self.ry, self.dev_y), (self.rd, self.dev_d))):
            self.arrive((self.total, g, r), self.rs[g]["plane"][k], device)

    def sum_drain(self, g):
        for copy in self.out[g]:
            copy().wait_send()
        self.out[g] = []


def layer_kernel(linked, *refs):
    if linked:
        (tok_h, cot_h, del_ref, len_ref, vec_in, qkv_h, out_h, up_h, down_h) = refs[:9]
        (y_h, tg_h, t0_h, t1_h, t2_h, vg_out) = refs[9:15]
        rest = refs[15:]
    else:
        (tok_h, cot_h, del_ref, len_ref, vec_in, ws_h, wd_h) = refs[:7]
        (y_h, tg_h, g0_h, g1_h, g2_h, vg_out) = refs[7:13]
        rest = refs[13:]
    (ws, wd, x, qkv, pt, mixed, nrm1, root1, fl, act, act3, gp, gs, gsec, cot, keep, vec_ref, vg_ref, sem) = rest[:19]
    if linked:
        names = ("vb", "rc", "r1", "r2", "rz", "r1t", "r2t", "rzt", "gt", "vs", "vr", "send_sem", "recv_sem", "credit_sem", "half_sem")
        net = Links(dict(zip(names, rest[19:]), ws=ws, wd=wd, gp=gp, act3=act3, vec_total=vg_out))
        net.plan_gather()
        net.plan_sum()

    cp_x = pltpu.make_async_copy(tok_h, x, sem.at[0])
    cp_cot = pltpu.make_async_copy(cot_h, cot, sem.at[1])
    lane = lax.broadcasted_iota(jnp.int32, (CROP, 128), 1)
    low_half = lane < 64

    def half(v, h):
        return jnp.where(low_half if h == 0 else ~low_half, v, jnp.zeros_like(v))

    def vrow(r):
        return vec_ref[r : r + 1, :]

    def mat(g, j):
        if g == 2:
            return wd[j].reshape(D, D)
        return ws[g, j // 2, j % 2].reshape(D, D)

    def mat_third(j, t):
        return ws[0, j // 2, j % 2, :, :, :, third(t)].reshape(D, 256)

    def step(name, *a):
        return functools.partial(getattr(net, name), *a) if linked else (lambda: None)

    def after(name):
        plan = {}
        for kind, table in (("gather_", GATHER_PLAN), ("sum_", SUM_PLAN)):
            for c, steps in table.get(name, {}).items():
                plan[c] = [step(kind + what, g) for what, g in steps]
        return plan

    def now(name):
        for act_now in after(name).get(0, ()):
            act_now()

    if linked:
        net.greet()
        loads = []
        for j in range(4):
            src = qkv_h.at[:, j * D : (j + 1) * D] if j < 3 else out_h
            loads.append(pltpu.make_async_copy(src, gs.at[j * SUB : (j + 1) * SUB], sem.at[2 + j]))
        for j in range(4):
            loads.append(
                pltpu.make_async_copy(
                    up_h.at[:, j * D : (j + 1) * D], nrm1.at[j * SUB : (j + 1) * SUB], sem.at[6 + j]
                )
            )
        loads.append(pltpu.make_async_copy(down_h, gs.at[4 * SUB : 8 * SUB], sem.at[10]))
        for load in loads:
            load.start()
        cp_x.start()
        cp_cot.start()
        net.vs[0, :, 0:128] = jnp.zeros((16, 128), f32)
        net.vs[0, 0 : vec_in.shape[0], 0 : vec_in.shape[1]] = vec_in[...]
        net.vb[net.s] = net.vs[0, :, 0:128].astype(bf)
        for j in range(4):
            loads[j].wait()
            ws[0, j // 2, j % 2, net.z, net.c] = gs[j * SUB : (j + 1) * SUB].astype(bf)
        net.greeted()
        net.gather_start(0)
        for j in range(4):
            loads[4 + j].wait()
            ws[1, j // 2, j % 2, net.z, net.c] = nrm1[j * SUB : (j + 1) * SUB].astype(bf)
        loads[8].wait()
        for j in range(4):
            wd[net.z, net.c, j // 2, j % 2] = gs[(4 + j) * SUB : (5 + j) * SUB].astype(bf)
    else:
        vec_ref[...] = vec_in[...]
        cp_ws = pltpu.make_async_copy(ws_h, ws, sem.at[2])
        cp_wd = pltpu.make_async_copy(wd_h, wd, sem.at[3])
        for copy in (cp_ws, cp_wd, cp_x, cp_cot):
            copy.start()
        cp_ws.wait()
        cp_wd.wait()
    place = lax.broadcasted_iota(jnp.int32, (1, CROP), 1)
    allowed = [
        jnp.where(((del_ref[c : c + 1, :] == 1) | (place == 0)) & (place < len_ref[c]), 1.0, 0.0) for c in range(NC)
    ]
    mcol = jnp.concatenate(allowed * (8 // NC), axis=0).T
    for c in range(NC):
        keep[c * CROP : (c + 1) * CROP, :] = jnp.broadcast_to(mcol[:, c : c + 1], (CROP, 128)).astype(bf)
    vg_ref[...] = jnp.zeros_like(vg_ref)
    cp_x.wait()
    cp_cot.wait()
    if linked:
        now("start")
        row = lax.broadcasted_iota(jnp.int32, (128, D), 0)
        col = lax.broadcasted_iota(jnp.int32, (128, D), 1)
        vec = jnp.zeros((16, D), f32)
        for s in range(8):
            pick = ((col == row + s * SUB) & (row < SUB)).astype(f32).astype(bf)
            vec = vec + dg(net.vb[s], pick, 1, 0)
        vec_ref[...] = vec

    def project(t, c):
        r = rows_of(c)
        xv = x[r, :]
        for b in range(3):
            y = dg(xv, mat_third(b, t), 1, 0)
            if b == 0:
                y = y + vec_ref[0:1, third(t)]
            if b == 2:
                y = y + vec_ref[1:2, third(t)]
            qkv[r, t * D + b * 256 : t * D + (b + 1) * 256] = y.astype(bf)

    def attend(t, c):
        r = rows_of(c)
        kp = lanes(keep[r, :].astype(f32), 2) > 0.5
        for p in range(2):
            q, k, v = (qkv[r, t * D + b * 256 + p * 128 : t * D + b * 256 + (p + 1) * 128] for b in range(3))
            q = q * jnp.asarray(0.125, bf)
            o = None
            for h in range(2):
                st = dg(k, half(q, h), 1, 1)
                st = jnp.where(kp, st, -1e30)
                e = jnp.exp(st - jnp.max(st, axis=0, keepdims=True))
                pr = (e * (1.0 / jnp.sum(e, axis=0, keepdims=True))).astype(bf)
                pt[c, 4 * t + 2 * p + h] = pr
                w = dg(pr, half(v, h), 0, 0)
                o = w if o is None else o + w
            mixed[r, t * 256 + p * 128 : t * 256 + (p + 1) * 128] = o.astype(bf)

    for t in range(3):
        crop_loop(functools.partial(project, t), after(f"project{t}"))
        crop_loop(functools.partial(attend, t), after(f"attend{t}"))

    def body(c):
        r = rows_of(c)
        h = x[r, :].astype(f32) + (dg(mixed[r, :], mat(0, 3), 1, 0) + vrow(2))
        h = h - lane_mean(h)
        root = lax.rsqrt(lane_mean(h * h) + norm_epsilon)
        n = h * root
        nrm1[r, :] = n
        root1[r, :] = jnp.broadcast_to(root, (CROP, 128))
        fl[r, :] = (n * vrow(3) + vrow(4)).astype(bf)

    crop_loop(body, after("out"))

    def body(c):
        r = rows_of(c)
        a = fl[r, :]
        for j in range(4):
            u = dg(a, mat(1, j), 1, 0) + vrow(5 + j)
            g, d = gelu_parts(u)
            if j < 3:
                act[r, j * D : (j + 1) * D] = g.astype(bf)
            else:
                act3[c // 2, c % 2] = g.astype(bf).reshape(2, 128, D)
            gp[j // 2, j % 2, r, :] = d.astype(bf)

    crop_loop(body, after("up"))

    def body(c):
        r = rows_of(c)
        s = dg(act[r, :], wd[0:3].reshape(3 * D, D), 1, 0)
        s = s + dg(act3[c // 2, c % 2].reshape(CROP, D), wd[3].reshape(D, D), 1, 0) + vrow(9)
        h = nrm1[r, :] * vrow(3) + vrow(4) + s
        h = h - lane_mean(h)
        root = lax.rsqrt(lane_mean(h * h) + norm_epsilon)
        n = h * root
        G = cot[r, :].astype(f32) * lanes(keep[r, :].astype(f32), 6)
        cot[r, :] = (n * vrow(10) + vrow(11)).astype(bf)
        vg_ref[10:11, :] += jnp.sum(G * n, axis=0, keepdims=True)
        vg_ref[11:12, :] += jnp.sum(G, axis=0, keepdims=True)
        dn = G * vrow(10)
        g2 = root * (dn - lane_mean(dn) - n * lane_mean(dn * n))
        gs[r, :] = g2
        gb = g2.astype(bf)
        gsec[r, :] = gb
        vg_ref[9:10, :] += jnp.sum(gb.astype(f32), axis=0, keepdims=True)

    crop_loop(body, after("down"))
    cp_y = pltpu.make_async_copy(cot, y_h, sem.at[0])
    cp_y.start()

    def body(c):
        r = rows_of(c)
        a = gsec[r, :]
        for j in range(4):
            ga = dg(a, mat(2, j), 1, 1)
            gi = (ga * gp[j // 2, j % 2, r, :].astype(f32)).astype(bf)
            gp[j // 2, j % 2, r, :] = gi
            vg_ref[5 + j : 6 + j, :] += jnp.sum(gi.astype(f32), axis=0, keepdims=True)

    crop_loop(body, after("act_back"))
    step("gather_drain")()

    @pl.loop(0, 3)
    def _(i):
        m = pl.ds(pl.multiple_of(i * D, D), D)
        wd[i] = dg(act[:, m], gsec[...], 0, 0).astype(bf).reshape(2, 2, 2, SUB, D)

    wd[3] = dg(act3[...].reshape(T, D), gsec[...], 0, 0).astype(bf).reshape(2, 2, 2, SUB, D)

    now("down_grad")

    def body(c):
        r = rows_of(c)
        G = gs[r, :]
        for j in range(4):
            G = G + dg(gp[j // 2, j % 2, r, :], mat(1, j), 1, 1)
        n = nrm1[r, :]
        vg_ref[3:4, :] += jnp.sum(G * n, axis=0, keepdims=True)
        vg_ref[4:5, :] += jnp.sum(G, axis=0, keepdims=True)
        dn = G * vrow(3)
        g1 = lanes(root1[r, :], 6) * (dn - lane_mean(dn) - n * lane_mean(dn * n))
        gs[r, :] = g1
        gb = g1.astype(bf)
        gsec[r, :] = gb
        vg_ref[2:3, :] += jnp.sum(gb.astype(f32), axis=0, keepdims=True)

    crop_loop(body, after("first_back"))

    def body(j):
        ws[1, j // 2, j % 2] = dg(fl[...], gp[j // 2, j % 2], 0, 0).astype(bf).reshape(4, 2, SUB, D)

    crop_loop(body, after("up_grad"))

    def body(c):
        r = rows_of(c)
        fl[r, :] = dg(gsec[r, :], mat(0, 3), 1, 1).astype(bf)

    crop_loop(body, after("mixed_back"))

    def attend_back(t, c):
        r = rows_of(c)
        for p in range(2):
            at = [slice(t * D + b * 256 + p * 128, t * D + b * 256 + (p + 1) * 128) for b in range(3)]
            cols = slice(t * 256 + p * 128, t * 256 + (p + 1) * 128)
            q, k, v = (qkv[r, cut] for cut in at)
            q = q * jnp.asarray(0.125, bf)
            do = fl[r, cols]
            dq = dk = dv = None
            for h in range(2):
                dom = half(do, h)
                dp = dg(v, dom, 1, 1)
                prb = pt[c, 4 * t + 2 * p + h]
                pr = prb.astype(f32)
                delta = jnp.sum(pr * dp, axis=0, keepdims=True)
                ds = (pr * (dp - delta)).astype(bf)
                tv = dg(prb, dom, 1, 0)
                tk = dg(ds, half(q, h), 1, 0)
                tq = dg(ds, half(k, h), 0, 0)
                dq, dk, dv = (tq, tk, tv) if dq is None else (dq + tq, dk + tk, dv + tv)
            dq = (dq * 0.125).astype(bf)
            dv = dv.astype(bf)
            act[r, at[0]] = dq
            act[r, at[1]] = dk.astype(bf)
            act[r, at[2]] = dv
            vg_ref[0:1, cols] += jnp.sum(dq.astype(f32), axis=0, keepdims=True)
            vg_ref[1:2, cols] += jnp.sum(dv.astype(f32), axis=0, keepdims=True)

    def third_grads(t):
        g = dg(x[...], act[:, t * D : (t + 1) * D], 0, 0).astype(bf)
        for j in range(3):
            gp[j // 2, j % 2, 0:D, third(t)] = g[:, third(j)]
        gp[1, 1, 0:D, third(t)] = dg(mixed[...], gsec[:, third(t)], 0, 0).astype(bf)

    for t in range(3):
        crop_loop(functools.partial(attend_back, t), after(f"attend_back{t}"))
        if linked and t == 2:
            net.vs[0] = vg_ref[...]
        third_grads(t)
        now(f"grads{t}")

    def body(c):
        r = rows_of(c)
        G = gs[r, :]
        for b in range(3):
            for t in range(3):
                G = G + dg(act[r, t * D + b * 256 : t * D + (b + 1) * 256], mat_third(b, t), 1, 1)
        gsec[r, :] = G.astype(bf)

    crop_loop(body, after("token"))
    cp_tg = pltpu.make_async_copy(gsec, tg_h, sem.at[1])
    cp_tg.start()
    if linked:
        now("end")
        shares = [pltpu.make_async_copy(net.gt.at[i], t_h, sem.at[2 + i]) for i, t_h in enumerate((t0_h, t1_h, t2_h))]
        for copy in shares:
            copy.start()
        for g in range(7):
            net.sum_drain(g)
        for copy in shares:
            copy.wait()
    else:
        vg_out[...] = vg_ref[...]
        copies = [
            pltpu.make_async_copy(gp.at[:, :, 0:D], g0_h, sem.at[2]),
            pltpu.make_async_copy(ws.at[1], g1_h, sem.at[3]),
            pltpu.make_async_copy(wd, g2_h, sem.at[4]),
        ]
        for copy in copies:
            copy.start()
        for copy in copies:
            copy.wait()
    cp_y.wait()
    cp_tg.wait()


WS = (2, 2, 2, 4, 2, SUB, D)
WD = (4, 2, 2, 2, SUB, D)


def layer(linked, *arrays):
    hbm = pl.BlockSpec(memory_space=pl.ANY)
    near = pl.BlockSpec(memory_space=pltpu.VMEM)
    VM = pltpu.VMEM
    shape = jax.ShapeDtypeStruct
    outs = [(shape((T, D), bf), hbm), (shape((T, D), bf), hbm)]
    if linked:
        outs += [(shape((4, SUB, D), bf), hbm)] * 3
    else:
        outs += [(shape((2, 2, D, D), bf), hbm), (shape(WS[1:], bf), hbm), (shape(WD, bf), hbm)]
    outs += [(shape((16, 128 if linked else D), f32), near)]
    scratch = [
        VM(WS, bf),
        VM(WD, bf),
        VM((T, D), bf),
        VM((T, 3 * D), bf),
        VM((NC, H, CROP, CROP), bf),
        VM((T, D), bf),
        VM((T, D), f32),
        VM((T, 128), f32),
        VM((T, D), bf),
        VM((T, 3 * D), bf),
        VM((2, 2, 2, 128, D), bf),
        VM((2, 2, T, D), bf),
        VM((T, D), f32),
        VM((T, D), bf),
        VM((T, D), bf),
        VM((T, 128), bf),
        VM((16, D), f32),
        VM((16, D), f32),
        pltpu.SemaphoreType.DMA((11,)),
    ]
    params = dict(vmem_limit_bytes=63 * 2**20)
    if linked:
        transfers = 7 * (3 + 3 + 3 + 3 + 4) + 7 + 7 * (4 + 4 + 4 + 2 + 3 + 3) + 6
        scratch += [
            VM((8, 16, 128), bf),
            VM((4, 2, 2, SUB, D), bf),
            VM((4, 2, SUB, D), bf),
            VM((4, SUB, D), bf),
            VM((3, SUB, D), bf),
            VM((4, 2, SUB, D), bf),
            VM((4, SUB, D), bf),
            VM((3, SUB, D), bf),
            VM((3, 4, SUB, D), bf),
            VM((4, 16, D), f32),
            VM((6, 16, D), f32),
            pltpu.SemaphoreType.DMA((transfers,)),
            pltpu.SemaphoreType.DMA((transfers,)),
            pltpu.SemaphoreType.REGULAR((16,)),
            pltpu.SemaphoreType.REGULAR((7,)),
        ]
        params.update(collective_id=0, has_side_effects=True)
    return pl.pallas_call(
        functools.partial(layer_kernel, linked),
        out_shape=[o[0] for o in outs],
        in_specs=[hbm, hbm, near, pl.BlockSpec(memory_space=pltpu.SMEM), near] + [hbm] * (len(arrays) - 5),
        out_specs=[o[1] for o in outs],
        scratch_shapes=scratch,
        compiler_params=pltpu.CompilerParams(**params),
    )(*arrays)


def adam_update(gradient, first_moment, second_moment):
    first_new = decay_first * first_moment + (1.0 - decay_first) * gradient
    second_new = decay_second * second_moment + (1.0 - decay_second) * gradient * gradient
    step_dir = first_new / correct_first / (jnp.sqrt(second_new / correct_second) + adam_epsilon)
    return (step_dir, first_new)


def finish(output, token_grad, gradients, moments):
    updated = [adam_update(g, m, s) for g, m, s in zip(gradients, moments[:5], moments[5:])]
    return (
        (output, token_grad)
        + tuple(gradients)
        + tuple(u[0] for u in updated)
        + tuple(u[1] for u in updated)
    )


def side_by_side(blocks):
    return jnp.concatenate([blocks[j] for j in range(blocks.shape[0])], axis=1)


def adam_kernel(*refs):
    sums, moments, passed, outs, placed = refs[:4], refs[4:14], refs[14:16], refs[16:31], refs[31:33]
    hold, sem = refs[33:]
    fetch = [pltpu.make_async_copy(a, hold.at[i], sem.at[i]) for i, a in enumerate(passed)]
    store = [pltpu.make_async_copy(hold.at[i], a, sem.at[2 + i]) for i, a in enumerate(placed)]

    @pl.when(pl.program_id(0) == 0)
    def _():
        for copy in fetch:
            copy.start()

    @pl.when(pl.program_id(0) == 1)
    def _():
        for i in range(2):
            fetch[i].wait()
            store[i].start()

    square, up, down, vec = (ref[...] for ref in sums)

    def update(k, cut, g):
        at = Ellipsis if cut is None else (slice(None), cut)
        g = g.astype(f32)
        step, first = adam_update(g, moments[k][at], moments[5 + k][at])
        outs[k][at] = g
        outs[5 + k][at] = step
        outs[10 + k][at] = first

    for j in range(4):
        cut = slice(j * D, (j + 1) * D)
        update(*((0, cut) if j < 3 else (1, None)), square[j])
        update(2, cut, up[j])
    update(3, None, down)

    @pl.when(pl.program_id(0) == 0)
    def _():
        rows, width = outs[4].shape
        update(4, None, vec[0:rows, 0:width])

    @pl.when(pl.program_id(0) == pl.num_programs(0) - 1)
    def _():
        for copy in store:
            copy.wait()


def adam(sums, moments, passed, steps=3):
    def rows(shape):
        return pl.BlockSpec((shape[0] // steps, shape[1]), lambda i: (i, 0))

    def whole(shape):
        return pl.BlockSpec(shape, lambda i: (0, 0))

    hbm = pl.BlockSpec(memory_space=pl.ANY)
    parts = pl.BlockSpec((4, SUB // steps, D), lambda i: (0, i, 0))
    specs = [whole(m.shape) if k == 4 else rows(m.shape) for k, m in enumerate(moments[:5])]
    return pl.pallas_call(
        adam_kernel,
        grid=(steps,),
        out_shape=[jax.ShapeDtypeStruct(m.shape, f32) for m in moments[:5]] * 3
        + [jax.ShapeDtypeStruct(a.shape, a.dtype) for a in passed],
        in_specs=[parts, parts, rows((4 * SUB, D)), whole((16, 128))] + specs * 2 + [hbm] * 2,
        out_specs=specs * 3 + [hbm] * 2,
        scratch_shapes=[pltpu.VMEM((2, *passed[0].shape), bf), pltpu.SemaphoreType.DMA((4,))],
        compiler_params=pltpu.CompilerParams(vmem_limit_bytes=63 * 2**20),
    )(*sums, *moments, *passed)


def per_device_linked(tokens, cotangent, deletion, lengths, qkv, out, up, down, vectors, *moments):
    output, token_grad, square, tall, wide, vec = layer(
        True, tokens, cotangent, deletion, lengths, vectors, qkv, out, up, down
    )
    *updated, output, token_grad = adam((square, tall, wide.reshape(4 * SUB, D), vec), moments, (output, token_grad))
    return (output, token_grad) + tuple(updated)


def per_device_plain(tokens, cotangent, deletion, lengths, qkv, out, up, down, vectors, *moments):
    blocks = [qkv[:, b * D : (b + 1) * D] for b in range(3)] + [out]
    blocks += [up[:, b * D : (b + 1) * D] for b in range(4)]
    square = lax.all_gather(jnp.stack(blocks).astype(bf), "shard", axis=1, tiled=True)
    tall = lax.all_gather(down.astype(bf), "shard", axis=0, tiled=True)
    vec = lax.all_gather(vectors.astype(bf), "shard", axis=1, tiled=True).astype(f32)
    output, token_grad, g0, g1, g2, vec = layer(
        False,
        tokens,
        cotangent,
        deletion,
        lengths,
        jnp.pad(vec, ((0, 4), (0, 0))),
        square.reshape(WS),
        tall.reshape(WD),
    )
    g0 = g0.reshape(4, D, D)
    square = lax.psum_scatter(
        jnp.concatenate([g0, g1.reshape(4, D, D)]).astype(f32), "shard", scatter_dimension=1, tiled=True
    )
    tall = lax.psum_scatter(g2.reshape(FF, D).astype(f32), "shard", scatter_dimension=0, tiled=True)
    vec = lax.psum_scatter(vec[:12], "shard", scatter_dimension=1, tiled=True)
    square, tall, vec = (lax.psum(g.astype(bf), "rep").astype(f32) for g in (square, tall, vec))
    gradients = (side_by_side(square[:3]), square[3], side_by_side(square[4:]), tall, vec)
    return finish(output, token_grad, gradients, moments)


def solution(mesh):
    rows = P(("rep", "shard"), None)
    weights = (P("shard", None),) * 4 + (P(None, "shard"),)
    linked = mesh.shape["rep"] == 4 and mesh.shape["shard"] == 8
    return jax.shard_map(
        per_device_linked if linked else per_device_plain,
        mesh=mesh,
        in_specs=(rows, rows, rows, P(("rep", "shard"))) + weights * 3,
        out_specs=(rows, rows) + weights * 3,
        check_vma=False,
    )
```

```python
import functools
import math

import jax
import jax.numpy as jnp
from jax import lax
from jax.experimental import pallas as pl
from jax.experimental.pallas import tpu as pltpu
from jax.sharding import PartitionSpec as P

D = 768
H = 12
FF = 3072
CROP = 256
T = 1024
NC = 4
SUB = 96
bf = jnp.bfloat16
f32 = jnp.float32
MESH = pl.DeviceIdType.MESH
Z_FIRST = (4, 6, 2)
GATHER_PLAN = {
    "start": {
        0: [("plane", 0), ("start", 1), ("relay", 0), ("plane", 1), ("start", 2), ("last", 0), ("wait", 0), ("start", 3)],
    },
    "project0": {
        1: [("relay", 1)],
        2: [("plane", 2)],
    },
    "attend0": {
        1: [("last", 1)],
        2: [("start", 4)],
        3: [("wait", 1), ("relay", 2), ("plane", 3)],
    },
    "attend1": {
        0: [("last", 2), ("start", 5)],
        2: [("wait", 2), ("plane", 4)],
        3: [("relay", 3)],
    },
    "project2": {
        2: [("start", 6)],
    },
    "attend2": {
        1: [("plane", 5), ("relay", 4)],
        3: [("last", 3)],
    },
    "out": {
        1: [("wait", 3)],
        3: [("plane", 6), ("relay", 5), ("last", 4), ("wait", 4)],
    },
    "up": {
        1: [("relay", 6)],
        2: [("last", 5)],
        3: [("last", 6), ("wait", 5), ("wait", 6)],
    },
}
SUM_PLAN = {
    "down_grad": {
        0: [("start", 5), ("start", 6)],
    },
    "first_back": {
        1: [("one", 5)],
        2: [("half", 6)],
    },
    "up_grad": {
        2: [("two", 5)],
        3: [("start", 3), ("start", 4)],
    },
    "attend_back0": {
        0: [("zed", 5), ("one", 3)],
        1: [("one", 6), ("half", 4)],
    },
    "grads0": {
        0: [("start", 0), ("plane", 5)],
    },
    "attend_back1": {
        0: [("two", 3)],
        1: [("one", 0), ("two", 6)],
    },
    "grads1": {
        0: [("wait", 5), ("start", 1)],
    },
    "attend_back2": {
        0: [("zed", 3)],
        1: [("one", 4), ("one", 1)],
        2: [("two", 0)],
        3: [("zed", 6)],
    },
    "grads2": {
        0: [("plane", 3), ("start", 2), ("two", 4)],
    },
    "token": {
        1: [("plane", 6), ("half", 2), ("two", 1)],
    },
    "end": {
        0: [("zed", 0), ("wait", 3), ("zed", 4), ("one", 2), ("wait", 6), ("zed", 1), ("plane", 0), ("two", 2), ("plane", 4), ("wait", 0), ("zed", 2), ("plane", 1), ("wait", 4), ("plane", 2), ("wait", 1), ("wait", 2)],
    },
}

norm_epsilon = 1e-06
decay_first = 0.9
decay_second = 0.999
correct_first = 1.0 - 2.6561398887587544e-05
correct_second = 0.0952078528862904
adam_epsilon = 1e-08


def dg(a, b, ca, cb):
    return lax.dot_general(a, b, (((ca,), (cb,)), ((), ())), preferred_element_type=f32)


def rows_of(c):
    return pl.ds(pl.multiple_of(c * CROP, CROP), CROP)


def third(t):
    return slice(t * 256, (t + 1) * 256)


def columns(g):
    return third(g) if g < 3 else slice((g + 1) % 2 * 384, (g + 1) % 2 * 384 + 384)


def lane_mean(v):
    return jnp.sum(v, axis=-1, keepdims=True) * (1.0 / D)


def lanes(v, n):
    return jnp.concatenate([v] * n, axis=1)


def gelu_parts(u):
    density = jnp.exp(u * u * -0.5) * (1.0 / math.sqrt(2.0 * math.pi))
    cdf = 0.5 * (1.0 + lax.erf(u * math.sqrt(0.5)))
    return u * cdf, cdf + u * density


def crop_loop(body, after):
    @pl.loop(0, NC)
    def _(c):
        body(c)
        for k, steps in after.items():

            @pl.when(c == k)
            def _():
                for step in steps:
                    step()


class Links:
    def __init__(self, refs):
        self.__dict__.update(refs)
        r = lax.axis_index("rep")
        s = lax.axis_index("shard")
        self.y, self.x = r // 2, r % 2
        self.z, self.c = s // 2, s % 2
        self.r, self.s = r, s
        self.rx = self.y * 2 + 1 - self.x
        self.ry = (1 - self.y) * 2 + self.x
        self.rd = 3 - r
        self.others = [(self.z + d) % 4 for d in (1, 2, 3)]
        self.dev_core = (r, self.z * 2 + 1 - self.c)
        self.dev_x = (self.rx, s)
        self.dev_y = (self.ry, s)
        self.dev_d = (self.rd, s)
        self.dev_z = [(r, z * 2 + self.c) for z in self.others]
        self.x1, self.y1, self.c1 = 1 - self.x, 1 - self.y, 1 - self.c
        self.s1 = self.z * 2 + self.c1
        self.s_others = [z * 2 + self.c for z in self.others]
        self.s1_others = [z * 2 + self.c1 for z in self.others]
        z1 = self.z // 2 * 2 + 1 - self.z % 2
        self.dev_z1 = (r, z1 * 2 + self.c)
        self.z_give = [1 - self.z % 2, 3 - self.z % 2]
        self.z_keep = [self.z % 2, 2 + self.z % 2]
        self.count = 0
        self.sent = []

    def greet(self):
        barrier = pltpu.get_barrier_semaphore()
        partners = [self.dev_core, self.dev_x, self.dev_y, self.dev_d] + self.dev_z
        for device in partners:
            pl.semaphore_signal(barrier, inc=1, device_id=device, device_id_type=MESH)

    def greeted(self):
        pl.semaphore_wait(pltpu.get_barrier_semaphore(), 7)

    def slot(self):
        self.count += 1
        return self.count - 1

    def copy(self, src, dst, k, device):
        return pltpu.make_async_remote_copy(
            src_ref=src,
            dst_ref=dst,
            send_sem=self.send_sem.at[k],
            recv_sem=self.recv_sem.at[k],
            device_id=device,
            device_id_type=MESH,
        )

    def part(self, g, jy, jx, z, c):
        if g > 4:
            return self.wd.at[z, c, jy, jx, :, columns(g)]
        return self.ws.at[g // 3, jy, jx, z, c, :, columns(g)]

    def column(self, g, jy, jx, c):
        return self.part(g, jy, jx, slice(None), c)

    def plan_gather(self):
        self.ag = [
            dict(
                zed=[self.slot() for _ in range(3)],
                px=[self.slot() for _ in range(3)],
                py=[self.slot() for _ in range(3)],
                relay=[self.slot() for _ in range(3)],
                sib=[self.slot() for _ in range(4)],
            )
            for _ in range(7)
        ]
        self.ag_vec = dict(
            core=self.slot(), zed=[self.slot() for _ in range(3)], sib=[self.slot() for _ in range(3)]
        )

    def send(self, src, dst, k, device, keep):
        def describe():
            return self.copy(src[0](*src[1:]), dst[0](*dst[1:]), k, device)

        describe().start()
        keep.append(describe)

    def at(self, name, *index):
        return getattr(self, name).at[index if len(index) > 1 else index[0]]

    def same(self, ref, k, device, keep):
        self.send(ref, ref, k, device, keep)

    def arrive(self, ref, k, device):
        self.copy(ref[0](*ref[1:]), ref[0](*ref[1:]), k, device).wait_recv()

    def gather_start(self, g):
        own = (self.part, g, self.y, self.x, self.z, self.c)
        for d in range(3):
            self.same(own, self.ag[g]["zed"][d], self.dev_z[d], self.sent)
        if g == 0:
            block = (self.at, "vb", self.s)
            self.same(block, self.ag_vec["core"], self.dev_core, self.sent)
            for d in range(3):
                self.same(block, self.ag_vec["zed"][d], self.dev_z[d], self.sent)

    def x_first(self, g, d):
        return (d != 1) == (g % 2 == 0)

    def gather_plane(self, g):
        for d in range(3):
            z, k = self.others[d], 2 - d
            ref = (self.part, g, self.y, self.x, z, self.c)
            self.arrive(ref, self.ag[g]["zed"][k], self.dev_z[d])
            self.same(ref, self.ag[g]["px"][d], self.dev_x, self.sent)
            self.same(ref, self.ag[g]["py"][d], self.dev_y, self.sent)
            if g == 0:
                block = (self.at, "vb", self.s_others[d])
                self.arrive(block, self.ag_vec["zed"][k], self.dev_z[d])
                self.same(block, self.ag_vec["sib"][d], self.dev_core, self.sent)

        self.same((self.column, g, self.y, self.x, self.c), self.ag[g]["sib"][0], self.dev_core, self.sent)

    def gather_relay(self, g):
        for d in range(3):
            z = self.others[d]
            ref_x = (self.part, g, self.y, self.x1, z, self.c)
            self.arrive(ref_x, self.ag[g]["px"][d], self.dev_x)
            if self.x_first(g, d):
                self.same(ref_x, self.ag[g]["relay"][d], self.dev_y, self.sent)
            ref_y = (self.part, g, self.y1, self.x, z, self.c)
            self.arrive(ref_y, self.ag[g]["py"][d], self.dev_y)
            if not self.x_first(g, d):
                self.same(ref_y, self.ag[g]["relay"][d], self.dev_x, self.sent)

        self.same((self.column, g, self.y, self.x1, self.c), self.ag[g]["sib"][1], self.dev_core, self.sent)
        self.same((self.column, g, self.y1, self.x, self.c), self.ag[g]["sib"][2], self.dev_core, self.sent)

    def gather_last(self, g):
        for d in range(3):
            ref = (self.part, g, self.y1, self.x1, self.others[d], self.c)
            self.arrive(ref, self.ag[g]["relay"][d], self.dev_y if self.x_first(g, d) else self.dev_x)

        self.same((self.column, g, self.y1, self.x1, self.c), self.ag[g]["sib"][3], self.dev_core, self.sent)

    def gather_wait(self, g):
        c = self.c1
        spots = [
            (self.y, self.x),
            (self.y, self.x1),
            (self.y1, self.x),
            (self.y1, self.x1),
        ]
        for j, (jy, jx) in enumerate(spots):
            self.arrive((self.column, g, jy, jx, c), self.ag[g]["sib"][j], self.dev_core)
        if g == 0:
            self.arrive((self.at, "vb", self.s1), self.ag_vec["core"], self.dev_core)
            for d in range(3):
                self.arrive((self.at, "vb", self.s1_others[d]), self.ag_vec["sib"][d], self.dev_core)

    def gather_drain(self):
        for copy in self.sent:
            copy().wait_send()
        self.sent = []

    def plan_sum(self):
        self.rs = [
            dict(
                core=[self.slot() for _ in range(4)],
                one=[self.slot() for _ in range(4)],
                two=[self.slot() for _ in range(4)],
                half=[self.slot() for _ in range(2)],
                zed=[self.slot() for _ in range(3)],
                plane=[self.slot() for _ in range(3)],
            )
            for _ in range(7)
        ]
        self.rs_vec = dict(
            core=self.slot(), one=self.slot(), two=self.slot(), zed=[self.slot() for _ in range(3)]
        )
        self.out = [[] for _ in range(7)]

    def grads(self, g, z, c, jy=slice(None), jx=slice(None)):
        if g > 2:
            return self.part(g, jy, jx, z, c)
        return self.gp.at[jy, jx, pl.ds(pl.multiple_of((z * 2 + c) * SUB, SUB), SUB), third(g)]

    def land(self, name, g, *index):
        ref = getattr(self, name if name == "rc" or g > 2 else name + "t")
        return ref.at[index + (slice(None),) * (len(ref.shape) - len(index) - 1) + (columns(g),)]

    def halved(self, g, k):
        cols = slice(0, 384) if g == 4 else slice(384, 768 if g > 2 else 640)
        return self.act3.at[k, :, :, 0:SUB, cols]

    def total(self, g, r):
        return self.gt.at[0 if g < 3 else (g - 1) // 2, r, :, columns(g)]

    def credit(self, g, i, device):
        if g > 4 or (g > 2 and i == 0):
            pl.semaphore_signal(self.credit_sem.at[(g + 1) % 2 * 8 + i], inc=1, device_id=device, device_id_type=MESH)

    def spend(self, g, i):
        for h in range(2):
            if g == 3 + h or (g == h and i == 0):
                pl.semaphore_wait(self.credit_sem.at[h * 8 + i], 1)

    def add(self, ref, other):
        ref, other = ref[0](*ref[1:]), other[0](*other[1:])
        ref[...] = ref[...] + other[...]

    def sum_start(self, g):
        self.spend(g, 0)
        for z in range(4):
            self.send(
                (self.grads, g, z, self.c1), (self.land, "rc", g, z), self.rs[g]["core"][z], self.dev_core, self.out[g]
            )
        if g == 2:
            self.send((self.at, "vs", 0), (self.at, "vr", 0), self.rs_vec["core"], self.dev_core, self.out[g])

    def items(self, g):
        if g in Z_FIRST:
            return [(0, self.z_keep[0]), (2, self.z_keep[1])]
        return [(z, z) for z in range(4)]

    def sum_half(self, g):
        c = self.c
        for z in range(4):
            self.arrive((self.land, "rc", g, z), self.rs[g]["core"][z], self.dev_core)
            self.add((self.grads, g, z, c), (self.land, "rc", g, z))
        self.credit(g, 0, self.dev_core)
        pl.semaphore_signal(self.half_sem.at[g], inc=1, device_id=self.dev_z1, device_id_type=MESH)
        pl.semaphore_wait(self.half_sem.at[g], 1)
        for k in range(2):
            self.send(
                (self.grads, g, self.z_give[k], c), (self.halved, g, k), self.rs[g]["half"][k], self.dev_z1, self.out[g]
            )

    def sum_one(self, g):
        y, x, c = self.y, self.x, self.c
        for i, (slot, z) in enumerate(self.items(g)):
            mine, came = (self.grads, g, z, c), (self.land, "rc", g, i)
            if g in Z_FIRST:
                came = (self.halved, g, i)
                self.arrive(came, self.rs[g]["half"][i], self.dev_z1)
            else:
                self.arrive(came, self.rs[g]["core"][i], self.dev_core)
            self.add(mine, came)
            if i == 0:
                self.spend(g, 1)
                self.spend(g, 2)
            land = (self.land, "r1", g, slot)
            if slot < 2:
                self.send((self.grads, g, z, c, slice(None), self.x1), land, self.rs[g]["one"][i], self.dev_x, self.out[g])
            else:
                self.send((self.grads, g, z, c, self.y1), land, self.rs[g]["one"][i], self.dev_y, self.out[g])
        if g not in Z_FIRST:
            self.credit(g, 0, self.dev_core)
        if g == 2:
            self.arrive((self.at, "vr", 0), self.rs_vec["core"], self.dev_core)
            self.vs[1] = self.vs[0] + self.vr[0]
            self.send((self.at, "vs", 1), (self.at, "vr", 1), self.rs_vec["one"], self.dev_x, self.out[g])

    def sum_two(self, g):
        y, x, c = self.y, self.x, self.c
        for i, (slot, z) in enumerate(self.items(g)):
            came = (self.land, "r1", g, slot)
            self.arrive(came, self.rs[g]["one"][i], self.dev_x if slot < 2 else self.dev_y)
            self.add((self.grads, g, z, c, slice(None), x) if slot < 2 else (self.grads, g, z, c, y), came)
            if i == 0:
                self.spend(g, 3)
                self.spend(g, 4)
            land = (self.land, "r2", g, slot)
            if slot < 2:
                self.send((self.grads, g, z, c, self.y1, x), land, self.rs[g]["two"][i], self.dev_y, self.out[g])
            else:
                self.send((self.grads, g, z, c, y, self.x1), land, self.rs[g]["two"][i], self.dev_x, self.out[g])
        self.credit(g, 1, self.dev_x)
        self.credit(g, 2, self.dev_y)
        if g == 2:
            self.arrive((self.at, "vr", 1), self.rs_vec["one"], self.dev_x)
            self.vs[2] = self.vs[1] + self.vr[1]
            self.send((self.at, "vs", 2), (self.at, "vr", 2), self.rs_vec["two"], self.dev_y, self.out[g])

    def sum_zed(self, g):
        y, x, c = self.y, self.x, self.c
        for i, (slot, z) in enumerate(self.items(g)):
            came = (self.land, "r2", g, slot)
            self.arrive(came, self.rs[g]["two"][i], self.dev_y if slot < 2 else self.dev_x)
            self.add((self.grads, g, z, c, y, x), came)
        for d in range(3):
            self.spend(g, 5 + d)
        if g in Z_FIRST:
            self.send(
                (self.grads, g, self.others[1], c, y, x),
                (self.land, "rz", g, 1),
                self.rs[g]["zed"][1],
                self.dev_z[1],
                self.out[g],
            )
        else:
            for d in range(3):
                self.send(
                    (self.grads, g, self.others[d], c, y, x),
                    (self.land, "rz", g, 2 - d),
                    self.rs[g]["zed"][d],
                    self.dev_z[d],
                    self.out[g],
                )
        self.credit(g, 3, self.dev_y)
        self.credit(g, 4, self.dev_x)
        if g == 2:
            self.arrive((self.at, "vr", 2), self.rs_vec["two"], self.dev_y)
            self.vs[3] = self.vs[2] + self.vr[2]
            for d in range(3):
                self.send((self.at, "vs", 3), (self.at, "vr", 3 + 2 - d), self.rs_vec["zed"][d], self.dev_z[d], self.out[g])

    def sum_plane(self, g):
        total = self.grads(g, self.z, self.c, self.y, self.x)[...].astype(f32)
        for d in (1,) if g in Z_FIRST else range(3):
            self.arrive((self.land, "rz", g, d), self.rs[g]["zed"][2 - d], self.dev_z[d])
            total = total + self.land("rz", g, d)[...].astype(f32)
        own = (self.total, g, self.r)
        self.total(g, self.r)[...] = total.astype(bf)
        for k, device in enumerate((self.dev_x, self.dev_y, self.dev_d)):
            self.send(own, own, self.rs[g]["plane"][k], device, self.out[g])
        for d in range(3):
            self.credit(g, 5 + 2 - d, self.dev_z[d])
        if g == 2:
            vec = self.vs[3]
            for d in range(3):
                self.arrive((self.at, "vr", 3 + d), self.rs_vec["zed"][2 - d], self.dev_z[d])
                vec = vec + self.vr[3 + d]
            self.vec_total[...] = pltpu.roll(vec, lax.rem(D - self.s * SUB, D), 1)[:, 0:128]

    def sum_wait(self, g):
        for k, (r, device) in enumerate(((self.rx, self.dev_x), (self.ry, self.dev_y), (self.rd, self.dev_d))):
            self.arrive((self.total, g, r), self.rs[g]["plane"][k], device)

    def sum_drain(self, g):
        for copy in self.out[g]:
            copy().wait_send()
        self.out[g] = []


def layer_kernel(linked, *refs):
    if linked:
        (tok_h, cot_h, del_ref, len_ref, vec_in, qkv_h, out_h, up_h, down_h) = refs[:9]
        (y_h, tg_h, t0_h, t1_h, t2_h, vg_out) = refs[9:15]
        rest = refs[15:]
    else:
        (tok_h, cot_h, del_ref, len_ref, vec_in, ws_h, wd_h) = refs[:7]
        (y_h, tg_h, g0_h, g1_h, g2_h, vg_out) = refs[7:13]
        rest = refs[13:]
    (ws, wd, x, qkv, pt, mixed, nrm1, root1, fl, act, act3, gp, gs, gsec, cot, keep, vec_ref, vg_ref, sem) = rest[:19]
    if linked:
        names = ("vb", "rc", "r1", "r2", "rz", "r1t", "r2t", "rzt", "gt", "vs", "vr", "send_sem", "recv_sem", "credit_sem", "half_sem")
        net = Links(dict(zip(names, rest[19:]), ws=ws, wd=wd, gp=gp, act3=act3, vec_total=vg_out))
        net.plan_gather()
        net.plan_sum()

    cp_x = pltpu.make_async_copy(tok_h, x, sem.at[0])
    cp_cot = pltpu.make_async_copy(cot_h, cot, sem.at[1])
    lane = lax.broadcasted_iota(jnp.int32, (CROP, 128), 1)
    low_half = lane < 64

    def half(v, h):
        return jnp.where(low_half if h == 0 else ~low_half, v, jnp.zeros_like(v))

    def vrow(r):
        return vec_ref[r : r + 1, :]

    def mat(g, j):
        if g == 2:
            return wd[j].reshape(D, D)
        return ws[g, j // 2, j % 2].reshape(D, D)

    def mat_third(j, t):
        return ws[0, j // 2, j % 2, :, :, :, third(t)].reshape(D, 256)

    def step(name, *a):
        return functools.partial(getattr(net, name), *a) if linked else (lambda: None)

    def after(name):
        plan = {}
        for kind, table in (("gather_", GATHER_PLAN), ("sum_", SUM_PLAN)):
            for c, steps in table.get(name, {}).items():
                plan[c] = [step(kind + what, g) for what, g in steps]
        return plan

    def now(name):
        for act_now in after(name).get(0, ()):
            act_now()

    if linked:
        net.greet()
        loads = []
        for j in range(4):
            src = qkv_h.at[:, j * D : (j + 1) * D] if j < 3 else out_h
            loads.append(pltpu.make_async_copy(src, gs.at[j * SUB : (j + 1) * SUB], sem.at[2 + j]))
        for j in range(4):
            loads.append(
                pltpu.make_async_copy(
                    up_h.at[:, j * D : (j + 1) * D], nrm1.at[j * SUB : (j + 1) * SUB], sem.at[6 + j]
                )
            )
        loads.append(pltpu.make_async_copy(down_h, gs.at[4 * SUB : 8 * SUB], sem.at[10]))
        for load in loads:
            load.start()
        cp_x.start()
        cp_cot.start()
        net.vs[0, :, 0:128] = jnp.zeros((16, 128), f32)
        net.vs[0, 0 : vec_in.shape[0], 0 : vec_in.shape[1]] = vec_in[...]
        net.vb[net.s] = net.vs[0, :, 0:128].astype(bf)
        for j in range(4):
            loads[j].wait()
            ws[0, j // 2, j % 2, net.z, net.c] = gs[j * SUB : (j + 1) * SUB].astype(bf)
        net.greeted()
        net.gather_start(0)
        for j in range(4):
            loads[4 + j].wait()
            ws[1, j // 2, j % 2, net.z, net.c] = nrm1[j * SUB : (j + 1) * SUB].astype(bf)
        loads[8].wait()
        for j in range(4):
            wd[net.z, net.c, j // 2, j % 2] = gs[(4 + j) * SUB : (5 + j) * SUB].astype(bf)
    else:
        vec_ref[...] = vec_in[...]
        cp_ws = pltpu.make_async_copy(ws_h, ws, sem.at[2])
        cp_wd = pltpu.make_async_copy(wd_h, wd, sem.at[3])
        for copy in (cp_ws, cp_wd, cp_x, cp_cot):
            copy.start()
        cp_ws.wait()
        cp_wd.wait()
    place = lax.broadcasted_iota(jnp.int32, (1, CROP), 1)
    allowed = [
        jnp.where(((del_ref[c : c + 1, :] == 1) | (place == 0)) & (place < len_ref[c]), 1.0, 0.0) for c in range(NC)
    ]
    mcol = jnp.concatenate(allowed * (8 // NC), axis=0).T
    for c in range(NC):
        keep[c * CROP : (c + 1) * CROP, :] = jnp.broadcast_to(mcol[:, c : c + 1], (CROP, 128)).astype(bf)
    vg_ref[...] = jnp.zeros_like(vg_ref)
    cp_x.wait()
    cp_cot.wait()
    if linked:
        now("start")
        row = lax.broadcasted_iota(jnp.int32, (128, D), 0)
        col = lax.broadcasted_iota(jnp.int32, (128, D), 1)
        vec = jnp.zeros((16, D), f32)
        for s in range(8):
            pick = ((col == row + s * SUB) & (row < SUB)).astype(f32).astype(bf)
            vec = vec + dg(net.vb[s], pick, 1, 0)
        vec_ref[...] = vec

    def project(t, c):
        r = rows_of(c)
        xv = x[r, :]
        for b in range(3):
            y = dg(xv, mat_third(b, t), 1, 0)
            if b == 0:
                y = y + vec_ref[0:1, third(t)]
            if b == 2:
                y = y + vec_ref[1:2, third(t)]
            qkv[r, t * D + b * 256 : t * D + (b + 1) * 256] = y.astype(bf)

    def attend(t, c):
        r = rows_of(c)
        kp = lanes(keep[r, :].astype(f32), 2) > 0.5
        for p in range(2):
            q, k, v = (qkv[r, t * D + b * 256 + p * 128 : t * D + b * 256 + (p + 1) * 128] for b in range(3))
            q = q * jnp.asarray(0.125, bf)
            o = None
            for h in range(2):
                st = dg(k, half(q, h), 1, 1)
                st = jnp.where(kp, st, -1e30)
                e = jnp.exp(st - jnp.max(st, axis=0, keepdims=True))
                pr = (e * (1.0 / jnp.sum(e, axis=0, keepdims=True))).astype(bf)
                pt[c, 4 * t + 2 * p + h] = pr
                w = dg(pr, half(v, h), 0, 0)
                o = w if o is None else o + w
            mixed[r, t * 256 + p * 128 : t * 256 + (p + 1) * 128] = o.astype(bf)

    for t in range(3):
        crop_loop(functools.partial(project, t), after(f"project{t}"))
        crop_loop(functools.partial(attend, t), after(f"attend{t}"))

    def body(c):
        r = rows_of(c)
        h = x[r, :].astype(f32) + (dg(mixed[r, :], mat(0, 3), 1, 0) + vrow(2))
        h = h - lane_mean(h)
        root = lax.rsqrt(lane_mean(h * h) + norm_epsilon)
        n = h * root
        nrm1[r, :] = n
        root1[r, :] = jnp.broadcast_to(root, (CROP, 128))
        fl[r, :] = (n * vrow(3) + vrow(4)).astype(bf)

    crop_loop(body, after("out"))

    def body(c):
        r = rows_of(c)
        a = fl[r, :]
        for j in range(4):
            u = dg(a, mat(1, j), 1, 0) + vrow(5 + j)
            g, d = gelu_parts(u)
            if j < 3:
                act[r, j * D : (j + 1) * D] = g.astype(bf)
            else:
                act3[c // 2, c % 2] = g.astype(bf).reshape(2, 128, D)
            gp[j // 2, j % 2, r, :] = d.astype(bf)

    crop_loop(body, after("up"))

    def body(c):
        r = rows_of(c)
        s = dg(act[r, :], wd[0:3].reshape(3 * D, D), 1, 0)
        s = s + dg(act3[c // 2, c % 2].reshape(CROP, D), wd[3].reshape(D, D), 1, 0) + vrow(9)
        h = nrm1[r, :] * vrow(3) + vrow(4) + s
        h = h - lane_mean(h)
        root = lax.rsqrt(lane_mean(h * h) + norm_epsilon)
        n = h * root
        G = cot[r, :].astype(f32) * lanes(keep[r, :].astype(f32), 6)
        cot[r, :] = (n * vrow(10) + vrow(11)).astype(bf)
        vg_ref[10:11, :] += jnp.sum(G * n, axis=0, keepdims=True)
        vg_ref[11:12, :] += jnp.sum(G, axis=0, keepdims=True)
        dn = G * vrow(10)
        g2 = root * (dn - lane_mean(dn) - n * lane_mean(dn * n))
        gs[r, :] = g2
        gb = g2.astype(bf)
        gsec[r, :] = gb
        vg_ref[9:10, :] += jnp.sum(gb.astype(f32), axis=0, keepdims=True)

    crop_loop(body, after("down"))
    cp_y = pltpu.make_async_copy(cot, y_h, sem.at[0])
    cp_y.start()

    def body(c):
        r = rows_of(c)
        a = gsec[r, :]
        for j in range(4):
            ga = dg(a, mat(2, j), 1, 1)
            gi = (ga * gp[j // 2, j % 2, r, :].astype(f32)).astype(bf)
            gp[j // 2, j % 2, r, :] = gi
            vg_ref[5 + j : 6 + j, :] += jnp.sum(gi.astype(f32), axis=0, keepdims=True)

    crop_loop(body, after("act_back"))
    step("gather_drain")()

    @pl.loop(0, 3)
    def _(i):
        m = pl.ds(pl.multiple_of(i * D, D), D)
        wd[i] = dg(act[:, m], gsec[...], 0, 0).astype(bf).reshape(2, 2, 2, SUB, D)

    wd[3] = dg(act3[...].reshape(T, D), gsec[...], 0, 0).astype(bf).reshape(2, 2, 2, SUB, D)

    now("down_grad")

    def body(c):
        r = rows_of(c)
        G = gs[r, :]
        for j in range(4):
            G = G + dg(gp[j // 2, j % 2, r, :], mat(1, j), 1, 1)
        n = nrm1[r, :]
        vg_ref[3:4, :] += jnp.sum(G * n, axis=0, keepdims=True)
        vg_ref[4:5, :] += jnp.sum(G, axis=0, keepdims=True)
        dn = G * vrow(3)
        g1 = lanes(root1[r, :], 6) * (dn - lane_mean(dn) - n * lane_mean(dn * n))
        gs[r, :] = g1
        gb = g1.astype(bf)
        gsec[r, :] = gb
        vg_ref[2:3, :] += jnp.sum(gb.astype(f32), axis=0, keepdims=True)

    crop_loop(body, after("first_back"))

    def body(j):
        ws[1, j // 2, j % 2] = dg(fl[...], gp[j // 2, j % 2], 0, 0).astype(bf).reshape(4, 2, SUB, D)

    crop_loop(body, after("up_grad"))

    def body(c):
        r = rows_of(c)
        fl[r, :] = dg(gsec[r, :], mat(0, 3), 1, 1).astype(bf)

    crop_loop(body, after("mixed_back"))

    def attend_back(t, c):
        r = rows_of(c)
        for p in range(2):
            at = [slice(t * D + b * 256 + p * 128, t * D + b * 256 + (p + 1) * 128) for b in range(3)]
            cols = slice(t * 256 + p * 128, t * 256 + (p + 1) * 128)
            q, k, v = (qkv[r, cut] for cut in at)
            q = q * jnp.asarray(0.125, bf)
            do = fl[r, cols]
            dq = dk = dv = None
            for h in range(2):
                dom = half(do, h)
                dp = dg(v, dom, 1, 1)
                prb = pt[c, 4 * t + 2 * p + h]
                pr = prb.astype(f32)
                delta = jnp.sum(pr * dp, axis=0, keepdims=True)
                ds = (pr * (dp - delta)).astype(bf)
                tv = dg(prb, dom, 1, 0)
                tk = dg(ds, half(q, h), 1, 0)
                tq = dg(ds, half(k, h), 0, 0)
                dq, dk, dv = (tq, tk, tv) if dq is None else (dq + tq, dk + tk, dv + tv)
            dq = (dq * 0.125).astype(bf)
            dv = dv.astype(bf)
            act[r, at[0]] = dq
            act[r, at[1]] = dk.astype(bf)
            act[r, at[2]] = dv
            vg_ref[0:1, cols] += jnp.sum(dq.astype(f32), axis=0, keepdims=True)
            vg_ref[1:2, cols] += jnp.sum(dv.astype(f32), axis=0, keepdims=True)

    def third_grads(t):
        g = dg(x[...], act[:, t * D : (t + 1) * D], 0, 0).astype(bf)
        for j in range(3):
            gp[j // 2, j % 2, 0:D, third(t)] = g[:, third(j)]
        gp[1, 1, 0:D, third(t)] = dg(mixed[...], gsec[:, third(t)], 0, 0).astype(bf)

    for t in range(3):
        crop_loop(functools.partial(attend_back, t), after(f"attend_back{t}"))
        if linked and t == 2:
            net.vs[0] = vg_ref[...]
        third_grads(t)
        now(f"grads{t}")

    def body(c):
        r = rows_of(c)
        G = gs[r, :]
        for b in range(3):
            for t in range(3):
                G = G + dg(act[r, t * D + b * 256 : t * D + (b + 1) * 256], mat_third(b, t), 1, 1)
        gsec[r, :] = G.astype(bf)

    crop_loop(body, after("token"))
    cp_tg = pltpu.make_async_copy(gsec, tg_h, sem.at[1])
    cp_tg.start()
    if linked:
        now("end")
        shares = [pltpu.make_async_copy(net.gt.at[i], t_h, sem.at[2 + i]) for i, t_h in enumerate((t0_h, t1_h, t2_h))]
        for copy in shares:
            copy.start()
        for g in range(7):
            net.sum_drain(g)
        for copy in shares:
            copy.wait()
    else:
        vg_out[...] = vg_ref[...]
        copies = [
            pltpu.make_async_copy(gp.at[:, :, 0:D], g0_h, sem.at[2]),
            pltpu.make_async_copy(ws.at[1], g1_h, sem.at[3]),
            pltpu.make_async_copy(wd, g2_h, sem.at[4]),
        ]
        for copy in copies:
            copy.start()
        for copy in copies:
            copy.wait()
    cp_y.wait()
    cp_tg.wait()


WS = (2, 2, 2, 4, 2, SUB, D)
WD = (4, 2, 2, 2, SUB, D)


def layer(linked, *arrays):
    hbm = pl.BlockSpec(memory_space=pl.ANY)
    near = pl.BlockSpec(memory_space=pltpu.VMEM)
    VM = pltpu.VMEM
    shape = jax.ShapeDtypeStruct
    outs = [(shape((T, D), bf), hbm), (shape((T, D), bf), hbm)]
    if linked:
        outs += [(shape((4, SUB, D), bf), hbm)] * 3
    else:
        outs += [(shape((2, 2, D, D), bf), hbm), (shape(WS[1:], bf), hbm), (shape(WD, bf), hbm)]
    outs += [(shape((16, 128 if linked else D), f32), near)]
    scratch = [
        VM(WS, bf),
        VM(WD, bf),
        VM((T, D), bf),
        VM((T, 3 * D), bf),
        VM((NC, H, CROP, CROP), bf),
        VM((T, D), bf),
        VM((T, D), f32),
        VM((T, 128), f32),
        VM((T, D), bf),
        VM((T, 3 * D), bf),
        VM((2, 2, 2, 128, D), bf),
        VM((2, 2, T, D), bf),
        VM((T, D), f32),
        VM((T, D), bf),
        VM((T, D), bf),
        VM((T, 128), bf),
        VM((16, D), f32),
        VM((16, D), f32),
        pltpu.SemaphoreType.DMA((11,)),
    ]
    params = dict(vmem_limit_bytes=63 * 2**20)
    if linked:
        transfers = 7 * (3 + 3 + 3 + 3 + 4) + 7 + 7 * (4 + 4 + 4 + 2 + 3 + 3) + 6
        scratch += [
            VM((8, 16, 128), bf),
            VM((4, 2, 2, SUB, D), bf),
            VM((4, 2, SUB, D), bf),
            VM((4, SUB, D), bf),
            VM((3, SUB, D), bf),
            VM((4, 2, SUB, D), bf),
            VM((4, SUB, D), bf),
            VM((3, SUB, D), bf),
            VM((3, 4, SUB, D), bf),
            VM((4, 16, D), f32),
            VM((6, 16, D), f32),
            pltpu.SemaphoreType.DMA((transfers,)),
            pltpu.SemaphoreType.DMA((transfers,)),
            pltpu.SemaphoreType.REGULAR((16,)),
            pltpu.SemaphoreType.REGULAR((7,)),
        ]
        params.update(collective_id=0, has_side_effects=True)
    return pl.pallas_call(
        functools.partial(layer_kernel, linked),
        out_shape=[o[0] for o in outs],
        in_specs=[hbm, hbm, near, pl.BlockSpec(memory_space=pltpu.SMEM), near] + [hbm] * (len(arrays) - 5),
        out_specs=[o[1] for o in outs],
        scratch_shapes=scratch,
        compiler_params=pltpu.CompilerParams(**params),
    )(*arrays)


def adam_update(gradient, first_moment, second_moment):
    first_new = decay_first * first_moment + (1.0 - decay_first) * gradient
    second_new = decay_second * second_moment + (1.0 - decay_second) * gradient * gradient
    step_dir = first_new / correct_first / (jnp.sqrt(second_new / correct_second) + adam_epsilon)
    return (step_dir, first_new)


def finish(output, token_grad, gradients, moments):
    updated = [adam_update(g, m, s) for g, m, s in zip(gradients, moments[:5], moments[5:])]
    return (
        (output, token_grad)
        + tuple(gradients)
        + tuple(u[0] for u in updated)
        + tuple(u[1] for u in updated)
    )


def side_by_side(blocks):
    return jnp.concatenate([blocks[j] for j in range(blocks.shape[0])], axis=1)


def adam_kernel(*refs):
    sums, moments, passed, outs, placed = refs[:4], refs[4:14], refs[14:16], refs[16:31], refs[31:33]
    hold, sem = refs[33:]
    fetch = [pltpu.make_async_copy(a, hold.at[i], sem.at[i]) for i, a in enumerate(passed)]
    store = [pltpu.make_async_copy(hold.at[i], a, sem.at[2 + i]) for i, a in enumerate(placed)]

    @pl.when(pl.program_id(0) == 0)
    def _():
        for copy in fetch:
            copy.start()

    @pl.when(pl.program_id(0) == 1)
    def _():
        for i in range(2):
            fetch[i].wait()
            store[i].start()

    square, up, down, vec = (ref[...] for ref in sums)

    def update(k, cut, g):
        at = Ellipsis if cut is None else (slice(None), cut)
        g = g.astype(f32)
        step, first = adam_update(g, moments[k][at], moments[5 + k][at])
        outs[k][at] = g
        outs[5 + k][at] = step
        outs[10 + k][at] = first

    for j in range(4):
        cut = slice(j * D, (j + 1) * D)
        update(*((0, cut) if j < 3 else (1, None)), square[j])
        update(2, cut, up[j])
    update(3, None, down)

    @pl.when(pl.program_id(0) == 0)
    def _():
        rows, width = outs[4].shape
        update(4, None, vec[0:rows, 0:width])

    @pl.when(pl.program_id(0) == pl.num_programs(0) - 1)
    def _():
        for copy in store:
            copy.wait()


def adam(sums, moments, passed, steps=3):
    def rows(shape):
        return pl.BlockSpec((shape[0] // steps, shape[1]), lambda i: (i, 0))

    def whole(shape):
        return pl.BlockSpec(shape, lambda i: (0, 0))

    hbm = pl.BlockSpec(memory_space=pl.ANY)
    parts = pl.BlockSpec((4, SUB // steps, D), lambda i: (0, i, 0))
    specs = [whole(m.shape) if k == 4 else rows(m.shape) for k, m in enumerate(moments[:5])]
    return pl.pallas_call(
        adam_kernel,
        grid=(steps,),
        out_shape=[jax.ShapeDtypeStruct(m.shape, f32) for m in moments[:5]] * 3
        + [jax.ShapeDtypeStruct(a.shape, a.dtype) for a in passed],
        in_specs=[parts, parts, rows((4 * SUB, D)), whole((16, 128))] + specs * 2 + [hbm] * 2,
        out_specs=specs * 3 + [hbm] * 2,
        scratch_shapes=[pltpu.VMEM((2, *passed[0].shape), bf), pltpu.SemaphoreType.DMA((4,))],
        compiler_params=pltpu.CompilerParams(vmem_limit_bytes=63 * 2**20),
    )(*sums, *moments, *passed)


def per_device_linked(tokens, cotangent, deletion, lengths, qkv, out, up, down, vectors, *moments):
    output, token_grad, square, tall, wide, vec = layer(
        True, tokens, cotangent, deletion, lengths, vectors, qkv, out, up, down
    )
    *updated, output, token_grad = adam((square, tall, wide.reshape(4 * SUB, D), vec), moments, (output, token_grad))
    return (output, token_grad) + tuple(updated)


def per_device_plain(tokens, cotangent, deletion, lengths, qkv, out, up, down, vectors, *moments):
    blocks = [qkv[:, b * D : (b + 1) * D] for b in range(3)] + [out]
    blocks += [up[:, b * D : (b + 1) * D] for b in range(4)]
    square = lax.all_gather(jnp.stack(blocks).astype(bf), "shard", axis=1, tiled=True)
    tall = lax.all_gather(down.astype(bf), "shard", axis=0, tiled=True)
    vec = lax.all_gather(vectors.astype(bf), "shard", axis=1, tiled=True).astype(f32)
    output, token_grad, g0, g1, g2, vec = layer(
        False,
        tokens,
        cotangent,
        deletion,
        lengths,
        jnp.pad(vec, ((0, 4), (0, 0))),
        square.reshape(WS),
        tall.reshape(WD),
    )
    g0 = g0.reshape(4, D, D)
    square = lax.psum_scatter(
        jnp.concatenate([g0, g1.reshape(4, D, D)]).astype(f32), "shard", scatter_dimension=1, tiled=True
    )
    tall = lax.psum_scatter(g2.reshape(FF, D).astype(f32), "shard", scatter_dimension=0, tiled=True)
    vec = lax.psum_scatter(vec[:12], "shard", scatter_dimension=1, tiled=True)
    square, tall, vec = (lax.psum(g.astype(bf), "rep").astype(f32) for g in (square, tall, vec))
    gradients = (side_by_side(square[:3]), square[3], side_by_side(square[4:]), tall, vec)
    return finish(output, token_grad, gradients, moments)


def solution(mesh):
    rows = P(("rep", "shard"), None)
    weights = (P("shard", None),) * 4 + (P(None, "shard"),)
    linked = mesh.shape["rep"] == 4 and mesh.shape["shard"] == 8
    return jax.shard_map(
        per_device_linked if linked else per_device_plain,
        mesh=mesh,
        in_specs=(rows, rows, rows, P(("rep", "shard"))) + weights * 3,
        out_specs=(rows, rows) + weights * 3,
        check_vma=False,
    )
```

```python
import functools
import math

import jax
import jax.numpy as jnp
from jax import lax
from jax.experimental import pallas as pl
from jax.experimental.pallas import tpu as pltpu
from jax.sharding import PartitionSpec as P

D = 768
H = 12
FF = 3072
CROP = 256
T = 1024
NC = 4
SUB = 96
bf = jnp.bfloat16
f32 = jnp.float32
MESH = pl.DeviceIdType.MESH
Z_FIRST = (4, 6, 2)
GATHER_PLAN = {
    "start": {
        0: [("plane", 0), ("start", 1), ("relay", 0), ("plane", 1), ("start", 2), ("last", 0), ("wait", 0), ("start", 3)],
    },
    "project0": {
        1: [("relay", 1)],
        2: [("plane", 2)],
    },
    "attend0": {
        1: [("last", 1)],
        2: [("start", 4)],
        3: [("wait", 1), ("relay", 2), ("plane", 3)],
    },
    "attend1": {
        0: [("last", 2), ("start", 5)],
        2: [("wait", 2), ("plane", 4)],
        3: [("relay", 3)],
    },
    "project2": {
        2: [("start", 6)],
    },
    "attend2": {
        1: [("plane", 5), ("relay", 4)],
        3: [("last", 3)],
    },
    "out": {
        1: [("wait", 3)],
        3: [("plane", 6), ("relay", 5), ("last", 4), ("wait", 4)],
    },
    "up": {
        1: [("relay", 6)],
        2: [("last", 5)],
        3: [("last", 6), ("wait", 5), ("wait", 6)],
    },
}
SUM_PLAN = {
    "down_grad": {
        0: [("start", 5), ("start", 6)],
    },
    "first_back": {
        1: [("one", 5)],
        2: [("half", 6)],
    },
    "up_grad": {
        2: [("two", 5)],
        3: [("start", 3), ("start", 4)],
    },
    "attend_back0": {
        0: [("zed", 5), ("one", 3)],
        1: [("one", 6), ("half", 4)],
    },
    "grads0": {
        0: [("start", 0), ("plane", 5)],
    },
    "attend_back1": {
        0: [("two", 3)],
        1: [("one", 0), ("two", 6)],
    },
    "grads1": {
        0: [("wait", 5), ("start", 1)],
    },
    "attend_back2": {
        0: [("zed", 3)],
        1: [("one", 4), ("one", 1)],
        2: [("two", 0)],
        3: [("zed", 6)],
    },
    "grads2": {
        0: [("plane", 3), ("start", 2), ("two", 4)],
    },
    "token": {
        1: [("plane", 6), ("half", 2), ("two", 1)],
    },
    "end": {
        0: [("zed", 0), ("wait", 3), ("zed", 4), ("one", 2), ("wait", 6), ("zed", 1), ("plane", 0), ("two", 2), ("plane", 4), ("wait", 0), ("zed", 2), ("plane", 1), ("wait", 4), ("plane", 2), ("wait", 1), ("wait", 2)],
    },
}

norm_epsilon = 1e-06
decay_first = 0.9
decay_second = 0.999
correct_first = 1.0 - 2.6561398887587544e-05
correct_second = 0.0952078528862904
adam_epsilon = 1e-08


def dg(a, b, ca, cb):
    return lax.dot_general(a, b, (((ca,), (cb,)), ((), ())), preferred_element_type=f32)


def rows_of(c):
    return pl.ds(pl.multiple_of(c * CROP, CROP), CROP)


def third(t):
    return slice(t * 256, (t + 1) * 256)


def columns(g):
    return third(g) if g < 3 else slice((g + 1) % 2 * 384, (g + 1) % 2 * 384 + 384)


def lane_mean(v):
    return jnp.sum(v, axis=-1, keepdims=True) * (1.0 / D)


def lanes(v, n):
    return jnp.concatenate([v] * n, axis=1)


def gelu_parts(u):
    density = jnp.exp(u * u * -0.5) * (1.0 / math.sqrt(2.0 * math.pi))
    cdf = 0.5 * (1.0 + lax.erf(u * math.sqrt(0.5)))
    return u * cdf, cdf + u * density


def crop_loop(body, after):
    @pl.loop(0, NC)
    def _(c):
        body(c)
        for k, steps in after.items():

            @pl.when(c == k)
            def _():
                for step in steps:
                    step()


class Links:
    def __init__(self, refs):
        self.__dict__.update(refs)
        r = lax.axis_index("rep")
        s = lax.axis_index("shard")
        self.y, self.x = r // 2, r % 2
        self.z, self.c = s // 2, s % 2
        self.r, self.s = r, s
        self.rx = self.y * 2 + 1 - self.x
        self.ry = (1 - self.y) * 2 + self.x
        self.rd = 3 - r
        self.others = [(self.z + d) % 4 for d in (1, 2, 3)]
        self.dev_core = (r, self.z * 2 + 1 - self.c)
        self.dev_x = (self.rx, s)
        self.dev_y = (self.ry, s)
        self.dev_d = (self.rd, s)
        self.dev_z = [(r, z * 2 + self.c) for z in self.others]
        self.x1, self.y1, self.c1 = 1 - self.x, 1 - self.y, 1 - self.c
        self.s1 = self.z * 2 + self.c1
        self.s_others = [z * 2 + self.c for z in self.others]
        self.s1_others = [z * 2 + self.c1 for z in self.others]
        z1 = self.z // 2 * 2 + 1 - self.z % 2
        self.dev_z1 = (r, z1 * 2 + self.c)
        self.z_give = [1 - self.z % 2, 3 - self.z % 2]
        self.z_keep = [self.z % 2, 2 + self.z % 2]
        self.count = 0
        self.sent = []

    def greet(self):
        barrier = pltpu.get_barrier_semaphore()
        partners = [self.dev_core, self.dev_x, self.dev_y, self.dev_d] + self.dev_z
        for device in partners:
            pl.semaphore_signal(barrier, inc=1, device_id=device, device_id_type=MESH)

    def greeted(self):
        pl.semaphore_wait(pltpu.get_barrier_semaphore(), 7)

    def slot(self):
        self.count += 1
        return self.count - 1

    def copy(self, src, dst, k, device):
        return pltpu.make_async_remote_copy(
            src_ref=src,
            dst_ref=dst,
            send_sem=self.send_sem.at[k],
            recv_sem=self.recv_sem.at[k],
            device_id=device,
            device_id_type=MESH,
        )

    def part(self, g, jy, jx, z, c):
        if g > 4:
            return self.wd.at[z, c, jy, jx, :, columns(g)]
        return self.ws.at[g // 3, jy, jx, z, c, :, columns(g)]

    def column(self, g, jy, jx, c):
        return self.part(g, jy, jx, slice(None), c)

    def plan_gather(self):
        self.ag = [
            dict(
                zed=[self.slot() for _ in range(3)],
                px=[self.slot() for _ in range(3)],
                py=[self.slot() for _ in range(3)],
                relay=[self.slot() for _ in range(3)],
                sib=[self.slot() for _ in range(4)],
            )
            for _ in range(7)
        ]
        self.ag_vec = dict(
            core=self.slot(), zed=[self.slot() for _ in range(3)], sib=[self.slot() for _ in range(3)]
        )

    def send(self, src, dst, k, device, keep):
        def describe():
            return self.copy(src[0](*src[1:]), dst[0](*dst[1:]), k, device)

        describe().start()
        keep.append(describe)

    def at(self, name, *index):
        return getattr(self, name).at[index if len(index) > 1 else index[0]]

    def same(self, ref, k, device, keep):
        self.send(ref, ref, k, device, keep)

    def arrive(self, ref, k, device):
        self.copy(ref[0](*ref[1:]), ref[0](*ref[1:]), k, device).wait_recv()

    def gather_start(self, g):
        own = (self.part, g, self.y, self.x, self.z, self.c)
        for d in range(3):
            self.same(own, self.ag[g]["zed"][d], self.dev_z[d], self.sent)
        if g == 0:
            block = (self.at, "vb", self.s)
            self.same(block, self.ag_vec["core"], self.dev_core, self.sent)
            for d in range(3):
                self.same(block, self.ag_vec["zed"][d], self.dev_z[d], self.sent)

    def x_first(self, g, d):
        return (d != 1) == (g % 2 == 0)

    def gather_plane(self, g):
        for d in range(3):
            z, k = self.others[d], 2 - d
            ref = (self.part, g, self.y, self.x, z, self.c)
            self.arrive(ref, self.ag[g]["zed"][k], self.dev_z[d])
            self.same(ref, self.ag[g]["px"][d], self.dev_x, self.sent)
            self.same(ref, self.ag[g]["py"][d], self.dev_y, self.sent)
            if g == 0:
                block = (self.at, "vb", self.s_others[d])
                self.arrive(block, self.ag_vec["zed"][k], self.dev_z[d])
                self.same(block, self.ag_vec["sib"][d], self.dev_core, self.sent)

        self.same((self.column, g, self.y, self.x, self.c), self.ag[g]["sib"][0], self.dev_core, self.sent)

    def gather_relay(self, g):
        for d in range(3):
            z = self.others[d]
            ref_x = (self.part, g, self.y, self.x1, z, self.c)
            self.arrive(ref_x, self.ag[g]["px"][d], self.dev_x)
            if self.x_first(g, d):
                self.same(ref_x, self.ag[g]["relay"][d], self.dev_y, self.sent)
            ref_y = (self.part, g, self.y1, self.x, z, self.c)
            self.arrive(ref_y, self.ag[g]["py"][d], self.dev_y)
            if not self.x_first(g, d):
                self.same(ref_y, self.ag[g]["relay"][d], self.dev_x, self.sent)

        self.same((self.column, g, self.y, self.x1, self.c), self.ag[g]["sib"][1], self.dev_core, self.sent)
        self.same((self.column, g, self.y1, self.x, self.c), self.ag[g]["sib"][2], self.dev_core, self.sent)

    def gather_last(self, g):
        for d in range(3):
            ref = (self.part, g, self.y1, self.x1, self.others[d], self.c)
            self.arrive(ref, self.ag[g]["relay"][d], self.dev_y if self.x_first(g, d) else self.dev_x)

        self.same((self.column, g, self.y1, self.x1, self.c), self.ag[g]["sib"][3], self.dev_core, self.sent)

    def gather_wait(self, g):
        c = self.c1
        spots = [
            (self.y, self.x),
            (self.y, self.x1),
            (self.y1, self.x),
            (self.y1, self.x1),
        ]
        for j, (jy, jx) in enumerate(spots):
            self.arrive((self.column, g, jy, jx, c), self.ag[g]["sib"][j], self.dev_core)
        if g == 0:
            self.arrive((self.at, "vb", self.s1), self.ag_vec["core"], self.dev_core)
            for d in range(3):
                self.arrive((self.at, "vb", self.s1_others[d]), self.ag_vec["sib"][d], self.dev_core)

    def gather_drain(self):
        for copy in self.sent:
            copy().wait_send()
        self.sent = []

    def plan_sum(self):
        self.rs = [
            dict(
                core=[self.slot() for _ in range(4)],
                one=[self.slot() for _ in range(4)],
                two=[self.slot() for _ in range(4)],
                half=[self.slot() for _ in range(2)],
                zed=[self.slot() for _ in range(3)],
                plane=[self.slot() for _ in range(3)],
            )
            for _ in range(7)
        ]
        self.rs_vec = dict(
            core=self.slot(), one=self.slot(), two=self.slot(), zed=[self.slot() for _ in range(3)]
        )
        self.out = [[] for _ in range(7)]

    def grads(self, g, z, c, jy=slice(None), jx=slice(None)):
        if g > 2:
            return self.part(g, jy, jx, z, c)
        return self.gp.at[jy, jx, pl.ds(pl.multiple_of((z * 2 + c) * SUB, SUB), SUB), third(g)]

    def land(self, name, g, *index):
        ref = getattr(self, name if name == "rc" or g > 2 else name + "t")
        return ref.at[index + (slice(None),) * (len(ref.shape) - len(index) - 1) + (columns(g),)]

    def halved(self, g, k):
        cols = slice(0, 384) if g == 4 else slice(384, 768 if g > 2 else 640)
        return self.act3.at[k, :, :, 0:SUB, cols]

    def total(self, g, r):
        return self.gt.at[0 if g < 3 else (g - 1) // 2, r, :, columns(g)]

    def credit(self, g, i, device):
        if g > 4 or (g > 2 and i == 0):
            pl.semaphore_signal(self.credit_sem.at[(g + 1) % 2 * 8 + i], inc=1, device_id=device, device_id_type=MESH)

    def spend(self, g, i):
        for h in range(2):
            if g == 3 + h or (g == h and i == 0):
                pl.semaphore_wait(self.credit_sem.at[h * 8 + i], 1)

    def add(self, ref, other):
        ref, other = ref[0](*ref[1:]), other[0](*other[1:])
        ref[...] = ref[...] + other[...]

    def sum_start(self, g):
        self.spend(g, 0)
        for z in range(4):
            self.send(
                (self.grads, g, z, self.c1), (self.land, "rc", g, z), self.rs[g]["core"][z], self.dev_core, self.out[g]
            )
        if g == 2:
            self.send((self.at, "vs", 0), (self.at, "vr", 0), self.rs_vec["core"], self.dev_core, self.out[g])

    def items(self, g):
        if g in Z_FIRST:
            return [(0, self.z_keep[0]), (2, self.z_keep[1])]
        return [(z, z) for z in range(4)]

    def sum_half(self, g):
        c = self.c
        for z in range(4):
            self.arrive((self.land, "rc", g, z), self.rs[g]["core"][z], self.dev_core)
            self.add((self.grads, g, z, c), (self.land, "rc", g, z))
        self.credit(g, 0, self.dev_core)
        pl.semaphore_signal(self.half_sem.at[g], inc=1, device_id=self.dev_z1, device_id_type=MESH)
        pl.semaphore_wait(self.half_sem.at[g], 1)
        for k in range(2):
            self.send(
                (self.grads, g, self.z_give[k], c), (self.halved, g, k), self.rs[g]["half"][k], self.dev_z1, self.out[g]
            )

    def sum_one(self, g):
        y, x, c = self.y, self.x, self.c
        for i, (slot, z) in enumerate(self.items(g)):
            mine, came = (self.grads, g, z, c), (self.land, "rc", g, i)
            if g in Z_FIRST:
                came = (self.halved, g, i)
                self.arrive(came, self.rs[g]["half"][i], self.dev_z1)
            else:
                self.arrive(came, self.rs[g]["core"][i], self.dev_core)
            self.add(mine, came)
            if i == 0:
                self.spend(g, 1)
                self.spend(g, 2)
            land = (self.land, "r1", g, slot)
            if slot < 2:
                self.send((self.grads, g, z, c, slice(None), self.x1), land, self.rs[g]["one"][i], self.dev_x, self.out[g])
            else:
                self.send((self.grads, g, z, c, self.y1), land, self.rs[g]["one"][i], self.dev_y, self.out[g])
        if g not in Z_FIRST:
            self.credit(g, 0, self.dev_core)
        if g == 2:
            self.arrive((self.at, "vr", 0), self.rs_vec["core"], self.dev_core)
            self.vs[1] = self.vs[0] + self.vr[0]
            self.send((self.at, "vs", 1), (self.at, "vr", 1), self.rs_vec["one"], self.dev_x, self.out[g])

    def sum_two(self, g):
        y, x, c = self.y, self.x, self.c
        for i, (slot, z) in enumerate(self.items(g)):
            came = (self.land, "r1", g, slot)
            self.arrive(came, self.rs[g]["one"][i], self.dev_x if slot < 2 else self.dev_y)
            self.add((self.grads, g, z, c, slice(None), x) if slot < 2 else (self.grads, g, z, c, y), came)
            if i == 0:
                self.spend(g, 3)
                self.spend(g, 4)
            land = (self.land, "r2", g, slot)
            if slot < 2:
                self.send((self.grads, g, z, c, self.y1, x), land, self.rs[g]["two"][i], self.dev_y, self.out[g])
            else:
                self.send((self.grads, g, z, c, y, self.x1), land, self.rs[g]["two"][i], self.dev_x, self.out[g])
        self.credit(g, 1, self.dev_x)
        self.credit(g, 2, self.dev_y)
        if g == 2:
            self.arrive((self.at, "vr", 1), self.rs_vec["one"], self.dev_x)
            self.vs[2] = self.vs[1] + self.vr[1]
            self.send((self.at, "vs", 2), (self.at, "vr", 2), self.rs_vec["two"], self.dev_y, self.out[g])

    def sum_zed(self, g):
        y, x, c = self.y, self.x, self.c
        for i, (slot, z) in enumerate(self.items(g)):
            came = (self.land, "r2", g, slot)
            self.arrive(came, self.rs[g]["two"][i], self.dev_y if slot < 2 else self.dev_x)
            self.add((self.grads, g, z, c, y, x), came)
        for d in range(3):
            self.spend(g, 5 + d)
        if g in Z_FIRST:
            self.send(
                (self.grads, g, self.others[1], c, y, x),
                (self.land, "rz", g, 1),
                self.rs[g]["zed"][1],
                self.dev_z[1],
                self.out[g],
            )
        else:
            for d in range(3):
                self.send(
                    (self.grads, g, self.others[d], c, y, x),
                    (self.land, "rz", g, 2 - d),
                    self.rs[g]["zed"][d],
                    self.dev_z[d],
                    self.out[g],
                )
        self.credit(g, 3, self.dev_y)
        self.credit(g, 4, self.dev_x)
        if g == 2:
            self.arrive((self.at, "vr", 2), self.rs_vec["two"], self.dev_y)
            self.vs[3] = self.vs[2] + self.vr[2]
            for d in range(3):
                self.send((self.at, "vs", 3), (self.at, "vr", 3 + 2 - d), self.rs_vec["zed"][d], self.dev_z[d], self.out[g])

    def sum_plane(self, g):
        total = self.grads(g, self.z, self.c, self.y, self.x)[...].astype(f32)
        for d in (1,) if g in Z_FIRST else range(3):
            self.arrive((self.land, "rz", g, d), self.rs[g]["zed"][2 - d], self.dev_z[d])
            total = total + self.land("rz", g, d)[...].astype(f32)
        own = (self.total, g, self.r)
        self.total(g, self.r)[...] = total.astype(bf)
        for k, device in enumerate((self.dev_x, self.dev_y, self.dev_d)):
            self.send(own, own, self.rs[g]["plane"][k], device, self.out[g])
        for d in range(3):
            self.credit(g, 5 + 2 - d, self.dev_z[d])
        if g == 2:
            vec = self.vs[3]
            for d in range(3):
                self.arrive((self.at, "vr", 3 + d), self.rs_vec["zed"][2 - d], self.dev_z[d])
                vec = vec + self.vr[3 + d]
            self.vec_total[...] = pltpu.roll(vec, lax.rem(D - self.s * SUB, D), 1)[:, 0:128]

    def sum_wait(self, g):
        for k, (r, device) in enumerate(((self.rx, self.dev_x), (self.ry, self.dev_y), (self.rd, self.dev_d))):
            self.arrive((self.total, g, r), self.rs[g]["plane"][k], device)

    def sum_drain(self, g):
        for copy in self.out[g]:
            copy().wait_send()
        self.out[g] = []


def layer_kernel(linked, *refs):
    if linked:
        (tok_h, cot_h, del_ref, len_ref, vec_in, qkv_h, out_h, up_h, down_h) = refs[:9]
        (y_h, tg_h, t0_h, t1_h, t2_h, vg_out) = refs[9:15]
        rest = refs[15:]
    else:
        (tok_h, cot_h, del_ref, len_ref, vec_in, ws_h, wd_h) = refs[:7]
        (y_h, tg_h, g0_h, g1_h, g2_h, vg_out) = refs[7:13]
        rest = refs[13:]
    (ws, wd, x, qkv, pt, mixed, nrm1, root1, fl, act, act3, gp, gs, gsec, cot, keep, vec_ref, vg_ref, sem) = rest[:19]
    if linked:
        names = ("vb", "rc", "r1", "r2", "rz", "r1t", "r2t", "rzt", "gt", "vs", "vr", "send_sem", "recv_sem", "credit_sem", "half_sem")
        net = Links(dict(zip(names, rest[19:]), ws=ws, wd=wd, gp=gp, act3=act3, vec_total=vg_out))
        net.plan_gather()
        net.plan_sum()

    cp_x = pltpu.make_async_copy(tok_h, x, sem.at[0])
    cp_cot = pltpu.make_async_copy(cot_h, cot, sem.at[1])
    lane = lax.broadcasted_iota(jnp.int32, (CROP, 128), 1)
    low_half = lane < 64

    def half(v, h):
        return jnp.where(low_half if h == 0 else ~low_half, v, jnp.zeros_like(v))

    def vrow(r):
        return vec_ref[r : r + 1, :]

    def mat(g, j):
        if g == 2:
            return wd[j].reshape(D, D)
        return ws[g, j // 2, j % 2].reshape(D, D)

    def mat_third(j, t):
        return ws[0, j // 2, j % 2, :, :, :, third(t)].reshape(D, 256)

    def step(name, *a):
        return functools.partial(getattr(net, name), *a) if linked else (lambda: None)

    def after(name):
        plan = {}
        for kind, table in (("gather_", GATHER_PLAN), ("sum_", SUM_PLAN)):
            for c, steps in table.get(name, {}).items():
                plan[c] = [step(kind + what, g) for what, g in steps]
        return plan

    def now(name):
        for act_now in after(name).get(0, ()):
            act_now()

    if linked:
        net.greet()
        loads = []
        for j in range(4):
            src = qkv_h.at[:, j * D : (j + 1) * D] if j < 3 else out_h
            loads.append(pltpu.make_async_copy(src, gs.at[j * SUB : (j + 1) * SUB], sem.at[2 + j]))
        for j in range(4):
            loads.append(
                pltpu.make_async_copy(
                    up_h.at[:, j * D : (j + 1) * D], nrm1.at[j * SUB : (j + 1) * SUB], sem.at[6 + j]
                )
            )
        loads.append(pltpu.make_async_copy(down_h, gs.at[4 * SUB : 8 * SUB], sem.at[10]))
        for load in loads:
            load.start()
        cp_x.start()
        cp_cot.start()
        net.vs[0, :, 0:128] = jnp.zeros((16, 128), f32)
        net.vs[0, 0 : vec_in.shape[0], 0 : vec_in.shape[1]] = vec_in[...]
        net.vb[net.s] = net.vs[0, :, 0:128].astype(bf)
        for j in range(4):
            loads[j].wait()
            ws[0, j // 2, j % 2, net.z, net.c] = gs[j * SUB : (j + 1) * SUB].astype(bf)
        net.greeted()
        net.gather_start(0)
        for j in range(4):
            loads[4 + j].wait()
            ws[1, j // 2, j % 2, net.z, net.c] = nrm1[j * SUB : (j + 1) * SUB].astype(bf)
        loads[8].wait()
        for j in range(4):
            wd[net.z, net.c, j // 2, j % 2] = gs[(4 + j) * SUB : (5 + j) * SUB].astype(bf)
    else:
        vec_ref[...] = vec_in[...]
        cp_ws = pltpu.make_async_copy(ws_h, ws, sem.at[2])
        cp_wd = pltpu.make_async_copy(wd_h, wd, sem.at[3])
        for copy in (cp_ws, cp_wd, cp_x, cp_cot):
            copy.start()
        cp_ws.wait()
        cp_wd.wait()
    place = lax.broadcasted_iota(jnp.int32, (1, CROP), 1)
    allowed = [
        jnp.where(((del_ref[c : c + 1, :] == 1) | (place == 0)) & (place < len_ref[c]), 1.0, 0.0) for c in range(NC)
    ]
    mcol = jnp.concatenate(allowed * (8 // NC), axis=0).T
    for c in range(NC):
        keep[c * CROP : (c + 1) * CROP, :] = jnp.broadcast_to(mcol[:, c : c + 1], (CROP, 128)).astype(bf)
    vg_ref[...] = jnp.zeros_like(vg_ref)
    cp_x.wait()
    cp_cot.wait()
    if linked:
        now("start")
        row = lax.broadcasted_iota(jnp.int32, (128, D), 0)
        col = lax.broadcasted_iota(jnp.int32, (128, D), 1)
        vec = jnp.zeros((16, D), f32)
        for s in range(8):
            pick = ((col == row + s * SUB) & (row < SUB)).astype(f32).astype(bf)
            vec = vec + dg(net.vb[s], pick, 1, 0)
        vec_ref[...] = vec

    def project(t, c):
        r = rows_of(c)
        xv = x[r, :]
        for b in range(3):
            y = dg(xv, mat_third(b, t), 1, 0)
            if b == 0:
                y = y + vec_ref[0:1, third(t)]
            if b == 2:
                y = y + vec_ref[1:2, third(t)]
            qkv[r, t * D + b * 256 : t * D + (b + 1) * 256] = y.astype(bf)

    def attend(t, c):
        r = rows_of(c)
        kp = lanes(keep[r, :].astype(f32), 2) > 0.5
        for p in range(2):
            q, k, v = (qkv[r, t * D + b * 256 + p * 128 : t * D + b * 256 + (p + 1) * 128] for b in range(3))
            q = q * jnp.asarray(0.125, bf)
            o = None
            for h in range(2):
                st = dg(k, half(q, h), 1, 1)
                st = jnp.where(kp, st, -1e30)
                e = jnp.exp(st - jnp.max(st, axis=0, keepdims=True))
                pr = (e * (1.0 / jnp.sum(e, axis=0, keepdims=True))).astype(bf)
                pt[c, 4 * t + 2 * p + h] = pr
                w = dg(pr, half(v, h), 0, 0)
                o = w if o is None else o + w
            mixed[r, t * 256 + p * 128 : t * 256 + (p + 1) * 128] = o.astype(bf)

    for t in range(3):
        crop_loop(functools.partial(project, t), after(f"project{t}"))
        crop_loop(functools.partial(attend, t), after(f"attend{t}"))

    def body(c):
        r = rows_of(c)
        h = x[r, :].astype(f32) + (dg(mixed[r, :], mat(0, 3), 1, 0) + vrow(2))
        h = h - lane_mean(h)
        root = lax.rsqrt(lane_mean(h * h) + norm_epsilon)
        n = h * root
        nrm1[r, :] = n
        root1[r, :] = jnp.broadcast_to(root, (CROP, 128))
        fl[r, :] = (n * vrow(3) + vrow(4)).astype(bf)

    crop_loop(body, after("out"))

    def body(c):
        r = rows_of(c)
        a = fl[r, :]
        for j in range(4):
            u = dg(a, mat(1, j), 1, 0) + vrow(5 + j)
            g, d = gelu_parts(u)
            if j < 3:
                act[r, j * D : (j + 1) * D] = g.astype(bf)
            else:
                act3[c // 2, c % 2] = g.astype(bf).reshape(2, 128, D)
            gp[j // 2, j % 2, r, :] = d.astype(bf)

    crop_loop(body, after("up"))

    def body(c):
        r = rows_of(c)
        s = dg(act[r, :], wd[0:3].reshape(3 * D, D), 1, 0)
        s = s + dg(act3[c // 2, c % 2].reshape(CROP, D), wd[3].reshape(D, D), 1, 0) + vrow(9)
        h = nrm1[r, :] * vrow(3) + vrow(4) + s
        h = h - lane_mean(h)
        root = lax.rsqrt(lane_mean(h * h) + norm_epsilon)
        n = h * root
        G = cot[r, :].astype(f32) * lanes(keep[r, :].astype(f32), 6)
        cot[r, :] = (n * vrow(10) + vrow(11)).astype(bf)
        vg_ref[10:11, :] += jnp.sum(G * n, axis=0, keepdims=True)
        vg_ref[11:12, :] += jnp.sum(G, axis=0, keepdims=True)
        dn = G * vrow(10)
        g2 = root * (dn - lane_mean(dn) - n * lane_mean(dn * n))
        gs[r, :] = g2
        gb = g2.astype(bf)
        gsec[r, :] = gb
        vg_ref[9:10, :] += jnp.sum(gb.astype(f32), axis=0, keepdims=True)

    crop_loop(body, after("down"))
    cp_y = pltpu.make_async_copy(cot, y_h, sem.at[0])
    cp_y.start()

    def body(c):
        r = rows_of(c)
        a = gsec[r, :]
        for j in range(4):
            ga = dg(a, mat(2, j), 1, 1)
            gi = (ga * gp[j // 2, j % 2, r, :].astype(f32)).astype(bf)
            gp[j // 2, j % 2, r, :] = gi
            vg_ref[5 + j : 6 + j, :] += jnp.sum(gi.astype(f32), axis=0, keepdims=True)

    crop_loop(body, after("act_back"))
    step("gather_drain")()

    @pl.loop(0, 3)
    def _(i):
        m = pl.ds(pl.multiple_of(i * D, D), D)
        wd[i] = dg(act[:, m], gsec[...], 0, 0).astype(bf).reshape(2, 2, 2, SUB, D)

    wd[3] = dg(act3[...].reshape(T, D), gsec[...], 0, 0).astype(bf).reshape(2, 2, 2, SUB, D)

    now("down_grad")

    def body(c):
        r = rows_of(c)
        G = gs[r, :]
        for j in range(4):
            G = G + dg(gp[j // 2, j % 2, r, :], mat(1, j), 1, 1)
        n = nrm1[r, :]
        vg_ref[3:4, :] += jnp.sum(G * n, axis=0, keepdims=True)
        vg_ref[4:5, :] += jnp.sum(G, axis=0, keepdims=True)
        dn = G * vrow(3)
        g1 = lanes(root1[r, :], 6) * (dn - lane_mean(dn) - n * lane_mean(dn * n))
        gs[r, :] = g1
        gb = g1.astype(bf)
        gsec[r, :] = gb
        vg_ref[2:3, :] += jnp.sum(gb.astype(f32), axis=0, keepdims=True)

    crop_loop(body, after("first_back"))

    def body(j):
        ws[1, j // 2, j % 2] = dg(fl[...], gp[j // 2, j % 2], 0, 0).astype(bf).reshape(4, 2, SUB, D)

    crop_loop(body, after("up_grad"))

    def body(c):
        r = rows_of(c)
        fl[r, :] = dg(gsec[r, :], mat(0, 3), 1, 1).astype(bf)

    crop_loop(body, after("mixed_back"))

    def attend_back(t, c):
        r = rows_of(c)
        for p in range(2):
            at = [slice(t * D + b * 256 + p * 128, t * D + b * 256 + (p + 1) * 128) for b in range(3)]
            cols = slice(t * 256 + p * 128, t * 256 + (p + 1) * 128)
            q, k, v = (qkv[r, cut] for cut in at)
            q = q * jnp.asarray(0.125, bf)
            do = fl[r, cols]
            dq = dk = dv = None
            for h in range(2):
                dom = half(do, h)
                dp = dg(v, dom, 1, 1)
                prb = pt[c, 4 * t + 2 * p + h]
                pr = prb.astype(f32)
                delta = jnp.sum(pr * dp, axis=0, keepdims=True)
                ds = (pr * (dp - delta)).astype(bf)
                tv = dg(prb, dom, 1, 0)
                tk = dg(ds, half(q, h), 1, 0)
                tq = dg(ds, half(k, h), 0, 0)
                dq, dk, dv = (tq, tk, tv) if dq is None else (dq + tq, dk + tk, dv + tv)
            dq = (dq * 0.125).astype(bf)
            dv = dv.astype(bf)
            act[r, at[0]] = dq
            act[r, at[1]] = dk.astype(bf)
            act[r, at[2]] = dv
            vg_ref[0:1, cols] += jnp.sum(dq.astype(f32), axis=0, keepdims=True)
            vg_ref[1:2, cols] += jnp.sum(dv.astype(f32), axis=0, keepdims=True)

    def third_grads(t):
        g = dg(x[...], act[:, t * D : (t + 1) * D], 0, 0).astype(bf)
        for j in range(3):
            gp[j // 2, j % 2, 0:D, third(t)] = g[:, third(j)]
        gp[1, 1, 0:D, third(t)] = dg(mixed[...], gsec[:, third(t)], 0, 0).astype(bf)

    for t in range(3):
        crop_loop(functools.partial(attend_back, t), after(f"attend_back{t}"))
        if linked and t == 2:
            net.vs[0] = vg_ref[...]
        third_grads(t)
        now(f"grads{t}")

    def body(c):
        r = rows_of(c)
        G = gs[r, :]
        for b in range(3):
            for t in range(3):
                G = G + dg(act[r, t * D + b * 256 : t * D + (b + 1) * 256], mat_third(b, t), 1, 1)
        gsec[r, :] = G.astype(bf)

    crop_loop(body, after("token"))
    cp_tg = pltpu.make_async_copy(gsec, tg_h, sem.at[1])
    cp_tg.start()
    if linked:
        now("end")
        shares = [pltpu.make_async_copy(net.gt.at[i], t_h, sem.at[2 + i]) for i, t_h in enumerate((t0_h, t1_h, t2_h))]
        for copy in shares:
            copy.start()
        for g in range(7):
            net.sum_drain(g)
        for copy in shares:
            copy.wait()
    else:
        vg_out[...] = vg_ref[...]
        copies = [
            pltpu.make_async_copy(gp.at[:, :, 0:D], g0_h, sem.at[2]),
            pltpu.make_async_copy(ws.at[1], g1_h, sem.at[3]),
            pltpu.make_async_copy(wd, g2_h, sem.at[4]),
        ]
        for copy in copies:
            copy.start()
        for copy in copies:
            copy.wait()
    cp_y.wait()
    cp_tg.wait()


WS = (2, 2, 2, 4, 2, SUB, D)
WD = (4, 2, 2, 2, SUB, D)


def layer(linked, *arrays):
    hbm = pl.BlockSpec(memory_space=pl.ANY)
    near = pl.BlockSpec(memory_space=pltpu.VMEM)
    VM = pltpu.VMEM
    shape = jax.ShapeDtypeStruct
    outs = [(shape((T, D), bf), hbm), (shape((T, D), bf), hbm)]
    if linked:
        outs += [(shape((4, SUB, D), bf), hbm)] * 3
    else:
        outs += [(shape((2, 2, D, D), bf), hbm), (shape(WS[1:], bf), hbm), (shape(WD, bf), hbm)]
    outs += [(shape((16, 128 if linked else D), f32), near)]
    scratch = [
        VM(WS, bf),
        VM(WD, bf),
        VM((T, D), bf),
        VM((T, 3 * D), bf),
        VM((NC, H, CROP, CROP), bf),
        VM((T, D), bf),
        VM((T, D), f32),
        VM((T, 128), f32),
        VM((T, D), bf),
        VM((T, 3 * D), bf),
        VM((2, 2, 2, 128, D), bf),
        VM((2, 2, T, D), bf),
        VM((T, D), f32),
        VM((T, D), bf),
        VM((T, D), bf),
        VM((T, 128), bf),
        VM((16, D), f32),
        VM((16, D), f32),
        pltpu.SemaphoreType.DMA((11,)),
    ]
    params = dict(vmem_limit_bytes=63 * 2**20)
    if linked:
        transfers = 7 * (3 + 3 + 3 + 3 + 4) + 7 + 7 * (4 + 4 + 4 + 2 + 3 + 3) + 6
        scratch += [
            VM((8, 16, 128), bf),
            VM((4, 2, 2, SUB, D), bf),
            VM((4, 2, SUB, D), bf),
            VM((4, SUB, D), bf),
            VM((3, SUB, D), bf),
            VM((4, 2, SUB, D), bf),
            VM((4, SUB, D), bf),
            VM((3, SUB, D), bf),
            VM((3, 4, SUB, D), bf),
            VM((4, 16, D), f32),
            VM((6, 16, D), f32),
            pltpu.SemaphoreType.DMA((transfers,)),
            pltpu.SemaphoreType.DMA((transfers,)),
            pltpu.SemaphoreType.REGULAR((16,)),
            pltpu.SemaphoreType.REGULAR((7,)),
        ]
        params.update(collective_id=0, has_side_effects=True)
    return pl.pallas_call(
        functools.partial(layer_kernel, linked),
        out_shape=[o[0] for o in outs],
        in_specs=[hbm, hbm, near, pl.BlockSpec(memory_space=pltpu.SMEM), near] + [hbm] * (len(arrays) - 5),
        out_specs=[o[1] for o in outs],
        scratch_shapes=scratch,
        compiler_params=pltpu.CompilerParams(**params),
    )(*arrays)


def adam_update(gradient, first_moment, second_moment):
    first_new = decay_first * first_moment + (1.0 - decay_first) * gradient
    second_new = decay_second * second_moment + (1.0 - decay_second) * gradient * gradient
    step_dir = first_new / correct_first / (jnp.sqrt(second_new / correct_second) + adam_epsilon)
    return (step_dir, first_new)


def finish(output, token_grad, gradients, moments):
    updated = [adam_update(g, m, s) for g, m, s in zip(gradients, moments[:5], moments[5:])]
    return (
        (output, token_grad)
        + tuple(gradients)
        + tuple(u[0] for u in updated)
        + tuple(u[1] for u in updated)
    )


def side_by_side(blocks):
    return jnp.concatenate([blocks[j] for j in range(blocks.shape[0])], axis=1)


def adam_kernel(*refs):
    sums, moments, passed, outs, placed = refs[:4], refs[4:14], refs[14:16], refs[16:31], refs[31:33]
    hold, sem = refs[33:]
    fetch = [pltpu.make_async_copy(a, hold.at[i], sem.at[i]) for i, a in enumerate(passed)]
    store = [pltpu.make_async_copy(hold.at[i], a, sem.at[2 + i]) for i, a in enumerate(placed)]

    @pl.when(pl.program_id(0) == 0)
    def _():
        for copy in fetch:
            copy.start()

    @pl.when(pl.program_id(0) == 1)
    def _():
        for i in range(2):
            fetch[i].wait()
            store[i].start()

    square, up, down, vec = (ref[...] for ref in sums)

    def update(k, cut, g):
        at = Ellipsis if cut is None else (slice(None), cut)
        g = g.astype(f32)
        step, first = adam_update(g, moments[k][at], moments[5 + k][at])
        outs[k][at] = g
        outs[5 + k][at] = step
        outs[10 + k][at] = first

    for j in range(4):
        cut = slice(j * D, (j + 1) * D)
        update(*((0, cut) if j < 3 else (1, None)), square[j])
        update(2, cut, up[j])
    update(3, None, down)

    @pl.when(pl.program_id(0) == 0)
    def _():
        rows, width = outs[4].shape
        update(4, None, vec[0:rows, 0:width])

    @pl.when(pl.program_id(0) == pl.num_programs(0) - 1)
    def _():
        for copy in store:
            copy.wait()


def adam(sums, moments, passed, steps=2):
    def rows(shape):
        return pl.BlockSpec((shape[0] // steps, shape[1]), lambda i: (i, 0))

    def whole(shape):
        return pl.BlockSpec(shape, lambda i: (0, 0))

    hbm = pl.BlockSpec(memory_space=pl.ANY)
    parts = pl.BlockSpec((4, SUB // steps, D), lambda i: (0, i, 0))
    specs = [whole(m.shape) if k == 4 else rows(m.shape) for k, m in enumerate(moments[:5])]
    return pl.pallas_call(
        adam_kernel,
        grid=(steps,),
        out_shape=[jax.ShapeDtypeStruct(m.shape, f32) for m in moments[:5]] * 3
        + [jax.ShapeDtypeStruct(a.shape, a.dtype) for a in passed],
        in_specs=[parts, parts, rows((4 * SUB, D)), whole((16, 128))] + specs * 2 + [hbm] * 2,
        out_specs=specs * 3 + [hbm] * 2,
        scratch_shapes=[pltpu.VMEM((2, *passed[0].shape), bf), pltpu.SemaphoreType.DMA((4,))],
        compiler_params=pltpu.CompilerParams(vmem_limit_bytes=63 * 2**20),
    )(*sums, *moments, *passed)


def per_device_linked(tokens, cotangent, deletion, lengths, qkv, out, up, down, vectors, *moments):
    output, token_grad, square, tall, wide, vec = layer(
        True, tokens, cotangent, deletion, lengths, vectors, qkv, out, up, down
    )
    *updated, output, token_grad = adam((square, tall, wide.reshape(4 * SUB, D), vec), moments, (output, token_grad))
    return (output, token_grad) + tuple(updated)


def per_device_plain(tokens, cotangent, deletion, lengths, qkv, out, up, down, vectors, *moments):
    blocks = [qkv[:, b * D : (b + 1) * D] for b in range(3)] + [out]
    blocks += [up[:, b * D : (b + 1) * D] for b in range(4)]
    square = lax.all_gather(jnp.stack(blocks).astype(bf), "shard", axis=1, tiled=True)
    tall = lax.all_gather(down.astype(bf), "shard", axis=0, tiled=True)
    vec = lax.all_gather(vectors.astype(bf), "shard", axis=1, tiled=True).astype(f32)
    output, token_grad, g0, g1, g2, vec = layer(
        False,
        tokens,
        cotangent,
        deletion,
        lengths,
        jnp.pad(vec, ((0, 4), (0, 0))),
        square.reshape(WS),
        tall.reshape(WD),
    )
    g0 = g0.reshape(4, D, D)
    square = lax.psum_scatter(
        jnp.concatenate([g0, g1.reshape(4, D, D)]).astype(f32), "shard", scatter_dimension=1, tiled=True
    )
    tall = lax.psum_scatter(g2.reshape(FF, D).astype(f32), "shard", scatter_dimension=0, tiled=True)
    vec = lax.psum_scatter(vec[:12], "shard", scatter_dimension=1, tiled=True)
    square, tall, vec = (lax.psum(g.astype(bf), "rep").astype(f32) for g in (square, tall, vec))
    gradients = (side_by_side(square[:3]), square[3], side_by_side(square[4:]), tall, vec)
    return finish(output, token_grad, gradients, moments)


def solution(mesh):
    rows = P(("rep", "shard"), None)
    weights = (P("shard", None),) * 4 + (P(None, "shard"),)
    linked = mesh.shape["rep"] == 4 and mesh.shape["shard"] == 8
    return jax.shard_map(
        per_device_linked if linked else per_device_plain,
        mesh=mesh,
        in_specs=(rows, rows, rows, P(("rep", "shard"))) + weights * 3,
        out_specs=(rows, rows) + weights * 3,
        check_vma=False,
    )
```
